512 devices in a mesh: ta: 8 (over x, y_lo), gz: 8 (over y_hi, core), gy: 8 (over z).
Axes of the slice: x: 4, y: 8 (y_hi: 4, y_lo: 2; y = y_hi * 2 + y_lo), z: 8, core: 2. Of those that a mesh axis runs over, the one named last changes fastest.
Arguments:
- quark_field: float32 [4, 3, 16, 32, 16, 128], P(None, None, 'ta', 'gz', 'gy'), may hold values from -6 to 6
- gauge_links: float32 [4, 3, 3, 16, 32, 16, 128], P(None, None, None, 'ta', 'gz', 'gy'), may hold values from -3 to 3
Outputs:
- result_field: float32 [4, 3, 16, 32, 16, 128], P(None, None, 'ta', 'gz', 'gy')
- link_force: float32 [4, 3, 3, 16, 32, 16, 128], P(None, None, None, 'ta', 'gz', 'gy')
The draws below stay inside these ranges and needn't reach their ends.
All inputs are finite; a program needn't handle non-finite values.
Results may differ from the reference program's by a relative error of at most 0.0001.
Values sent between devices are 32-bit elements; how exact they have to be, the bound alone decides.
A program may use at most 64 MiB of HBM per device.

```python
import jax
import jax.numpy as jnp
import numpy as np

LX = 64
NT = 16
NZ = 32
NY = 16


def block_levels(stream_key, shape, cuts, smallest, top_value):
    def one(dim, shards_of):
        steps = jax.random.uniform(jax.random.fold_in(jax.random.fold_in(stream_key, 6), dim), (shards_of,), jnp.float32, smallest / len(cuts), top_value / len(cuts))
        return jnp.repeat(jnp.exp(steps), shape[dim] // shards_of).reshape((-1,) + (1,) * (len(shape) - dim - 1))

    loudness = one(*cuts[0])
    for cut in cuts[1:]:
        loudness = loudness * one(*cut)
    return loudness


def scatter_about(stream_key, dims, width, most, pieces=(), kind=jnp.bfloat16):
    result = width * jax.random.normal(stream_key, dims, jnp.float32)
    if pieces:
        result = result * block_levels(stream_key, dims, pieces, -0.22, 0.18)
    return jnp.clip(result, -most, most).astype(kind)


def setup_inputs(seed: int = 0) -> dict:
    keys = jax.random.split(jax.random.key(seed), 3)
    quark_field = scatter_about(keys[0], (4, 3, NT, NZ, NY, 2 * LX), 1.0, 6.0, ((2, 8), (3, 8), (4, 8)), jnp.float32)
    gauge_links = scatter_about(keys[1], (4, 3, 3, NT, NZ, NY, 2 * LX), 0.41, 3.0, ((3, 8), (4, 8), (5, 8)), jnp.float32)
    return {"quark_field": quark_field, "gauge_links": gauge_links}


hopping_kappa = 0.125


def block_matrix(upper_left, upper_right, lower_left, lower_right):
    upper = np.concatenate([upper_left, upper_right], axis=1)
    lower = np.concatenate([lower_left, lower_right], axis=1)
    return np.concatenate([upper, lower], axis=0)


def gamma_tables():
    paulis = [np.array([[0, 1], [1, 0]], dtype=complex), np.array([[0, -1j], [1j, 0]], dtype=complex), np.array([[1, 0], [0, -1]], dtype=complex)]
    zero_block = np.zeros((2, 2), dtype=complex)
    unit_block = np.eye(2, dtype=complex)
    gammas = [block_matrix(zero_block, -1j * pauli_matrix, 1j * pauli_matrix, zero_block) for pauli_matrix in paulis]
    gammas.append(block_matrix(zero_block, unit_block, unit_block, zero_block))
    stacked = np.stack(gammas)
    return stacked.real.astype(np.float32), stacked.imag.astype(np.float32)


def mix_apply(table, part):
    factor = jnp.asarray(table, dtype=part.dtype).reshape((4, 4) + (1,) * (part.ndim - 1))
    return jnp.sum(factor * part[None], axis=1)


def spin_project(direction, parity, part_real, part_imag):
    table_real, table_imag = gamma_tables()
    mix_real = parity * table_real[direction]
    mix_imag = parity * table_imag[direction]
    new_real = part_real + mix_apply(mix_real, part_real) - mix_apply(mix_imag, part_imag)
    new_imag = part_imag + mix_apply(mix_real, part_imag) + mix_apply(mix_imag, part_real)
    return new_real, new_imag


def colour_times(link, part):
    return jnp.sum(link[None] * part[:, None], axis=2)


def link_apply(link_real, link_imag, part_real, part_imag):
    new_real = colour_times(link_real, part_real) - colour_times(link_imag, part_imag)
    new_imag = colour_times(link_real, part_imag) + colour_times(link_imag, part_real)
    return new_real, new_imag


def adjoint_apply(link_real, link_imag, part_real, part_imag):
    flip_real = jnp.swapaxes(link_real, 0, 1)
    flip_imag = jnp.swapaxes(link_imag, 0, 1)
    new_real = colour_times(flip_real, part_real) + colour_times(flip_imag, part_imag)
    new_imag = colour_times(flip_real, part_imag) - colour_times(flip_imag, part_real)
    return new_real, new_imag


def spin_outer(left, right):
    return jnp.sum(left[:, :, None] * right[:, None, :], axis=0)


def outer_product(left_real, left_imag, right_real, right_imag):
    new_real = spin_outer(left_real, right_real) + spin_outer(left_imag, right_imag)
    new_imag = spin_outer(left_imag, right_real) - spin_outer(left_real, right_imag)
    return new_real, new_imag


def matrix_times(left, right):
    return jnp.sum(left[:, :, None] * right[None, :, :], axis=1)


def times_link(link_real, link_imag, matrix_real, matrix_imag):
    new_real = matrix_times(link_real, matrix_real) - matrix_times(link_imag, matrix_imag)
    new_imag = matrix_times(link_real, matrix_imag) + matrix_times(link_imag, matrix_real)
    return new_real, new_imag


def traceless_part(whole_real, whole_imag):
    anti_real = 0.5 * (whole_real - jnp.swapaxes(whole_real, 0, 1))
    anti_imag = 0.5 * (whole_imag + jnp.swapaxes(whole_imag, 0, 1))
    trace_third = (whole_imag[0, 0] + whole_imag[1, 1] + whole_imag[2, 2]) / 3.0
    identity = jnp.eye(3, dtype=whole_imag.dtype)[:, :, None, None, None, None]
    return anti_real, anti_imag - identity * trace_third


def roll_along(part, direction, stride):
    dim_index = (5, 4, 3, 2)[direction]
    return jnp.roll(part, -stride, axis=dim_index)


def spinor_neighbour(part_real, part_imag, direction, stride):
    moved_real = roll_along(part_real, direction, stride)
    moved_imag = roll_along(part_imag, direction, stride)
    if direction == 3:
        edge = NT - 1 if stride > 0 else 0
        parity = jnp.where(jnp.arange(NT) == edge, -1.0, 1.0).astype(part_real.dtype)[:, None, None, None]
        moved_real = moved_real * parity
        moved_imag = moved_imag * parity
    return moved_real, moved_imag


def reference(quark_field, gauge_links):
    quark_real, quark_imag = quark_field[..., :LX], quark_field[..., LX:]
    gauge_real, gauge_imag = gauge_links[..., :LX], gauge_links[..., LX:]
    hop_real = jnp.zeros_like(quark_real)
    hop_imag = jnp.zeros_like(quark_imag)
    for direction in range(4):
        ahead_real, ahead_imag = spinor_neighbour(quark_real, quark_imag, direction, 1)
        moved_real, moved_imag = link_apply(gauge_real[direction], gauge_imag[direction], ahead_real, ahead_imag)
        term_real, term_imag = spin_project(direction, -1.0, moved_real, moved_imag)
        hop_real = hop_real + term_real
        hop_imag = hop_imag + term_imag
        behind_real, behind_imag = spinor_neighbour(quark_real, quark_imag, direction, -1)
        back_real = roll_along(gauge_real[direction], direction, -1)
        back_imag = roll_along(gauge_imag[direction], direction, -1)
        moved_real, moved_imag = adjoint_apply(back_real, back_imag, behind_real, behind_imag)
        term_real, term_imag = spin_project(direction, 1.0, moved_real, moved_imag)
        hop_real = hop_real + term_real
        hop_imag = hop_imag + term_imag
    result_real = quark_real - hopping_kappa * hop_real
    result_imag = quark_imag - hopping_kappa * hop_imag
    forces = []
    for direction in range(4):
        ahead_real, ahead_imag = spinor_neighbour(quark_real, quark_imag, direction, 1)
        ahead_real, ahead_imag = spin_project(direction, -1.0, ahead_real, ahead_imag)
        first_real, first_imag = outer_product(ahead_real, ahead_imag, result_real, result_imag)
        later_real, later_imag = spinor_neighbour(result_real, result_imag, direction, 1)
        later_real, later_imag = spin_project(direction, 1.0, later_real, later_imag)
        second_real, second_imag = outer_product(later_real, later_imag, quark_real, quark_imag)
        whole_real, whole_imag = times_link(gauge_real[direction], gauge_imag[direction], first_real + second_real, first_imag + second_imag)
        force_real, force_imag = traceless_part(whole_real, whole_imag)
        forces.append(jnp.concatenate([hopping_kappa * force_real, hopping_kappa * force_imag], axis=-1))
    return jnp.concatenate([result_real, result_imag], axis=-1), jnp.stack(forces)
```

```python
import jax
import jax.numpy as jnp
from jax import lax
from jax.experimental import pallas as pl
from jax.experimental.pallas import tpu as pltpu
from jax.sharding import PartitionSpec as P

KAPPA = 0.125
MESH = pl.DeviceIdType.MESH
X_DIR, Y_DIR, Z_DIR, T_DIR = 0, 1, 2, 3
AXES = {T_DIR: "ta", Z_DIR: "gz", Y_DIR: "gy"}
FACES = (T_DIR, Z_DIR, Y_DIR)
FACE_TILES = {T_DIR: 6, Z_DIR: 3, Y_DIR: 6}


def lane_roll(v, steps):
    return pltpu.roll(v.reshape(-1, 128), steps, 1).reshape(v.shape)


def row_roll(v, steps):
    if steps % 8 == 0:
        return v
    flat = v.reshape(-1, 8, 128)
    return jnp.stack([pltpu.roll(flat[i], steps % 8, 0) for i in range(flat.shape[0])]).reshape(v.shape)


def masks():
    lane = lax.broadcasted_iota(jnp.int32, (8, 128), 1)
    row = lax.broadcasted_iota(jnp.int32, (8, 128), 0)
    return {
        "low": lane < 64,
        "last_x": lane % 64 == 63,
        "first_x": lane % 64 == 0,
        "even": row % 2 == 0,
        "z_first": row < 2,
        "z_last": row >= 6,
        "row": row,
    }


def pick(mask, a, b):
    return jnp.where(jnp.broadcast_to(mask, a.shape), a, b)


def unpack(m, first, second):
    return (
        pick(m["low"], first, lane_roll(second, 64)),
        pick(m["low"], lane_roll(first, 64), second),
    )


def pack_first(m, re, im):
    return pick(m["low"], re, lane_roll(im, 64))


def pack_second(m, re, im):
    return pick(m["low"], lane_roll(re, 64), im)


def c_add(a, b):
    return (a[0] + b[0], a[1] + b[1])


def c_sub(a, b):
    return (a[0] - b[0], a[1] - b[1])


def add_i(a, b):
    return (a[0] - b[1], a[1] + b[0])


def sub_i(a, b):
    return (a[0] + b[1], a[1] - b[0])


def project(direction, sign, psi):
    u0, u1, l0, l1 = psi
    plus, minus = (c_add, c_sub) if sign < 0 else (c_sub, c_add)
    plus_i, minus_i = (add_i, sub_i) if sign < 0 else (sub_i, add_i)
    if direction == X_DIR:
        return [plus_i(u0, l1), plus_i(u1, l0)]
    if direction == Y_DIR:
        return [plus(u0, l1), minus(u1, l0)]
    if direction == Z_DIR:
        return [plus_i(u0, l0), minus_i(u1, l1)]
    return [minus(u0, l0), minus(u1, l1)]


def add_spins(direction, sign, total, half):
    h0, h1 = half
    plus, minus = (c_sub, c_add) if sign < 0 else (c_add, c_sub)
    plus_i, minus_i = (sub_i, add_i) if sign < 0 else (add_i, sub_i)
    t0, t1, t2, t3 = total
    upper = [c_add(t0, h0), c_add(t1, h1)]
    if direction == X_DIR:
        return upper + [plus_i(t2, h1), plus_i(t3, h0)]
    if direction == Y_DIR:
        return upper + [plus(t2, h1), minus(t3, h0)]
    if direction == Z_DIR:
        return upper + [plus_i(t2, h0), minus_i(t3, h1)]
    return upper + [plus(t2, h0), plus(t3, h1)]


def link_times(u, half):
    ur, ui = u
    out = []
    for hr, hi in half:
        re = im = None
        for b in range(3):
            cr, ci = ur[:, b], ui[:, b]
            r = cr * hr[b][None] - ci * hi[b][None]
            i = cr * hi[b][None] + ci * hr[b][None]
            re = r if re is None else re + r
            im = i if im is None else im + i
        out.append((re, im))
    return out


def adjoint_times(u, half):
    ur, ui = u
    out = []
    for hr, hi in half:
        re = im = None
        for b in range(3):
            cr, ci = ur[b], ui[b]
            r = cr * hr[b][None] + ci * hi[b][None]
            i = cr * hi[b][None] - ci * hr[b][None]
            re = r if re is None else re + r
            im = i if im is None else im + i
        out.append((re, im))
    return out


def outer(left, right):
    re = im = None
    for (lr, li), (rr, ri) in zip(left, right):
        r = lr[:, None] * rr[None] + li[:, None] * ri[None]
        i = li[:, None] * rr[None] - lr[:, None] * ri[None]
        re = r if re is None else re + r
        im = i if im is None else im + i
    return re, im


def shift_x(m, half, steps):
    def one(v):
        if steps > 0:
            return pick(m["last_x"], lane_roll(v, 63), lane_roll(v, 127))
        return pick(m["first_x"], lane_roll(v, 65), lane_roll(v, 1))

    return [(one(re), one(im)) for re, im in half]


def stage_face(m, direction, end, half, ref):
    if direction == T_DIR:
        for s, (re, im) in enumerate(half):
            ref[3 * s:3 * s + 3] = (pack_second if end else pack_first)(m, re, im)
    elif direction == Y_DIR:
        for s, (re, im) in enumerate(half):
            if end:
                tile = pick(m["even"], row_roll(re, -1), im)
            else:
                tile = pick(m["even"], re, row_roll(im, 1))
            ref[3 * s:3 * s + 3] = tile
    else:
        tiles = [part[c] for re, im in half for part in (re, im) for c in range(3)]
        for j in range(3):
            tile = row_roll(tiles[4 * j], 2 if end else 0)
            for k in range(1, 4):
                moved = row_roll(tiles[4 * j + k], 2 * k + (2 if end else 0))
                tile = pick(m["row"] < 2 * k, tile, moved)
            ref[j] = tile


def shift_face(m, direction, steps, half, ref, sign):
    out = []
    if direction == T_DIR:
        for s, (re, im) in enumerate(half):
            face = ref[3 * s:3 * s + 3] * sign
            if steps > 0:
                out.append((
                    lane_roll(pick(m["low"], face, re), 64),
                    pick(m["low"], lane_roll(im, 64), face),
                ))
            else:
                out.append((
                    pick(m["low"], face, lane_roll(re, 64)),
                    lane_roll(pick(m["low"], im, face), 64),
                ))
    elif direction == Y_DIR:
        for s, (re, im) in enumerate(half):
            face = ref[3 * s:3 * s + 3]
            if steps > 0:
                out.append((
                    pick(m["even"], row_roll(re, -1), row_roll(face, 1)),
                    pick(m["even"], row_roll(im, -1), face),
                ))
            else:
                out.append((
                    pick(m["even"], face, row_roll(re, 1)),
                    pick(m["even"], row_roll(face, -1), row_roll(im, 1)),
                ))
    else:
        n = 0
        for re, im in half:
            parts = []
            for part in (re, im):
                moved = []
                for c in range(3):
                    face = ref[n // 4]
                    k = n % 4
                    n += 1
                    if steps > 0:
                        moved.append(row_roll(pick(m["z_first"], row_roll(face, -2 * k), part[c]), -2))
                    else:
                        moved.append(row_roll(pick(m["z_last"], row_roll(face, 6 - 2 * k), part[c]), 2))
                parts.append(jnp.stack(moved))
            out.append(tuple(parts))
    return out


def kernel(
    x_hbm, u_hbm, y_hbm, f_hbm,
    x_buf, u_buf, y_buf, f_buf,
    st_t, st_z, st_y, rt_t, rt_z, rt_y,
    load_sem, send_sem, recv_sem, store_sem,
):
    send_buf = {T_DIR: st_t, Z_DIR: st_z, Y_DIR: st_y}
    recv_buf = {T_DIR: rt_t, Z_DIR: rt_z, Y_DIR: rt_y}
    x_load = pltpu.make_async_copy(x_hbm, x_buf, load_sem.at[4])
    x_load.start()
    u_load = {}
    for d in (T_DIR, Z_DIR, Y_DIR, X_DIR):
        u_load[d] = pltpu.make_async_copy(u_hbm.at[d], u_buf.at[d], load_sem.at[d])
        u_load[d].start()

    me = {d: lax.axis_index(AXES[d]) for d in FACES}
    size = {d: lax.axis_size(AXES[d]) for d in FACES}
    ahead = {d: lax.rem(me[d] + 1, size[d]) for d in FACES}
    behind = {d: lax.rem(me[d] + size[d] - 1, size[d]) for d in FACES}

    barrier = pltpu.get_barrier_semaphore()
    for d in FACES:
        for there in (ahead[d], behind[d]):
            pl.semaphore_signal(barrier, inc=1, device_id={AXES[d]: there}, device_id_type=MESH)

    def send(d, slot, there):
        n = 3 * (d - 1) + slot
        copy = pltpu.make_async_remote_copy(
            src_ref=send_buf[d].at[slot],
            dst_ref=recv_buf[d].at[slot],
            send_sem=send_sem.at[n],
            recv_sem=recv_sem.at[n],
            device_id={AXES[d]: there},
            device_id_type=MESH,
        )
        copy.start()
        return copy

    m = masks()
    last_t = jnp.where(me[T_DIR] == size[T_DIR] - 1, -1.0, 1.0).astype(jnp.float32)
    first_t = jnp.where(me[T_DIR] == 0, -1.0, 1.0).astype(jnp.float32)
    ahead_sign = {T_DIR: last_t, Z_DIR: None, Y_DIR: None}
    behind_sign = {T_DIR: first_t, Z_DIR: None, Y_DIR: None}

    x_load.wait()
    psi = [unpack(m, x_buf[3 * s:3 * s + 3, 0:8], x_buf[3 * s:3 * s + 3, 8:16]) for s in range(4)]
    minus = {}
    plus = {}
    for d in FACES:
        minus[d] = project(d, -1, psi)
        stage_face(m, d, 0, minus[d], send_buf[d].at[0])
    pl.semaphore_wait(barrier, 6)
    copies = [send(d, 0, behind[d]) for d in FACES]
    forward = dict(zip(FACES, copies))

    def links(d):
        first, second = unpack(m, u_buf[d, :, 0:8], u_buf[d, :, 8:16])
        return first.reshape(3, 3, 8, 128), second.reshape(3, 3, 8, 128)

    u = {}
    back = {}
    backward = {}
    for d in FACES:
        u_load[d].wait()
        u[d] = links(d)
        plus[d] = project(d, 1, psi)
        back[d] = adjoint_times(u[d], plus[d])
        stage_face(m, d, 1, back[d], send_buf[d].at[1])
        backward[d] = send(d, 1, ahead[d])

    zero = jnp.zeros((3, 8, 128), jnp.float32)
    hop = [(zero, zero)] * 4
    d = X_DIR
    u_load[d].wait()
    u[d] = links(d)
    plus[d] = project(d, 1, psi)
    minus[d] = project(d, -1, psi)
    moved = {}
    moved[d] = link_times(u[d], shift_x(m, minus[d], 1))
    hop = add_spins(d, -1, hop, moved[d])
    hop = add_spins(d, 1, hop, shift_x(m, adjoint_times(u[d], plus[d]), -1))
    for d in FACES:
        forward[d].wait_recv()
        there = shift_face(m, d, 1, minus[d], recv_buf[d].at[0], ahead_sign[d])
        moved[d] = link_times(u[d], there)
        hop = add_spins(d, -1, hop, moved[d])
    for d in FACES:
        backward[d].wait_recv()
        there = shift_face(m, d, -1, back[d], recv_buf[d].at[1], behind_sign[d])
        hop = add_spins(d, 1, hop, there)

    result = [
        (pr - KAPPA * hr, pi - KAPPA * hi) for (pr, pi), (hr, hi) in zip(psi, hop)
    ]
    later = {}
    upward = {}
    for d in FACES:
        later[d] = project(d, 1, result)
        stage_face(m, d, 0, later[d], send_buf[d].at[2])
        upward[d] = send(d, 2, behind[d])
    for s, (re, im) in enumerate(result):
        y_buf[3 * s:3 * s + 3, 0:8] = pack_first(m, re, im)
        y_buf[3 * s:3 * s + 3, 8:16] = pack_second(m, re, im)
    stores = [pltpu.make_async_copy(y_buf, y_hbm, store_sem.at[4])]
    stores[0].start()

    def finish(d, first, later_there):
        second = outer(link_times(u[d], later_there), plus[d])
        wr, wi = c_add(first, second)
        third = (wi[0, 0] + wi[1, 1] + wi[2, 2]) / 3.0
        for a in range(3):
            for b in range(a, 3):
                if a == b:
                    im = KAPPA * (wi[a, a] - third)
                    re = jnp.zeros_like(im)
                else:
                    re = (0.5 * KAPPA) * (wr[a, b] - wr[b, a])
                    im = (0.5 * KAPPA) * (wi[a, b] + wi[b, a])
                top = pack_first(m, re, im)
                bottom = pack_second(m, re, im)
                f_buf[d, 3 * a + b, 0:8] = top
                f_buf[d, 3 * a + b, 8:16] = bottom
                if a != b:
                    f_buf[d, 3 * b + a, 0:8] = pick(m["low"], -top, top)
                    f_buf[d, 3 * b + a, 8:16] = pick(m["low"], -bottom, bottom)
        store = pltpu.make_async_copy(f_buf.at[d], f_hbm.at[d], store_sem.at[d])
        store.start()
        stores.append(store)

    d = X_DIR
    finish(d, outer(moved[d], project(d, -1, result)), shift_x(m, project(d, 1, result), 1))
    first = {d: outer(moved[d], project(d, -1, result)) for d in FACES}
    for d in FACES:
        upward[d].wait_recv()
        finish(d, first[d], shift_face(m, d, 1, later[d], recv_buf[d].at[2], ahead_sign[d]))
    for d in FACES:
        forward[d].wait_send()
        backward[d].wait_send()
        upward[d].wait_send()
    for store in stores:
        store.wait()


def body(quark_field, gauge_links):
    x = quark_field.reshape(12, 16, 128)
    u = gauge_links.reshape(4, 9, 16, 128)
    faces = [pltpu.VMEM((3, FACE_TILES[d], 8, 128), jnp.float32) for d in FACES]
    y, f = pl.pallas_call(
        kernel,
        out_shape=(
            jax.ShapeDtypeStruct(x.shape, jnp.float32),
            jax.ShapeDtypeStruct(u.shape, jnp.float32),
        ),
        in_specs=[pl.BlockSpec(memory_space=pl.ANY)] * 2,
        out_specs=(pl.BlockSpec(memory_space=pl.ANY),) * 2,
        scratch_shapes=[
            pltpu.VMEM(x.shape, jnp.float32),
            pltpu.VMEM(u.shape, jnp.float32),
            pltpu.VMEM(x.shape, jnp.float32),
            pltpu.VMEM(u.shape, jnp.float32),
            *faces,
            *faces,
            pltpu.SemaphoreType.DMA((5,)),
            pltpu.SemaphoreType.DMA((9,)),
            pltpu.SemaphoreType.DMA((9,)),
            pltpu.SemaphoreType.DMA((5,)),
        ],
        compiler_params=pltpu.CompilerParams(collective_id=0, has_side_effects=True),
        cost_estimate=pl.CostEstimate(flops=6_000_000, bytes_accessed=800_000, transcendentals=0),
    )(x, u)
    return y.reshape(quark_field.shape), f.reshape(gauge_links.shape)


def solution(mesh):
    specs = (
        P(None, None, "ta", "gz", "gy", None),
        P(None, None, None, "ta", "gz", "gy", None),
    )
    return jax.shard_map(body, mesh=mesh, in_specs=specs, out_specs=specs, check_vma=False)
```

```python
import jax
import jax.numpy as jnp
from jax import lax
from jax.experimental import pallas as pl
from jax.experimental.pallas import tpu as pltpu
from jax.sharding import PartitionSpec as P

KAPPA = 0.125
MESH = pl.DeviceIdType.MESH
X_DIR, Y_DIR, Z_DIR, T_DIR = 0, 1, 2, 3
AXES = {T_DIR: "ta", Z_DIR: "gz", Y_DIR: "gy"}
FACES = (T_DIR, Z_DIR, Y_DIR)
FACE_TILES = {T_DIR: 6, Z_DIR: 3, Y_DIR: 6}


def lane_roll(v, steps):
    return pltpu.roll(v.reshape(-1, 128), steps, 1).reshape(v.shape)


def row_roll(v, steps):
    if steps % 8 == 0:
        return v
    flat = v.reshape(-1, 8, 128)
    return jnp.stack([pltpu.roll(flat[i], steps % 8, 0) for i in range(flat.shape[0])]).reshape(v.shape)


def masks():
    lane = lax.broadcasted_iota(jnp.int32, (8, 128), 1)
    row = lax.broadcasted_iota(jnp.int32, (8, 128), 0)
    return {
        "low": lane < 64,
        "last_x": lane % 64 == 63,
        "first_x": lane % 64 == 0,
        "even": row % 2 == 0,
        "z_first": row < 2,
        "z_last": row >= 6,
        "row": row,
    }


def pick(mask, a, b):
    return jnp.where(jnp.broadcast_to(mask, a.shape), a, b)


def unpack(m, first, second):
    return (
        pick(m["low"], first, lane_roll(second, 64)),
        pick(m["low"], lane_roll(first, 64), second),
    )


def pack_first(m, re, im):
    return pick(m["low"], re, lane_roll(im, 64))


def pack_second(m, re, im):
    return pick(m["low"], lane_roll(re, 64), im)


def c_add(a, b):
    return (a[0] + b[0], a[1] + b[1])


def c_sub(a, b):
    return (a[0] - b[0], a[1] - b[1])


def add_i(a, b):
    return (a[0] - b[1], a[1] + b[0])


def sub_i(a, b):
    return (a[0] + b[1], a[1] - b[0])


def project(direction, sign, psi):
    u0, u1, l0, l1 = psi
    plus, minus = (c_add, c_sub) if sign < 0 else (c_sub, c_add)
    plus_i, minus_i = (add_i, sub_i) if sign < 0 else (sub_i, add_i)
    if direction == X_DIR:
        return [plus_i(u0, l1), plus_i(u1, l0)]
    if direction == Y_DIR:
        return [plus(u0, l1), minus(u1, l0)]
    if direction == Z_DIR:
        return [plus_i(u0, l0), minus_i(u1, l1)]
    return [minus(u0, l0), minus(u1, l1)]


def add_spins(direction, sign, total, half):
    h0, h1 = half
    plus, minus = (c_sub, c_add) if sign < 0 else (c_add, c_sub)
    plus_i, minus_i = (sub_i, add_i) if sign < 0 else (add_i, sub_i)
    t0, t1, t2, t3 = total
    upper = [c_add(t0, h0), c_add(t1, h1)]
    if direction == X_DIR:
        return upper + [plus_i(t2, h1), plus_i(t3, h0)]
    if direction == Y_DIR:
        return upper + [plus(t2, h1), minus(t3, h0)]
    if direction == Z_DIR:
        return upper + [plus_i(t2, h0), minus_i(t3, h1)]
    return upper + [plus(t2, h0), plus(t3, h1)]


def link_times(u, half):
    ur, ui = u
    out = []
    for hr, hi in half:
        re = im = None
        for b in range(3):
            cr, ci = ur[:, b], ui[:, b]
            r = cr * hr[b][None] - ci * hi[b][None]
            i = cr * hi[b][None] + ci * hr[b][None]
            re = r if re is None else re + r
            im = i if im is None else im + i
        out.append((re, im))
    return out


def adjoint_times(u, half):
    ur, ui = u
    out = []
    for hr, hi in half:
        re = im = None
        for b in range(3):
            cr, ci = ur[b], ui[b]
            r = cr * hr[b][None] + ci * hi[b][None]
            i = cr * hi[b][None] - ci * hr[b][None]
            re = r if re is None else re + r
            im = i if im is None else im + i
        out.append((re, im))
    return out


def outer(left, right):
    re = im = None
    for (lr, li), (rr, ri) in zip(left, right):
        r = lr[:, None] * rr[None] + li[:, None] * ri[None]
        i = li[:, None] * rr[None] - lr[:, None] * ri[None]
        re = r if re is None else re + r
        im = i if im is None else im + i
    return re, im


def shift_x(m, half, steps):
    def one(v):
        if steps > 0:
            return pick(m["last_x"], lane_roll(v, 63), lane_roll(v, 127))
        return pick(m["first_x"], lane_roll(v, 65), lane_roll(v, 1))

    return [(one(re), one(im)) for re, im in half]


def stage_face(m, direction, end, half, ref):
    if direction == T_DIR:
        for s, (re, im) in enumerate(half):
            ref[3 * s:3 * s + 3] = (pack_second if end else pack_first)(m, re, im)
    elif direction == Y_DIR:
        for s, (re, im) in enumerate(half):
            if end:
                tile = pick(m["even"], row_roll(re, -1), im)
            else:
                tile = pick(m["even"], re, row_roll(im, 1))
            ref[3 * s:3 * s + 3] = tile
    else:
        tiles = [part[c] for re, im in half for part in (re, im) for c in range(3)]
        for j in range(3):
            tile = row_roll(tiles[4 * j], 2 if end else 0)
            for k in range(1, 4):
                moved = row_roll(tiles[4 * j + k], 2 * k + (2 if end else 0))
                tile = pick(m["row"] < 2 * k, tile, moved)
            ref[j] = tile


def shift_face(m, direction, steps, half, ref, sign):
    out = []
    if direction == T_DIR:
        for s, (re, im) in enumerate(half):
            face = ref[3 * s:3 * s + 3] * sign
            if steps > 0:
                out.append((
                    lane_roll(pick(m["low"], face, re), 64),
                    pick(m["low"], lane_roll(im, 64), face),
                ))
            else:
                out.append((
                    pick(m["low"], face, lane_roll(re, 64)),
                    lane_roll(pick(m["low"], im, face), 64),
                ))
    elif direction == Y_DIR:
        for s, (re, im) in enumerate(half):
            face = ref[3 * s:3 * s + 3]
            if steps > 0:
                out.append((
                    pick(m["even"], row_roll(re, -1), row_roll(face, 1)),
                    pick(m["even"], row_roll(im, -1), face),
                ))
            else:
                out.append((
                    pick(m["even"], face, row_roll(re, 1)),
                    pick(m["even"], row_roll(face, -1), row_roll(im, 1)),
                ))
    else:
        n = 0
        for re, im in half:
            parts = []
            for part in (re, im):
                moved = []
                for c in range(3):
                    face = ref[n // 4]
                    k = n % 4
                    n += 1
                    if steps > 0:
                        moved.append(row_roll(pick(m["z_first"], row_roll(face, -2 * k), part[c]), -2))
                    else:
                        moved.append(row_roll(pick(m["z_last"], row_roll(face, 6 - 2 * k), part[c]), 2))
                parts.append(jnp.stack(moved))
            out.append(tuple(parts))
    return out


def kernel(
    x_hbm, u_hbm, y_buf, f_buf,
    x_buf, u_buf,
    st_t, st_z, st_y, rt_t, rt_z, rt_y,
    load_sem, send_sem, recv_sem,
):
    send_buf = {T_DIR: st_t, Z_DIR: st_z, Y_DIR: st_y}
    recv_buf = {T_DIR: rt_t, Z_DIR: rt_z, Y_DIR: rt_y}
    me = {d: lax.axis_index(AXES[d]) for d in FACES}
    size = {d: lax.axis_size(AXES[d]) for d in FACES}
    ahead = {d: lax.rem(me[d] + 1, size[d]) for d in FACES}
    behind = {d: lax.rem(me[d] + size[d] - 1, size[d]) for d in FACES}

    barrier = pltpu.get_barrier_semaphore()
    for d in FACES:
        for there in (ahead[d], behind[d]):
            pl.semaphore_signal(barrier, inc=1, device_id={AXES[d]: there}, device_id_type=MESH)

    x_load = pltpu.make_async_copy(x_hbm, x_buf, load_sem.at[4])
    x_load.start()
    u_load = {}
    for d in (T_DIR, Z_DIR, Y_DIR, X_DIR):
        u_load[d] = pltpu.make_async_copy(u_hbm.at[d], u_buf.at[d], load_sem.at[d])
        u_load[d].start()

    def send(d, slot, there):
        n = 3 * (d - 1) + slot
        copy = pltpu.make_async_remote_copy(
            src_ref=send_buf[d].at[slot],
            dst_ref=recv_buf[d].at[slot],
            send_sem=send_sem.at[n],
            recv_sem=recv_sem.at[n],
            device_id={AXES[d]: there},
            device_id_type=MESH,
        )
        copy.start()
        return copy

    m = masks()
    last_t = jnp.where(me[T_DIR] == size[T_DIR] - 1, -1.0, 1.0).astype(jnp.float32)
    first_t = jnp.where(me[T_DIR] == 0, -1.0, 1.0).astype(jnp.float32)
    ahead_sign = {T_DIR: last_t, Z_DIR: None, Y_DIR: None}
    behind_sign = {T_DIR: first_t, Z_DIR: None, Y_DIR: None}

    x_load.wait()
    psi = [unpack(m, x_buf[3 * s:3 * s + 3, 0:8], x_buf[3 * s:3 * s + 3, 8:16]) for s in range(4)]
    minus = {}
    plus = {}
    for d in FACES:
        minus[d] = project(d, -1, psi)
        stage_face(m, d, 0, minus[d], send_buf[d].at[0])
    pl.semaphore_wait(barrier, 6)
    copies = [send(d, 0, behind[d]) for d in FACES]
    forward = dict(zip(FACES, copies))

    def links(d):
        first, second = unpack(m, u_buf[d, :, 0:8], u_buf[d, :, 8:16])
        return first.reshape(3, 3, 8, 128), second.reshape(3, 3, 8, 128)

    u = {}
    back = {}
    backward = {}
    for d in FACES:
        u_load[d].wait()
        u[d] = links(d)
        plus[d] = project(d, 1, psi)
        back[d] = adjoint_times(u[d], plus[d])
        stage_face(m, d, 1, back[d], send_buf[d].at[1])
        backward[d] = send(d, 1, ahead[d])

    zero = jnp.zeros((3, 8, 128), jnp.float32)
    hop = [(zero, zero)] * 4
    d = X_DIR
    u_load[d].wait()
    u[d] = links(d)
    plus[d] = project(d, 1, psi)
    minus[d] = project(d, -1, psi)
    moved = {}
    moved[d] = link_times(u[d], shift_x(m, minus[d], 1))
    hop = add_spins(d, -1, hop, moved[d])
    hop = add_spins(d, 1, hop, shift_x(m, adjoint_times(u[d], plus[d]), -1))
    for d in FACES:
        forward[d].wait_recv()
        there = shift_face(m, d, 1, minus[d], recv_buf[d].at[0], ahead_sign[d])
        moved[d] = link_times(u[d], there)
        hop = add_spins(d, -1, hop, moved[d])
    for d in FACES:
        backward[d].wait_recv()
        there = shift_face(m, d, -1, back[d], recv_buf[d].at[1], behind_sign[d])
        hop = add_spins(d, 1, hop, there)

    result = [
        (pr - KAPPA * hr, pi - KAPPA * hi) for (pr, pi), (hr, hi) in zip(psi, hop)
    ]
    later = {}
    upward = {}
    for d in FACES:
        later[d] = project(d, 1, result)
        stage_face(m, d, 0, later[d], send_buf[d].at[2])
        upward[d] = send(d, 2, behind[d])
    for s, (re, im) in enumerate(result):
        y_buf[3 * s:3 * s + 3, 0:8] = pack_first(m, re, im)
        y_buf[3 * s:3 * s + 3, 8:16] = pack_second(m, re, im)

    def finish(d, first, later_there):
        second = outer(link_times(u[d], later_there), plus[d])
        wr, wi = c_add(first, second)
        third = (wi[0, 0] + wi[1, 1] + wi[2, 2]) / 3.0
        for a in range(3):
            for b in range(a, 3):
                if a == b:
                    im = KAPPA * (wi[a, a] - third)
                    re = jnp.zeros_like(im)
                else:
                    re = (0.5 * KAPPA) * (wr[a, b] - wr[b, a])
                    im = (0.5 * KAPPA) * (wi[a, b] + wi[b, a])
                top = pack_first(m, re, im)
                bottom = pack_second(m, re, im)
                f_buf[d, 3 * a + b, 0:8] = top
                f_buf[d, 3 * a + b, 8:16] = bottom
                if a != b:
                    f_buf[d, 3 * b + a, 0:8] = pick(m["low"], -top, top)
                    f_buf[d, 3 * b + a, 8:16] = pick(m["low"], -bottom, bottom)

    d = X_DIR
    finish(d, outer(moved[d], project(d, -1, result)), shift_x(m, project(d, 1, result), 1))
    first = {d: outer(moved[d], project(d, -1, result)) for d in FACES}
    for d in FACES:
        upward[d].wait_recv()
        finish(d, first[d], shift_face(m, d, 1, later[d], recv_buf[d].at[2], ahead_sign[d]))
    for d in FACES:
        forward[d].wait_send()
        backward[d].wait_send()
        upward[d].wait_send()


def store_kernel(y_in, f_in, y_out, f_out, sems):
    copies = [pltpu.make_async_copy(y_in, y_out, sems.at[4])]
    copies += [pltpu.make_async_copy(f_in.at[d], f_out.at[d], sems.at[d]) for d in range(4)]
    for copy in copies:
        copy.start()
    for copy in copies:
        copy.wait()


def body(quark_field, gauge_links):
    x = quark_field.reshape(12, 16, 128)
    u = gauge_links.reshape(4, 9, 16, 128)
    faces = [pltpu.VMEM((3, FACE_TILES[d], 8, 128), jnp.float32) for d in FACES]
    y, f = pl.pallas_call(
        kernel,
        out_shape=(pltpu.VMEM(x.shape, jnp.float32), pltpu.VMEM(u.shape, jnp.float32)),
        in_specs=[pl.BlockSpec(memory_space=pltpu.HBM)] * 2,
        out_specs=(pl.BlockSpec(memory_space=pltpu.VMEM),) * 2,
        scratch_shapes=[
            pltpu.VMEM(x.shape, jnp.float32),
            pltpu.VMEM(u.shape, jnp.float32),
            *faces,
            *faces,
            pltpu.SemaphoreType.DMA((5,)),
            pltpu.SemaphoreType.DMA((9,)),
            pltpu.SemaphoreType.DMA((9,)),
        ],
        compiler_params=pltpu.CompilerParams(collective_id=0, has_side_effects=True, vmem_limit_bytes=16 * 1024 * 1024),
        cost_estimate=pl.CostEstimate(flops=6_000_000, bytes_accessed=800_000, transcendentals=0),
    )(pltpu.with_memory_space_constraint(x, pltpu.HBM), pltpu.with_memory_space_constraint(u, pltpu.HBM))
    y, f = pl.pallas_call(
        store_kernel,
        out_shape=(
            jax.ShapeDtypeStruct(x.shape, jnp.float32),
            jax.ShapeDtypeStruct(u.shape, jnp.float32),
        ),
        in_specs=[pl.BlockSpec(memory_space=pltpu.VMEM)] * 2,
        out_specs=(pl.BlockSpec(memory_space=pl.ANY),) * 2,
        scratch_shapes=[pltpu.SemaphoreType.DMA((5,))],
        compiler_params=pltpu.CompilerParams(vmem_limit_bytes=16 * 1024 * 1024),
        cost_estimate=pl.CostEstimate(flops=0, bytes_accessed=800_000, transcendentals=0),
    )(y, f)
    return y.reshape(quark_field.shape), f.reshape(gauge_links.shape)


def solution(mesh):
    specs = (
        P(None, None, "ta", "gz", "gy", None),
        P(None, None, None, "ta", "gz", "gy", None),
    )
    return jax.shard_map(body, mesh=mesh, in_specs=specs, out_specs=specs, check_vma=False)
```

```python
import jax
import jax.numpy as jnp
from jax import lax
from jax.experimental import pallas as pl
from jax.experimental.pallas import tpu as pltpu
from jax.sharding import PartitionSpec as P

KAPPA = 0.125
MESH = pl.DeviceIdType.MESH
X_DIR, Y_DIR, Z_DIR, T_DIR = 0, 1, 2, 3
AXES = {T_DIR: "ta", Z_DIR: "gz", Y_DIR: "gy"}
FACES = (T_DIR, Z_DIR, Y_DIR)
FACE_TILES = {T_DIR: 6, Z_DIR: 3, Y_DIR: 6}


def lane_roll(v, steps):
    return pltpu.roll(v.reshape(-1, 128), steps, 1).reshape(v.shape)


def row_roll(v, steps):
    if steps % 8 == 0:
        return v
    flat = v.reshape(-1, 8, 128)
    return jnp.stack([pltpu.roll(flat[i], steps % 8, 0) for i in range(flat.shape[0])]).reshape(v.shape)


def masks():
    lane = lax.broadcasted_iota(jnp.int32, (8, 128), 1)
    row = lax.broadcasted_iota(jnp.int32, (8, 128), 0)
    return {
        "low": lane < 64,
        "last_x": lane % 64 == 63,
        "first_x": lane % 64 == 0,
        "even": row % 2 == 0,
        "z_first": row < 2,
        "z_last": row >= 6,
        "row": row,
    }


def pick(mask, a, b):
    return jnp.where(jnp.broadcast_to(mask, a.shape), a, b)


def unpack(m, first, second):
    return (
        pick(m["low"], first, lane_roll(second, 64)),
        pick(m["low"], lane_roll(first, 64), second),
    )


def pack_first(m, re, im):
    return pick(m["low"], re, lane_roll(im, 64))


def pack_second(m, re, im):
    return pick(m["low"], lane_roll(re, 64), im)


def c_add(a, b):
    return (a[0] + b[0], a[1] + b[1])


def c_sub(a, b):
    return (a[0] - b[0], a[1] - b[1])


def add_i(a, b):
    return (a[0] - b[1], a[1] + b[0])


def sub_i(a, b):
    return (a[0] + b[1], a[1] - b[0])


def project(direction, sign, psi):
    u0, u1, l0, l1 = psi
    plus, minus = (c_add, c_sub) if sign < 0 else (c_sub, c_add)
    plus_i, minus_i = (add_i, sub_i) if sign < 0 else (sub_i, add_i)
    if direction == X_DIR:
        return [plus_i(u0, l1), plus_i(u1, l0)]
    if direction == Y_DIR:
        return [plus(u0, l1), minus(u1, l0)]
    if direction == Z_DIR:
        return [plus_i(u0, l0), minus_i(u1, l1)]
    return [minus(u0, l0), minus(u1, l1)]


def add_spins(direction, sign, total, half):
    h0, h1 = half
    plus, minus = (c_sub, c_add) if sign < 0 else (c_add, c_sub)
    plus_i, minus_i = (sub_i, add_i) if sign < 0 else (add_i, sub_i)
    t0, t1, t2, t3 = total
    upper = [c_add(t0, h0), c_add(t1, h1)]
    if direction == X_DIR:
        return upper + [plus_i(t2, h1), plus_i(t3, h0)]
    if direction == Y_DIR:
        return upper + [plus(t2, h1), minus(t3, h0)]
    if direction == Z_DIR:
        return upper + [plus_i(t2, h0), minus_i(t3, h1)]
    return upper + [plus(t2, h0), plus(t3, h1)]


def link_times(u, half):
    ur, ui = u
    out = []
    for hr, hi in half:
        re = im = None
        for b in range(3):
            cr, ci = ur[:, b], ui[:, b]
            r = cr * hr[b][None] - ci * hi[b][None]
            i = cr * hi[b][None] + ci * hr[b][None]
            re = r if re is None else re + r
            im = i if im is None else im + i
        out.append((re, im))
    return out


def adjoint_times(u, half):
    ur, ui = u
    out = []
    for hr, hi in half:
        re = im = None
        for b in range(3):
            cr, ci = ur[b], ui[b]
            r = cr * hr[b][None] + ci * hi[b][None]
            i = cr * hi[b][None] - ci * hr[b][None]
            re = r if re is None else re + r
            im = i if im is None else im + i
        out.append((re, im))
    return out


def outer(left, right):
    re = im = None
    for (lr, li), (rr, ri) in zip(left, right):
        r = lr[:, None] * rr[None] + li[:, None] * ri[None]
        i = li[:, None] * rr[None] - lr[:, None] * ri[None]
        re = r if re is None else re + r
        im = i if im is None else im + i
    return re, im


def shift_x(m, half, steps):
    def one(v):
        if steps > 0:
            return pick(m["last_x"], lane_roll(v, 63), lane_roll(v, 127))
        return pick(m["first_x"], lane_roll(v, 65), lane_roll(v, 1))

    return [(one(re), one(im)) for re, im in half]


def stage_face(m, direction, end, half, ref):
    if direction == T_DIR:
        for s, (re, im) in enumerate(half):
            ref[3 * s:3 * s + 3] = (pack_second if end else pack_first)(m, re, im)
    elif direction == Y_DIR:
        for s, (re, im) in enumerate(half):
            if end:
                tile = pick(m["even"], row_roll(re, -1), im)
            else:
                tile = pick(m["even"], re, row_roll(im, 1))
            ref[3 * s:3 * s + 3] = tile
    else:
        tiles = [part[c] for re, im in half for part in (re, im) for c in range(3)]
        for j in range(3):
            tile = row_roll(tiles[4 * j], 2 if end else 0)
            for k in range(1, 4):
                moved = row_roll(tiles[4 * j + k], 2 * k + (2 if end else 0))
                tile = pick(m["row"] < 2 * k, tile, moved)
            ref[j] = tile


def shift_face(m, direction, steps, half, ref, sign):
    out = []
    if direction == T_DIR:
        for s, (re, im) in enumerate(half):
            face = ref[3 * s:3 * s + 3] * sign
            if steps > 0:
                out.append((
                    lane_roll(pick(m["low"], face, re), 64),
                    pick(m["low"], lane_roll(im, 64), face),
                ))
            else:
                out.append((
                    pick(m["low"], face, lane_roll(re, 64)),
                    lane_roll(pick(m["low"], im, face), 64),
                ))
    elif direction == Y_DIR:
        for s, (re, im) in enumerate(half):
            face = ref[3 * s:3 * s + 3]
            if steps > 0:
                out.append((
                    pick(m["even"], row_roll(re, -1), row_roll(face, 1)),
                    pick(m["even"], row_roll(im, -1), face),
                ))
            else:
                out.append((
                    pick(m["even"], face, row_roll(re, 1)),
                    pick(m["even"], row_roll(face, -1), row_roll(im, 1)),
                ))
    else:
        n = 0
        for re, im in half:
            parts = []
            for part in (re, im):
                moved = []
                for c in range(3):
                    face = ref[n // 4]
                    k = n % 4
                    n += 1
                    if steps > 0:
                        moved.append(row_roll(pick(m["z_first"], row_roll(face, -2 * k), part[c]), -2))
                    else:
                        moved.append(row_roll(pick(m["z_last"], row_roll(face, 6 - 2 * k), part[c]), 2))
                parts.append(jnp.stack(moved))
            out.append(tuple(parts))
    return out


def kernel(
    x_hbm, u_hbm, y_buf, f_buf,
    x_buf, u_buf,
    st_t, st_z, st_y, rt_t, rt_z, rt_y,
    load_sem, send_sem, recv_sem,
):
    send_buf = {T_DIR: st_t, Z_DIR: st_z, Y_DIR: st_y}
    recv_buf = {T_DIR: rt_t, Z_DIR: rt_z, Y_DIR: rt_y}
    me = {d: lax.axis_index(AXES[d]) for d in FACES}
    size = {d: lax.axis_size(AXES[d]) for d in FACES}
    ahead = {d: lax.rem(me[d] + 1, size[d]) for d in FACES}
    behind = {d: lax.rem(me[d] + size[d] - 1, size[d]) for d in FACES}

    barrier = pltpu.get_barrier_semaphore()
    is_first = {d: me[d] == 0 for d in FACES}
    for d in FACES:
        pl.semaphore_signal(barrier, inc=1, device_id={AXES[d]: behind[d]}, device_id_type=MESH)

        @pl.when(me[d] != size[d] - 1)
        def _(d=d):
            pl.semaphore_signal(barrier, inc=1, device_id={AXES[d]: ahead[d]}, device_id_type=MESH)

    arrivals = 6 - sum(is_first[d].astype(jnp.int32) for d in FACES)
    x_load = pltpu.make_async_copy(x_hbm, x_buf, load_sem.at[4])
    x_load.start()
    u_load = {}
    for d in (T_DIR, Z_DIR, Y_DIR, X_DIR):
        u_load[d] = pltpu.make_async_copy(u_hbm.at[d], u_buf.at[d], load_sem.at[d])
        u_load[d].start()

    def link(d, slot, there):
        n = 3 * (d - 1) + slot
        return pltpu.make_async_remote_copy(
            src_ref=send_buf[d].at[slot],
            dst_ref=recv_buf[d].at[slot],
            send_sem=send_sem.at[n],
            recv_sem=recv_sem.at[n],
            device_id={AXES[d]: there},
            device_id_type=MESH,
        )

    forward = {d: link(d, 0, behind[d]) for d in FACES}
    backward = {d: link(d, 1, ahead[d]) for d in FACES}
    upward = {d: link(d, 2, behind[d]) for d in FACES}

    m = masks()
    last_t = jnp.where(me[T_DIR] == size[T_DIR] - 1, -1.0, 1.0).astype(jnp.float32)
    first_t = jnp.where(me[T_DIR] == 0, -1.0, 1.0).astype(jnp.float32)
    ahead_sign = {T_DIR: last_t, Z_DIR: None, Y_DIR: None}
    behind_sign = {T_DIR: first_t, Z_DIR: None, Y_DIR: None}

    x_load.wait()
    psi = [unpack(m, x_buf[3 * s:3 * s + 3, 0:8], x_buf[3 * s:3 * s + 3, 8:16]) for s in range(4)]
    minus = {}
    plus = {}
    for d in FACES:
        minus[d] = project(d, -1, psi)
        stage_face(m, d, 0, minus[d], send_buf[d].at[0])

    def links(d):
        first, second = unpack(m, u_buf[d, :, 0:8], u_buf[d, :, 8:16])
        return first.reshape(3, 3, 8, 128), second.reshape(3, 3, 8, 128)

    u = {}
    back = {}
    for d in FACES:
        u_load[d].wait()
        u[d] = links(d)
        plus[d] = project(d, 1, psi)
        back[d] = adjoint_times(u[d], plus[d])
        stage_face(m, d, 1, back[d], send_buf[d].at[1])

    pl.semaphore_wait(barrier, arrivals)
    for d in FACES:
        backward[d].start()
    for d in FACES:
        pl.when(jnp.logical_not(is_first[d]))(forward[d].start)

    zero = jnp.zeros((3, 8, 128), jnp.float32)
    hop = [(zero, zero)] * 4
    d = X_DIR
    u_load[d].wait()
    u[d] = links(d)
    plus[d] = project(d, 1, psi)
    minus[d] = project(d, -1, psi)
    moved = {}
    moved[d] = link_times(u[d], shift_x(m, minus[d], 1))
    hop = add_spins(d, -1, hop, moved[d])
    hop = add_spins(d, 1, hop, shift_x(m, adjoint_times(u[d], plus[d]), -1))

    def take_backward(d, hop):
        backward[d].wait_recv()
        pl.when(is_first[d])(forward[d].start)
        there = shift_face(m, d, -1, back[d], recv_buf[d].at[1], behind_sign[d])
        return add_spins(d, 1, hop, there)

    def take_forward(d, hop):
        forward[d].wait_recv()
        there = shift_face(m, d, 1, minus[d], recv_buf[d].at[0], ahead_sign[d])
        moved[d] = link_times(u[d], there)
        return add_spins(d, -1, hop, moved[d])

    for d in (Z_DIR, T_DIR):
        hop = take_backward(d, hop)
    for d in (Z_DIR, T_DIR, Y_DIR):
        hop = take_forward(d, hop)
    hop = take_backward(Y_DIR, hop)

    result = [
        (pr - KAPPA * hr, pi - KAPPA * hi) for (pr, pi), (hr, hi) in zip(psi, hop)
    ]
    later = {}
    for d in (Z_DIR, T_DIR, Y_DIR):
        later[d] = project(d, 1, result)
        stage_face(m, d, 0, later[d], send_buf[d].at[2])
        upward[d].start()
    for s, (re, im) in enumerate(result):
        y_buf[3 * s:3 * s + 3, 0:8] = pack_first(m, re, im)
        y_buf[3 * s:3 * s + 3, 8:16] = pack_second(m, re, im)

    def finish(d, first, later_there):
        second = outer(link_times(u[d], later_there), plus[d])
        wr, wi = c_add(first, second)
        third = (wi[0, 0] + wi[1, 1] + wi[2, 2]) / 3.0
        for a in range(3):
            for b in range(a, 3):
                if a == b:
                    im = KAPPA * (wi[a, a] - third)
                    re = jnp.zeros_like(im)
                else:
                    re = (0.5 * KAPPA) * (wr[a, b] - wr[b, a])
                    im = (0.5 * KAPPA) * (wi[a, b] + wi[b, a])
                top = pack_first(m, re, im)
                bottom = pack_second(m, re, im)
                f_buf[d, 3 * a + b, 0:8] = top
                f_buf[d, 3 * a + b, 8:16] = bottom
                if a != b:
                    f_buf[d, 3 * b + a, 0:8] = pick(m["low"], -top, top)
                    f_buf[d, 3 * b + a, 8:16] = pick(m["low"], -bottom, bottom)

    d = X_DIR
    finish(d, outer(moved[d], project(d, -1, result)), shift_x(m, project(d, 1, result), 1))
    first = {d: outer(moved[d], project(d, -1, result)) for d in FACES}
    for d in (Y_DIR, T_DIR, Z_DIR):
        upward[d].wait_recv()
        finish(d, first[d], shift_face(m, d, 1, later[d], recv_buf[d].at[2], ahead_sign[d]))
    for d in FACES:
        forward[d].wait_send()
        backward[d].wait_send()
        upward[d].wait_send()


def store_kernel(y_in, f_in, y_out, f_out, sems):
    copies = [pltpu.make_async_copy(y_in, y_out, sems.at[4])]
    copies += [pltpu.make_async_copy(f_in.at[d], f_out.at[d], sems.at[d]) for d in range(4)]
    for copy in copies:
        copy.start()
    for copy in copies:
        copy.wait()


def body(quark_field, gauge_links):
    x = quark_field.reshape(12, 16, 128)
    u = gauge_links.reshape(4, 9, 16, 128)
    faces = [pltpu.VMEM((3, FACE_TILES[d], 8, 128), jnp.float32) for d in FACES]
    y, f = pl.pallas_call(
        kernel,
        out_shape=(pltpu.VMEM(x.shape, jnp.float32), pltpu.VMEM(u.shape, jnp.float32)),
        in_specs=[pl.BlockSpec(memory_space=pltpu.HBM)] * 2,
        out_specs=(pl.BlockSpec(memory_space=pltpu.VMEM),) * 2,
        scratch_shapes=[
            pltpu.VMEM(x.shape, jnp.float32),
            pltpu.VMEM(u.shape, jnp.float32),
            *faces,
            *faces,
            pltpu.SemaphoreType.DMA((5,)),
            pltpu.SemaphoreType.DMA((9,)),
            pltpu.SemaphoreType.DMA((9,)),
        ],
        compiler_params=pltpu.CompilerParams(collective_id=0, has_side_effects=True, vmem_limit_bytes=16 * 1024 * 1024),
        cost_estimate=pl.CostEstimate(flops=6_000_000, bytes_accessed=800_000, transcendentals=0),
    )(pltpu.with_memory_space_constraint(x, pltpu.HBM), pltpu.with_memory_space_constraint(u, pltpu.HBM))
    y, f = pl.pallas_call(
        store_kernel,
        out_shape=(
            jax.ShapeDtypeStruct(x.shape, jnp.float32),
            jax.ShapeDtypeStruct(u.shape, jnp.float32),
        ),
        in_specs=[pl.BlockSpec(memory_space=pltpu.VMEM)] * 2,
        out_specs=(pl.BlockSpec(memory_space=pl.ANY),) * 2,
        scratch_shapes=[pltpu.SemaphoreType.DMA((5,))],
        compiler_params=pltpu.CompilerParams(vmem_limit_bytes=16 * 1024 * 1024),
        cost_estimate=pl.CostEstimate(flops=0, bytes_accessed=800_000, transcendentals=0),
    )(y, f)
    return y.reshape(quark_field.shape), f.reshape(gauge_links.shape)


def solution(mesh):
    specs = (
        P(None, None, "ta", "gz", "gy", None),
        P(None, None, None, "ta", "gz", "gy", None),
    )
    return jax.shard_map(body, mesh=mesh, in_specs=specs, out_specs=specs, check_vma=False)
```

```python
import functools

import jax
import jax.numpy as jnp
from jax import lax
from jax.experimental import pallas as pl
from jax.experimental.pallas import tpu as pltpu
from jax.sharding import PartitionSpec as P

KAPPA = 0.125
MESH = pl.DeviceIdType.MESH
X_DIR, Y_DIR, Z_DIR, T_DIR = 0, 1, 2, 3
AXES = {T_DIR: "ta", Z_DIR: "gz", Y_DIR: "gy"}
FACES = (T_DIR, Z_DIR, Y_DIR)
FACE_TILES = {T_DIR: 6, Z_DIR: 3, Y_DIR: 6}


def lane_roll(v, steps):
    return pltpu.roll(v.reshape(-1, 128), steps, 1).reshape(v.shape)


def row_roll(v, steps):
    if steps % 8 == 0:
        return v
    flat = v.reshape(-1, 8, 128)
    return jnp.stack([pltpu.roll(flat[i], steps % 8, 0) for i in range(flat.shape[0])]).reshape(v.shape)


def masks(at_start):
    lane = lax.broadcasted_iota(jnp.int32, (8, 128), 1)
    row = lax.broadcasted_iota(jnp.int32, (8, 128), 0)
    return {
        "low": lane < 64,
        "last_x": lane % 64 == 63,
        "first_x": lane % 64 == 0,
        "even": row % 2 == 0,
        "z_first": row < 2,
        "z_last": row >= 6,
        "row": row,
        "halo_now": row % 2 + at_start == 0,
        "halo_late": row % 2 + (1 - at_start) == 0,
        "edge_t": (row % 2 + (1 - at_start) == 0) & (lane >= 64),
        "edge_z": row + 8 * (1 - at_start) == 6,
    }


def pick(mask, a, b):
    return jnp.where(jnp.broadcast_to(mask, a.shape), a, b)


def unpack(m, first, second):
    return (
        pick(m["low"], first, lane_roll(second, 64)),
        pick(m["low"], lane_roll(first, 64), second),
    )


def pack_first(m, re, im):
    return pick(m["low"], re, lane_roll(im, 64))


def pack_second(m, re, im):
    return pick(m["low"], lane_roll(re, 64), im)


def c_add(a, b):
    return (a[0] + b[0], a[1] + b[1])


def c_sub(a, b):
    return (a[0] - b[0], a[1] - b[1])


def add_i(a, b):
    return (a[0] - b[1], a[1] + b[0])


def sub_i(a, b):
    return (a[0] + b[1], a[1] - b[0])


def project(direction, sign, psi):
    u0, u1, l0, l1 = psi
    plus, minus = (c_add, c_sub) if sign < 0 else (c_sub, c_add)
    plus_i, minus_i = (add_i, sub_i) if sign < 0 else (sub_i, add_i)
    if direction == X_DIR:
        return [plus_i(u0, l1), plus_i(u1, l0)]
    if direction == Y_DIR:
        return [plus(u0, l1), minus(u1, l0)]
    if direction == Z_DIR:
        return [plus_i(u0, l0), minus_i(u1, l1)]
    return [minus(u0, l0), minus(u1, l1)]


def add_spins(direction, sign, total, half):
    h0, h1 = half
    plus, minus = (c_sub, c_add) if sign < 0 else (c_add, c_sub)
    plus_i, minus_i = (sub_i, add_i) if sign < 0 else (add_i, sub_i)
    t0, t1, t2, t3 = total
    upper = [c_add(t0, h0), c_add(t1, h1)]
    if direction == X_DIR:
        return upper + [plus_i(t2, h1), plus_i(t3, h0)]
    if direction == Y_DIR:
        return upper + [plus(t2, h1), minus(t3, h0)]
    if direction == Z_DIR:
        return upper + [plus_i(t2, h0), minus_i(t3, h1)]
    return upper + [plus(t2, h0), plus(t3, h1)]


def link_times(u, half):
    ur, ui = u
    out = []
    for hr, hi in half:
        re = im = None
        for b in range(3):
            cr, ci = ur[:, b], ui[:, b]
            r = cr * hr[b][None] - ci * hi[b][None]
            i = cr * hi[b][None] + ci * hr[b][None]
            re = r if re is None else re + r
            im = i if im is None else im + i
        out.append((re, im))
    return out


def adjoint_times(u, half):
    ur, ui = u
    out = []
    for hr, hi in half:
        re = im = None
        for b in range(3):
            cr, ci = ur[b], ui[b]
            r = cr * hr[b][None] + ci * hi[b][None]
            i = cr * hi[b][None] - ci * hr[b][None]
            re = r if re is None else re + r
            im = i if im is None else im + i
        out.append((re, im))
    return out


def outer(left, right):
    re = im = None
    for (lr, li), (rr, ri) in zip(left, right):
        r = lr[:, None] * rr[None] + li[:, None] * ri[None]
        i = li[:, None] * rr[None] - lr[:, None] * ri[None]
        re = r if re is None else re + r
        im = i if im is None else im + i
    return re, im


def shift_x(m, half, steps):
    def one(v):
        if steps > 0:
            return pick(m["last_x"], lane_roll(v, 63), lane_roll(v, 127))
        return pick(m["first_x"], lane_roll(v, 65), lane_roll(v, 1))

    return [(one(re), one(im)) for re, im in half]


def stage_face(m, direction, end, half, ref):
    if direction == T_DIR:
        for s, (re, im) in enumerate(half):
            ref[3 * s:3 * s + 3] = (pack_second if end else pack_first)(m, re, im)
    elif direction == Y_DIR:
        for s, (re, im) in enumerate(half):
            if end:
                tile = pick(m["even"], row_roll(re, -1), im)
            else:
                tile = pick(m["even"], re, row_roll(im, 1))
            ref[3 * s:3 * s + 3] = tile
    else:
        tiles = [part[c] for re, im in half for part in (re, im) for c in range(3)]
        for j in range(3):
            tile = row_roll(tiles[4 * j], 2 if end else 0)
            for k in range(1, 4):
                moved = row_roll(tiles[4 * j + k], 2 * k + (2 if end else 0))
                tile = pick(m["row"] < 2 * k, tile, moved)
            ref[j] = tile


def shift_face(m, direction, steps, half, ref, sign):
    out = []
    if direction == T_DIR:
        for s, (re, im) in enumerate(half):
            face = ref[3 * s:3 * s + 3] * sign
            if steps > 0:
                out.append((
                    lane_roll(pick(m["low"], face, re), 64),
                    pick(m["low"], lane_roll(im, 64), face),
                ))
            else:
                out.append((
                    pick(m["low"], face, lane_roll(re, 64)),
                    lane_roll(pick(m["low"], im, face), 64),
                ))
    elif direction == Y_DIR:
        for s, (re, im) in enumerate(half):
            face = ref[3 * s:3 * s + 3]
            if steps > 0:
                out.append((
                    pick(m["even"], row_roll(re, -1), row_roll(face, 1)),
                    pick(m["even"], row_roll(im, -1), face),
                ))
            else:
                out.append((
                    pick(m["even"], face, row_roll(re, 1)),
                    pick(m["even"], row_roll(face, -1), row_roll(im, 1)),
                ))
    else:
        n = 0
        for re, im in half:
            parts = []
            for part in (re, im):
                moved = []
                for c in range(3):
                    face = ref[n // 4]
                    k = n % 4
                    n += 1
                    if steps > 0:
                        moved.append(row_roll(pick(m["z_first"], row_roll(face, -2 * k), part[c]), -2))
                    else:
                        moved.append(row_roll(pick(m["z_last"], row_roll(face, 6 - 2 * k), part[c]), 2))
                parts.append(jnp.stack(moved))
            out.append(tuple(parts))
    return out


def only(mask, v):
    return pick(mask, v, jnp.zeros_like(v))


def local_y(m, half):
    return [tuple(pick(m["even"], jnp.zeros_like(v), row_roll(v, 1)) for v in parts) for parts in half]


def face_y(mask, ref, steps=0):
    out = []
    for s in range(2):
        face = ref[3 * s:3 * s + 3]
        if steps:
            face = lane_roll(face, steps)
        out.append((only(mask, face), only(mask, row_roll(face, -1))))
    return out


def edge_term(direction, half):
    h0, h1 = half
    return project(direction, 1, [h0, h1, h1, (-h0[0], -h0[1])])


def kernel(
    x_hbm, u_hbm, y_buf, f_buf,
    x_buf, u_buf,
    st_t, st_z, st_y, rt_t, rt_z, rt_y, y_now, edge_t, edge_z,
    load_sem, send_sem, recv_sem, here_sem,
):
    send_buf = {T_DIR: st_t, Z_DIR: st_z, Y_DIR: st_y}
    recv_buf = {T_DIR: rt_t, Z_DIR: rt_z, Y_DIR: rt_y}
    me = {d: lax.axis_index(AXES[d]) for d in FACES}
    size = {d: lax.axis_size(AXES[d]) for d in FACES}
    ahead = {d: lax.rem(me[d] + 1, size[d]) for d in FACES}
    behind = {d: lax.rem(me[d] + size[d] - 1, size[d]) for d in FACES}

    barrier = pltpu.get_barrier_semaphore()
    is_first = {d: me[d] == 0 for d in FACES}
    for d in FACES:
        pl.semaphore_signal(barrier, inc=1, device_id={AXES[d]: behind[d]}, device_id_type=MESH)

        @pl.when(me[d] != size[d] - 1)
        def _(d=d):
            pl.semaphore_signal(barrier, inc=1, device_id={AXES[d]: ahead[d]}, device_id_type=MESH)

    is_last_y = me[Y_DIR] == size[Y_DIR] - 1

    @pl.when(is_first[Y_DIR])
    def _():
        for d in (T_DIR, Z_DIR):
            there = {AXES[d]: ahead[d], AXES[Y_DIR]: behind[Y_DIR]}
            pl.semaphore_signal(barrier, inc=1, device_id=there, device_id_type=MESH)

    arrivals = 6 - sum(is_first[d].astype(jnp.int32) for d in FACES) + 2 * is_last_y.astype(jnp.int32)
    x_load = pltpu.make_async_copy(x_hbm, x_buf, load_sem.at[4])
    x_load.start()
    u_load = {}
    for d in (T_DIR, Z_DIR, Y_DIR, X_DIR):
        u_load[d] = pltpu.make_async_copy(u_hbm.at[d], u_buf.at[d], load_sem.at[d])
        u_load[d].start()

    def link(d, slot, there):
        n = 3 * (d - 1) + slot
        return pltpu.make_async_remote_copy(
            src_ref=send_buf[d].at[slot],
            dst_ref=recv_buf[d].at[slot],
            send_sem=send_sem.at[n],
            recv_sem=recv_sem.at[n],
            device_id={AXES[d]: there},
            device_id_type=MESH,
        )

    forward = {d: link(d, 0, behind[d]) for d in FACES}
    backward = {d: link(d, 1, ahead[d]) for d in FACES}
    upward = {d: link(d, 2, behind[d]) for d in FACES}

    def edge_link(n, d, src, dst):
        return pltpu.make_async_remote_copy(
            src_ref=src,
            dst_ref=dst,
            send_sem=send_sem.at[n],
            recv_sem=recv_sem.at[n],
            device_id={AXES[d]: behind[d], AXES[Y_DIR]: ahead[Y_DIR]},
            device_id_type=MESH,
        )

    edges = {
        T_DIR: edge_link(9, T_DIR, st_y.at[1], edge_t),
        Z_DIR: edge_link(10, Z_DIR, st_y.at[1, :, 0:2], edge_z.at[:, 6:8]),
    }

    here = {T_DIR: here_sem.at[0], Z_DIR: here_sem.at[1]}

    def say_here():
        for d in (T_DIR, Z_DIR):

            @pl.when(me[d] == size[d] - 1)
            def _(d=d):
                pl.semaphore_signal(here[d], inc=1, device_id={AXES[d]: ahead[d]}, device_id_type=MESH)

    def greeted(d):
        pl.semaphore_wait(here[d], 1)
        forward[d].start()

    m = masks(is_first[Y_DIR].astype(jnp.int32))
    last_t = jnp.where(me[T_DIR] == size[T_DIR] - 1, -1.0, 1.0).astype(jnp.float32)
    first_t = jnp.where(me[T_DIR] == 0, -1.0, 1.0).astype(jnp.float32)
    ahead_sign = {T_DIR: last_t, Z_DIR: None, Y_DIR: None}
    behind_sign = {T_DIR: first_t, Z_DIR: None, Y_DIR: None}

    x_load.wait()
    psi = [unpack(m, x_buf[3 * s:3 * s + 3, 0:8], x_buf[3 * s:3 * s + 3, 8:16]) for s in range(4)]
    minus = {}
    plus = {}
    for d in FACES:
        minus[d] = project(d, -1, psi)
        stage_face(m, d, 0, minus[d], send_buf[d].at[0])

    def links(d):
        first, second = unpack(m, u_buf[d, :, 0:8], u_buf[d, :, 8:16])
        return first.reshape(3, 3, 8, 128), second.reshape(3, 3, 8, 128)

    u = {}
    back = {}
    for d in FACES:
        u_load[d].wait()
        u[d] = links(d)
        plus[d] = project(d, 1, psi)
        back[d] = adjoint_times(u[d], plus[d])
        stage_face(m, d, 1, back[d], send_buf[d].at[1])

    pl.semaphore_wait(barrier, arrivals)
    backward[Y_DIR].start()

    @pl.when(is_last_y)
    def _():
        edges[T_DIR].start()
        edges[Z_DIR].start()

    say_here()
    for d in (T_DIR, Z_DIR):
        backward[d].start()
    for d in FACES:
        pl.when(jnp.logical_not(is_first[d]))(forward[d].start)
    for d in (T_DIR, Z_DIR):
        pl.when(is_first[d])(functools.partial(greeted, d))

    zero = jnp.zeros((3, 8, 128), jnp.float32)
    hop = [(zero, zero)] * 4
    d = X_DIR
    u_load[d].wait()
    u[d] = links(d)
    plus[d] = project(d, 1, psi)
    minus[d] = project(d, -1, psi)
    moved = {}
    moved[d] = link_times(u[d], shift_x(m, minus[d], 1))
    hop = add_spins(d, -1, hop, moved[d])
    hop = add_spins(d, 1, hop, shift_x(m, adjoint_times(u[d], plus[d]), -1))

    def take_backward(d, hop):
        backward[d].wait_recv()
        there = shift_face(m, d, -1, back[d], recv_buf[d].at[1], behind_sign[d])
        return add_spins(d, 1, hop, there)

    def take_forward(d, hop):
        forward[d].wait_recv()
        there = shift_face(m, d, 1, minus[d], recv_buf[d].at[0], ahead_sign[d])
        moved[d] = link_times(u[d], there)
        return add_spins(d, -1, hop, moved[d])

    for d in (Z_DIR, T_DIR):
        hop = take_backward(d, hop)
    for d in (Z_DIR, T_DIR, Y_DIR):
        hop = take_forward(d, hop)
    hop = add_spins(Y_DIR, 1, hop, local_y(m, back[Y_DIR]))

    @pl.when(jnp.logical_not(is_first[Y_DIR]))
    def _():
        backward[Y_DIR].wait_recv()
        y_now[...] = rt_y[1]

    hop = add_spins(Y_DIR, 1, hop, face_y(m["halo_now"], y_now))
    early = [
        (pr - KAPPA * hr, pi - KAPPA * hi) for (pr, pi), (hr, hi) in zip(psi, hop)
    ]
    for d in (Z_DIR, T_DIR):
        stage_face(m, d, 0, project(d, 1, early), send_buf[d].at[2])
        upward[d].start()

    @pl.when(is_first[Y_DIR])
    def _():
        backward[Y_DIR].wait_recv()
        forward[Y_DIR].start()

    zero_spins = [(zero, zero)] * 4
    missing = add_spins(Y_DIR, 1, zero_spins, face_y(m["halo_late"], rt_y.at[1]))
    result = [
        (er - KAPPA * lr, ei - KAPPA * li) for (er, ei), (lr, li) in zip(early, missing)
    ]
    later = {d: project(d, 1, result) for d in FACES}
    stage_face(m, Y_DIR, 0, later[Y_DIR], send_buf[Y_DIR].at[2])
    upward[Y_DIR].start()
    for s, (re, im) in enumerate(result):
        y_buf[3 * s:3 * s + 3, 0:8] = pack_first(m, re, im)
        y_buf[3 * s:3 * s + 3, 8:16] = pack_second(m, re, im)

    def finish(d, first, later_there):
        second = outer(link_times(u[d], later_there), plus[d])
        wr, wi = c_add(first, second)
        third = (wi[0, 0] + wi[1, 1] + wi[2, 2]) / 3.0
        for a in range(3):
            for b in range(a, 3):
                if a == b:
                    im = KAPPA * (wi[a, a] - third)
                    re = jnp.zeros_like(im)
                else:
                    re = (0.5 * KAPPA) * (wr[a, b] - wr[b, a])
                    im = (0.5 * KAPPA) * (wi[a, b] + wi[b, a])
                top = pack_first(m, re, im)
                bottom = pack_second(m, re, im)
                f_buf[d, 3 * a + b, 0:8] = top
                f_buf[d, 3 * a + b, 8:16] = bottom
                if a != b:
                    f_buf[d, 3 * b + a, 0:8] = pick(m["low"], -top, top)
                    f_buf[d, 3 * b + a, 8:16] = pick(m["low"], -bottom, bottom)

    d = X_DIR
    finish(d, outer(moved[d], project(d, -1, result)), shift_x(m, project(d, 1, result), 1))
    first = {d: outer(moved[d], project(d, -1, result)) for d in FACES}
    upward[Y_DIR].wait_recv()
    finish(Y_DIR, first[Y_DIR], shift_face(m, Y_DIR, 1, later[Y_DIR], recv_buf[Y_DIR].at[2], None))
    edge_half = {
        T_DIR: lambda: face_y(m["edge_t"], edge_t, 64),
        Z_DIR: lambda: face_y(m["edge_z"], edge_z),
    }
    for d in (T_DIR, Z_DIR):
        upward[d].wait_recv()
        there = shift_face(m, d, 1, later[d], recv_buf[d].at[2], ahead_sign[d])
        pl.when(is_first[Y_DIR])(edges[d].wait_recv)
        scale = KAPPA * last_t if d == T_DIR else KAPPA
        extra = edge_term(d, edge_half[d]())
        there = [
            (tr - scale * er, ti - scale * ei) for (tr, ti), (er, ei) in zip(there, extra)
        ]
        finish(d, first[d], there)
    for d in FACES:
        forward[d].wait_send()
        backward[d].wait_send()
        upward[d].wait_send()

    @pl.when(is_last_y)
    def _():
        edges[T_DIR].wait_send()
        edges[Z_DIR].wait_send()


def store_kernel(y_in, f_in, y_out, f_out, sems):
    copies = [pltpu.make_async_copy(y_in, y_out, sems.at[4])]
    copies += [pltpu.make_async_copy(f_in.at[d], f_out.at[d], sems.at[d]) for d in range(4)]
    for copy in copies:
        copy.start()
    for copy in copies:
        copy.wait()


def body(quark_field, gauge_links):
    x = quark_field.reshape(12, 16, 128)
    u = gauge_links.reshape(4, 9, 16, 128)
    faces = [pltpu.VMEM((3, FACE_TILES[d], 8, 128), jnp.float32) for d in FACES]
    y, f = pl.pallas_call(
        kernel,
        out_shape=(pltpu.VMEM(x.shape, jnp.float32), pltpu.VMEM(u.shape, jnp.float32)),
        in_specs=[pl.BlockSpec(memory_space=pltpu.HBM)] * 2,
        out_specs=(pl.BlockSpec(memory_space=pltpu.VMEM),) * 2,
        scratch_shapes=[
            pltpu.VMEM(x.shape, jnp.float32),
            pltpu.VMEM(u.shape, jnp.float32),
            *faces,
            *faces,
            pltpu.VMEM((6, 8, 128), jnp.float32),
            pltpu.VMEM((6, 8, 128), jnp.float32),
            pltpu.VMEM((6, 8, 128), jnp.float32),
            pltpu.SemaphoreType.DMA((5,)),
            pltpu.SemaphoreType.DMA((11,)),
            pltpu.SemaphoreType.DMA((11,)),
            pltpu.SemaphoreType.REGULAR((2,)),
        ],
        compiler_params=pltpu.CompilerParams(collective_id=0, has_side_effects=True, vmem_limit_bytes=16 * 1024 * 1024),
        cost_estimate=pl.CostEstimate(flops=6_000_000, bytes_accessed=800_000, transcendentals=0),
    )(pltpu.with_memory_space_constraint(x, pltpu.HBM), pltpu.with_memory_space_constraint(u, pltpu.HBM))
    y, f = pl.pallas_call(
        store_kernel,
        out_shape=(
            jax.ShapeDtypeStruct(x.shape, jnp.float32),
            jax.ShapeDtypeStruct(u.shape, jnp.float32),
        ),
        in_specs=[pl.BlockSpec(memory_space=pltpu.VMEM)] * 2,
        out_specs=(pl.BlockSpec(memory_space=pl.ANY),) * 2,
        scratch_shapes=[pltpu.SemaphoreType.DMA((5,))],
        compiler_params=pltpu.CompilerParams(vmem_limit_bytes=16 * 1024 * 1024),
        cost_estimate=pl.CostEstimate(flops=0, bytes_accessed=800_000, transcendentals=0),
    )(y, f)
    return y.reshape(quark_field.shape), f.reshape(gauge_links.shape)


def solution(mesh):
    specs = (
        P(None, None, "ta", "gz", "gy", None),
        P(None, None, None, "ta", "gz", "gy", None),
    )
    return jax.shard_map(body, mesh=mesh, in_specs=specs, out_specs=specs, check_vma=False)
```

```python
import functools

import jax
import jax.numpy as jnp
from jax import lax
from jax.experimental import pallas as pl
from jax.experimental.pallas import tpu as pltpu
from jax.sharding import PartitionSpec as P

KAPPA = 0.125
MESH = pl.DeviceIdType.MESH
X_DIR, Y_DIR, Z_DIR, T_DIR = 0, 1, 2, 3
AXES = {T_DIR: "ta", Z_DIR: "gz", Y_DIR: "gy"}
FACES = (T_DIR, Z_DIR, Y_DIR)
FACE_TILES = {T_DIR: 6, Z_DIR: 3, Y_DIR: 6}


def lane_roll(v, steps):
    return pltpu.roll(v.reshape(-1, 128), steps, 1).reshape(v.shape)


def row_roll(v, steps):
    if steps % 8 == 0:
        return v
    flat = v.reshape(-1, 8, 128)
    return jnp.stack([pltpu.roll(flat[i], steps % 8, 0) for i in range(flat.shape[0])]).reshape(v.shape)


def masks(at_start, at_end):
    lane = lax.broadcasted_iota(jnp.int32, (8, 128), 1)
    row = lax.broadcasted_iota(jnp.int32, (8, 128), 0)
    return {
        "low": lane < 64,
        "last_x": lane % 64 == 63,
        "first_x": lane % 64 == 0,
        "even": row % 2 == 0,
        "z_first": row < 2,
        "z_last": row >= 6,
        "row": row,
        "halo_now": row % 2 + at_start == 0,
        "halo_late": row % 2 + (1 - at_start) == 0,
        "own_y": row % 2 * at_end == 1,
        "edge_t": (row % 2 + (1 - at_start) == 0) & (lane >= 64),
        "edge_z": row + 8 * (1 - at_start) == 6,
    }


def pick(mask, a, b):
    return jnp.where(jnp.broadcast_to(mask, a.shape), a, b)


def unpack(m, first, second):
    return (
        pick(m["low"], first, lane_roll(second, 64)),
        pick(m["low"], lane_roll(first, 64), second),
    )


def pack_first(m, re, im):
    return pick(m["low"], re, lane_roll(im, 64))


def pack_second(m, re, im):
    return pick(m["low"], lane_roll(re, 64), im)


def c_add(a, b):
    return (a[0] + b[0], a[1] + b[1])


def c_sub(a, b):
    return (a[0] - b[0], a[1] - b[1])


def add_i(a, b):
    return (a[0] - b[1], a[1] + b[0])


def sub_i(a, b):
    return (a[0] + b[1], a[1] - b[0])


def project(direction, sign, psi):
    u0, u1, l0, l1 = psi
    plus, minus = (c_add, c_sub) if sign < 0 else (c_sub, c_add)
    plus_i, minus_i = (add_i, sub_i) if sign < 0 else (sub_i, add_i)
    if direction == X_DIR:
        return [plus_i(u0, l1), plus_i(u1, l0)]
    if direction == Y_DIR:
        return [plus(u0, l1), minus(u1, l0)]
    if direction == Z_DIR:
        return [plus_i(u0, l0), minus_i(u1, l1)]
    return [minus(u0, l0), minus(u1, l1)]


def add_spins(direction, sign, total, half):
    h0, h1 = half
    plus, minus = (c_sub, c_add) if sign < 0 else (c_add, c_sub)
    plus_i, minus_i = (sub_i, add_i) if sign < 0 else (add_i, sub_i)
    t0, t1, t2, t3 = total
    upper = [c_add(t0, h0), c_add(t1, h1)]
    if direction == X_DIR:
        return upper + [plus_i(t2, h1), plus_i(t3, h0)]
    if direction == Y_DIR:
        return upper + [plus(t2, h1), minus(t3, h0)]
    if direction == Z_DIR:
        return upper + [plus_i(t2, h0), minus_i(t3, h1)]
    return upper + [plus(t2, h0), plus(t3, h1)]


def link_times(u, half):
    ur, ui = u
    out = []
    for hr, hi in half:
        re = im = None
        for b in range(3):
            cr, ci = ur[:, b], ui[:, b]
            r = cr * hr[b][None] - ci * hi[b][None]
            i = cr * hi[b][None] + ci * hr[b][None]
            re = r if re is None else re + r
            im = i if im is None else im + i
        out.append((re, im))
    return out


def adjoint_times(u, half):
    ur, ui = u
    out = []
    for hr, hi in half:
        re = im = None
        for b in range(3):
            cr, ci = ur[b], ui[b]
            r = cr * hr[b][None] + ci * hi[b][None]
            i = cr * hi[b][None] - ci * hr[b][None]
            re = r if re is None else re + r
            im = i if im is None else im + i
        out.append((re, im))
    return out


def outer(left, right):
    re = im = None
    for (lr, li), (rr, ri) in zip(left, right):
        r = lr[:, None] * rr[None] + li[:, None] * ri[None]
        i = li[:, None] * rr[None] - lr[:, None] * ri[None]
        re = r if re is None else re + r
        im = i if im is None else im + i
    return re, im


def shift_x(m, half, steps):
    def one(v):
        if steps > 0:
            return pick(m["last_x"], lane_roll(v, 63), lane_roll(v, 127))
        return pick(m["first_x"], lane_roll(v, 65), lane_roll(v, 1))

    return [(one(re), one(im)) for re, im in half]


def stage_face(m, direction, end, half, ref):
    if direction == T_DIR:
        for s, (re, im) in enumerate(half):
            ref[3 * s:3 * s + 3] = (pack_second if end else pack_first)(m, re, im)
    elif direction == Y_DIR:
        for s, (re, im) in enumerate(half):
            if end:
                tile = pick(m["even"], row_roll(re, -1), im)
            else:
                tile = pick(m["even"], re, row_roll(im, 1))
            ref[3 * s:3 * s + 3] = tile
    else:
        tiles = [part[c] for re, im in half for part in (re, im) for c in range(3)]
        for j in range(3):
            tile = row_roll(tiles[4 * j], 2 if end else 0)
            for k in range(1, 4):
                moved = row_roll(tiles[4 * j + k], 2 * k + (2 if end else 0))
                tile = pick(m["row"] < 2 * k, tile, moved)
            ref[j] = tile


def shift_face(m, direction, steps, half, ref, sign):
    out = []
    if direction == T_DIR:
        for s, (re, im) in enumerate(half):
            face = ref[3 * s:3 * s + 3] * sign
            if steps > 0:
                out.append((
                    lane_roll(pick(m["low"], face, re), 64),
                    pick(m["low"], lane_roll(im, 64), face),
                ))
            else:
                out.append((
                    pick(m["low"], face, lane_roll(re, 64)),
                    lane_roll(pick(m["low"], im, face), 64),
                ))
    elif direction == Y_DIR:
        for s, (re, im) in enumerate(half):
            face = ref[3 * s:3 * s + 3]
            if steps > 0:
                out.append((
                    pick(m["even"], row_roll(re, -1), row_roll(face, 1)),
                    pick(m["even"], row_roll(im, -1), face),
                ))
            else:
                out.append((
                    pick(m["even"], face, row_roll(re, 1)),
                    pick(m["even"], row_roll(face, -1), row_roll(im, 1)),
                ))
    else:
        n = 0
        for re, im in half:
            parts = []
            for part in (re, im):
                moved = []
                for c in range(3):
                    face = ref[n // 4]
                    k = n % 4
                    n += 1
                    if steps > 0:
                        moved.append(row_roll(pick(m["z_first"], row_roll(face, -2 * k), part[c]), -2))
                    else:
                        moved.append(row_roll(pick(m["z_last"], row_roll(face, 6 - 2 * k), part[c]), 2))
                parts.append(jnp.stack(moved))
            out.append(tuple(parts))
    return out


def only(mask, v):
    return pick(mask, v, jnp.zeros_like(v))


def local_y(m, half):
    return [tuple(pick(m["even"], jnp.zeros_like(v), row_roll(v, 1)) for v in parts) for parts in half]


def face_y(mask, faces):
    return [(only(mask, face), only(mask, row_roll(face, -1))) for face in faces]


def both_spins(ref):
    return [ref[0:3], ref[3:6]]


def edge_term(direction, half):
    h0, h1 = half
    return project(direction, 1, [h0, h1, h1, (-h0[0], -h0[1])])


def kernel(
    x_hbm, u_hbm, y_buf, f_buf,
    x_buf, u_buf,
    st_t, st_z, st_y, rt_t, rt_z, rt_y, y_now, edge_out, edge_t, edge_z,
    load_sem, send_sem, recv_sem, here_sem,
):
    send_buf = {T_DIR: st_t, Z_DIR: st_z, Y_DIR: st_y}
    recv_buf = {T_DIR: rt_t, Z_DIR: rt_z, Y_DIR: rt_y}
    x_load = pltpu.make_async_copy(x_hbm, x_buf, load_sem.at[4])
    u_load = {d: pltpu.make_async_copy(u_hbm.at[d], u_buf.at[d], load_sem.at[d]) for d in range(4)}
    x_load.start()
    u_load[Y_DIR].start()
    me = {d: lax.axis_index(AXES[d]) for d in FACES}
    size = {d: lax.axis_size(AXES[d]) for d in FACES}
    ahead = {d: lax.rem(me[d] + 1, size[d]) for d in FACES}
    behind = {d: lax.rem(me[d] + size[d] - 1, size[d]) for d in FACES}

    barrier = pltpu.get_barrier_semaphore()
    is_first = {d: me[d] == 0 for d in FACES}
    is_last = {d: me[d] == size[d] - 1 for d in FACES}
    is_last_y = is_last[Y_DIR]

    def greet(where):
        pl.semaphore_signal(barrier, inc=1, device_id=where, device_id_type=MESH)

    for d in (T_DIR, Z_DIR):
        greet({AXES[d]: behind[d]})
    for d in FACES:
        pl.when(jnp.logical_not(is_last[d]))(functools.partial(greet, {AXES[d]: ahead[d]}))

    @pl.when(is_first[Y_DIR])
    def _():
        greet({AXES[Y_DIR]: behind[Y_DIR]})
        for d in (T_DIR, Z_DIR):
            greet({AXES[d]: ahead[d], AXES[Y_DIR]: behind[Y_DIR]})

    arrivals = 5 - sum(is_first[d].astype(jnp.int32) for d in FACES) + 3 * is_last_y.astype(jnp.int32)
    for d in (T_DIR, Z_DIR, X_DIR):
        u_load[d].start()

    def link(d, slot, there):
        n = 3 * (d - 1) + slot
        return pltpu.make_async_remote_copy(
            src_ref=send_buf[d].at[slot],
            dst_ref=recv_buf[d].at[slot],
            send_sem=send_sem.at[n],
            recv_sem=recv_sem.at[n],
            device_id={AXES[d]: there},
            device_id_type=MESH,
        )

    forward = {d: link(d, 0, behind[d]) for d in FACES}
    backward = {d: link(d, 1, ahead[d]) for d in FACES}
    upward = {d: link(d, 2, behind[d]) for d in FACES}

    def edge_link(n, d, src, dst):
        return pltpu.make_async_remote_copy(
            src_ref=src,
            dst_ref=dst,
            send_sem=send_sem.at[n],
            recv_sem=recv_sem.at[n],
            device_id={AXES[d]: behind[d], AXES[Y_DIR]: ahead[Y_DIR]},
            device_id_type=MESH,
        )

    edges = {
        T_DIR: edge_link(9, T_DIR, edge_out, edge_t),
        Z_DIR: edge_link(10, Z_DIR, st_y.at[1, :, 0:2], edge_z.at[:, 6:8]),
    }

    here = {d: here_sem.at[d - 1] for d in FACES}
    here_ahead = here_sem.at[3]

    def say_here():
        def say(sem, there):
            pl.semaphore_signal(sem, inc=1, device_id=there, device_id_type=MESH)

        for d in FACES:
            pl.when(is_last[d])(functools.partial(say, here[d], {AXES[d]: ahead[d]}))
        there = {AXES[Y_DIR]: behind[Y_DIR]}
        pl.when(jnp.logical_not(is_first[Y_DIR]))(functools.partial(say, here_ahead, there))

    def greeted(d):
        pl.semaphore_wait(here[d], 1)
        forward[d].start()

    m = masks(is_first[Y_DIR].astype(jnp.int32), is_last_y.astype(jnp.int32))
    last_t = jnp.where(me[T_DIR] == size[T_DIR] - 1, -1.0, 1.0).astype(jnp.float32)
    first_t = jnp.where(me[T_DIR] == 0, -1.0, 1.0).astype(jnp.float32)
    ahead_sign = {T_DIR: last_t, Z_DIR: None, Y_DIR: None}
    behind_sign = {T_DIR: first_t, Z_DIR: None, Y_DIR: None}

    x_load.wait()
    psi = [unpack(m, x_buf[3 * s:3 * s + 3, 0:8], x_buf[3 * s:3 * s + 3, 8:16]) for s in range(4)]
    minus = {}
    plus = {}
    u = {}
    back = {}

    def links(d):
        first, second = unpack(m, u_buf[d, :, 0:8], u_buf[d, :, 8:16])
        return first.reshape(3, 3, 8, 128), second.reshape(3, 3, 8, 128)

    def prepare_backward(d):
        u_load[d].wait()
        u[d] = links(d)
        plus[d] = project(d, 1, psi)
        back[d] = adjoint_times(u[d], plus[d])
        stage_face(m, d, 1, back[d], send_buf[d].at[1])

    prepare_backward(Y_DIR)

    @pl.when(is_last_y)
    def _():
        edge_out[...] = pick(m["low"], st_y[1, 0:3], lane_roll(st_y[1, 3:6], 64))
        pl.semaphore_wait(barrier, arrivals)
        edges[Z_DIR].start()
        edges[T_DIR].start()
        backward[Y_DIR].start()
        say_here()

    for d in FACES:
        minus[d] = project(d, -1, psi)
        stage_face(m, d, 0, minus[d], send_buf[d].at[0])
    for d in (T_DIR, Z_DIR):
        prepare_backward(d)

    @pl.when(jnp.logical_not(is_last_y))
    def _():
        pl.semaphore_wait(barrier, arrivals)
        say_here()

    for d in (T_DIR, Z_DIR):
        backward[d].start()
    for d in FACES:
        pl.when(jnp.logical_not(is_first[d]))(forward[d].start)
    for d in (T_DIR, Z_DIR):
        pl.when(is_first[d])(functools.partial(greeted, d))

    @pl.when(jnp.logical_not(is_last_y))
    def _():
        pl.semaphore_wait(here_ahead, 1)
        backward[Y_DIR].start()

    zero = jnp.zeros((3, 8, 128), jnp.float32)
    hop = [(zero, zero)] * 4
    d = X_DIR
    u_load[d].wait()
    u[d] = links(d)
    plus[d] = project(d, 1, psi)
    minus[d] = project(d, -1, psi)
    moved = {}
    moved[d] = link_times(u[d], shift_x(m, minus[d], 1))
    hop = add_spins(d, -1, hop, moved[d])
    hop = add_spins(d, 1, hop, shift_x(m, adjoint_times(u[d], plus[d]), -1))

    def take_backward(d, hop):
        backward[d].wait_recv()
        there = shift_face(m, d, -1, back[d], recv_buf[d].at[1], behind_sign[d])
        return add_spins(d, 1, hop, there)

    def take_forward(d, hop):
        forward[d].wait_recv()
        there = shift_face(m, d, 1, minus[d], recv_buf[d].at[0], ahead_sign[d])
        moved[d] = link_times(u[d], there)
        return add_spins(d, -1, hop, moved[d])

    def wilson(hop):
        return [(pr - KAPPA * hr, pi - KAPPA * hi) for (pr, pi), (hr, hi) in zip(psi, hop)]

    hop = take_backward(Z_DIR, hop)
    hop = take_forward(Z_DIR, hop)
    hop = take_forward(Y_DIR, hop)
    hop = add_spins(Y_DIR, 1, hop, local_y(m, back[Y_DIR]))

    @pl.when(jnp.logical_not(is_first[Y_DIR]))
    def _():
        backward[Y_DIR].wait_recv()
        y_now[...] = rt_y[1]

    hop = add_spins(Y_DIR, 1, hop, face_y(m["halo_now"], both_spins(y_now)))

    inner = [tuple(lane_roll(v, 64) for v in parts) for parts in minus[T_DIR]]
    inner = add_spins(T_DIR, -1, hop, link_times(u[T_DIR], inner))
    stage_face(m, T_DIR, 0, project(T_DIR, 1, wilson(inner)), send_buf[T_DIR].at[2])
    upward[T_DIR].start()
    hop = take_backward(T_DIR, hop)
    hop = take_forward(T_DIR, hop)
    early = wilson(hop)
    for d in (Z_DIR, Y_DIR):
        stage_face(m, d, 0, project(d, 1, early), send_buf[d].at[2])
    upward[Z_DIR].start()
    pl.when(jnp.logical_not(is_first[Y_DIR]))(upward[Y_DIR].start)

    @pl.when(is_first[Y_DIR])
    def _():
        greeted(Y_DIR)
        upward[Y_DIR].start()
        backward[Y_DIR].wait_recv()

    late = face_y(m["halo_late"], both_spins(rt_y.at[1]))
    missing = add_spins(Y_DIR, 1, [(zero, zero)] * 4, late)
    result = [
        (er - KAPPA * lr, ei - KAPPA * li) for (er, ei), (lr, li) in zip(early, missing)
    ]
    later = {d: project(d, 1, result) for d in FACES}
    for s, (re, im) in enumerate(result):
        y_buf[3 * s:3 * s + 3, 0:8] = pack_first(m, re, im)
        y_buf[3 * s:3 * s + 3, 8:16] = pack_second(m, re, im)

    def finish(d, first, later_there):
        second = outer(link_times(u[d], later_there), plus[d])
        wr, wi = c_add(first, second)
        third = (wi[0, 0] + wi[1, 1] + wi[2, 2]) / 3.0
        for a in range(3):
            for b in range(a, 3):
                if a == b:
                    im = KAPPA * (wi[a, a] - third)
                    re = jnp.zeros_like(im)
                else:
                    re = (0.5 * KAPPA) * (wr[a, b] - wr[b, a])
                    im = (0.5 * KAPPA) * (wi[a, b] + wi[b, a])
                top = pack_first(m, re, im)
                bottom = pack_second(m, re, im)
                f_buf[d, 3 * a + b, 0:8] = top
                f_buf[d, 3 * a + b, 8:16] = bottom
                if a != b:
                    f_buf[d, 3 * b + a, 0:8] = pick(m["low"], -top, top)
                    f_buf[d, 3 * b + a, 8:16] = pick(m["low"], -bottom, bottom)

    d = X_DIR
    finish(d, outer(moved[d], project(d, -1, result)), shift_x(m, project(d, 1, result), 1))
    first = {d: outer(moved[d], project(d, -1, result)) for d in FACES}
    upward[Y_DIR].wait_recv()
    there = shift_face(m, Y_DIR, 1, later[Y_DIR], recv_buf[Y_DIR].at[2], None)
    there = [
        (tr - 2 * KAPPA * only(m["own_y"], br), ti - 2 * KAPPA * only(m["own_y"], bi))
        for (tr, ti), (br, bi) in zip(there, back[Y_DIR])
    ]
    finish(Y_DIR, first[Y_DIR], there)
    edge_half = {
        T_DIR: lambda: face_y(m["edge_t"], [lane_roll(edge_t[...], 64), edge_t[...]]),
        Z_DIR: lambda: face_y(m["edge_z"], both_spins(edge_z)),
    }
    for d in (T_DIR, Z_DIR):
        upward[d].wait_recv()
        there = shift_face(m, d, 1, later[d], recv_buf[d].at[2], ahead_sign[d])
        if d == T_DIR:
            there = [
                (tr - 2 * KAPPA * pick(m["low"], zero, br), ti - 2 * KAPPA * pick(m["low"], zero, bi))
                for (tr, ti), (br, bi) in zip(there, back[T_DIR])
            ]
        pl.when(is_first[Y_DIR])(edges[d].wait_recv)
        scale = KAPPA * last_t if d == T_DIR else KAPPA
        extra = edge_term(d, edge_half[d]())
        there = [
            (tr - scale * er, ti - scale * ei) for (tr, ti), (er, ei) in zip(there, extra)
        ]
        finish(d, first[d], there)
    for d in FACES:
        forward[d].wait_send()
        backward[d].wait_send()
        upward[d].wait_send()

    @pl.when(is_last_y)
    def _():
        edges[T_DIR].wait_send()
        edges[Z_DIR].wait_send()


def store_kernel(y_in, f_in, y_out, f_out, sems):
    copies = [
        pltpu.make_async_copy(f_in, f_out, sems.at[0]),
        pltpu.make_async_copy(y_in, y_out, sems.at[1]),
    ]
    for copy in copies:
        copy.start()
    for copy in copies:
        copy.wait()


def body(quark_field, gauge_links):
    x = quark_field.reshape(12, 16, 128)
    u = gauge_links.reshape(4, 9, 16, 128)
    faces = [pltpu.VMEM((3, FACE_TILES[d], 8, 128), jnp.float32) for d in FACES]
    y, f = pl.pallas_call(
        kernel,
        out_shape=(pltpu.VMEM(x.shape, jnp.float32), pltpu.VMEM(u.shape, jnp.float32)),
        in_specs=[pl.BlockSpec(memory_space=pltpu.HBM)] * 2,
        out_specs=(pl.BlockSpec(memory_space=pltpu.VMEM),) * 2,
        scratch_shapes=[
            pltpu.VMEM(x.shape, jnp.float32),
            pltpu.VMEM(u.shape, jnp.float32),
            *faces,
            *faces,
            pltpu.VMEM((6, 8, 128), jnp.float32),
            pltpu.VMEM((3, 8, 128), jnp.float32),
            pltpu.VMEM((3, 8, 128), jnp.float32),
            pltpu.VMEM((6, 8, 128), jnp.float32),
            pltpu.SemaphoreType.DMA((5,)),
            pltpu.SemaphoreType.DMA((11,)),
            pltpu.SemaphoreType.DMA((11,)),
            pltpu.SemaphoreType.REGULAR((4,)),
        ],
        compiler_params=pltpu.CompilerParams(collective_id=0, has_side_effects=True, vmem_limit_bytes=16 * 1024 * 1024),
        cost_estimate=pl.CostEstimate(flops=6_000_000, bytes_accessed=800_000, transcendentals=0),
    )(pltpu.with_memory_space_constraint(x, pltpu.HBM), pltpu.with_memory_space_constraint(u, pltpu.HBM))
    y, f = pl.pallas_call(
        store_kernel,
        out_shape=(
            jax.ShapeDtypeStruct(x.shape, jnp.float32),
            jax.ShapeDtypeStruct(u.shape, jnp.float32),
        ),
        in_specs=[pl.BlockSpec(memory_space=pltpu.VMEM)] * 2,
        out_specs=(pl.BlockSpec(memory_space=pl.ANY),) * 2,
        scratch_shapes=[pltpu.SemaphoreType.DMA((2,))],
        compiler_params=pltpu.CompilerParams(vmem_limit_bytes=16 * 1024 * 1024),
        cost_estimate=pl.CostEstimate(flops=0, bytes_accessed=800_000, transcendentals=0),
    )(y, f)
    return y.reshape(quark_field.shape), f.reshape(gauge_links.shape)


def solution(mesh):
    specs = (
        P(None, None, "ta", "gz", "gy", None),
        P(None, None, None, "ta", "gz", "gy", None),
    )
    return jax.shard_map(body, mesh=mesh, in_specs=specs, out_specs=specs, check_vma=False)
```

```python
import functools

import jax
import jax.numpy as jnp
from jax import lax
from jax.experimental import pallas as pl
from jax.experimental.pallas import tpu as pltpu
from jax.sharding import PartitionSpec as P

KAPPA = 0.125
MESH = pl.DeviceIdType.MESH
X_DIR, Y_DIR, Z_DIR, T_DIR = 0, 1, 2, 3
AXES = {T_DIR: "ta", Z_DIR: "gz", Y_DIR: "gy"}
FACES = (T_DIR, Z_DIR, Y_DIR)
FACE_TILES = {T_DIR: 6, Z_DIR: 3, Y_DIR: 6}
FACE_START = {T_DIR: 0, Z_DIR: 18, Y_DIR: 27}
ALL_TILES = 45
RECV_SEM = {(T_DIR, 0): 0, (T_DIR, 1): 0, (Z_DIR, 0): 1, (Z_DIR, 1): 1, (Y_DIR, 0): 2, (Y_DIR, 1): 3}


def lane_roll(v, steps):
    return pltpu.roll(v.reshape(-1, 128), steps, 1).reshape(v.shape)


def row_roll(v, steps):
    if steps % 8 == 0:
        return v
    flat = v.reshape(-1, 8, 128)
    return jnp.stack([pltpu.roll(flat[i], steps % 8, 0) for i in range(flat.shape[0])]).reshape(v.shape)


def masks(at_start, at_end):
    lane = lax.broadcasted_iota(jnp.int32, (8, 128), 1)
    row = lax.broadcasted_iota(jnp.int32, (8, 128), 0)
    return {
        "low": lane < 64,
        "last_x": lane % 64 == 63,
        "first_x": lane % 64 == 0,
        "even": row % 2 == 0,
        "z_first": row < 2,
        "z_last": row >= 6,
        "row": row,
        "halo_now": row % 2 + at_start == 0,
        "halo_late": row % 2 + (1 - at_start) == 0,
        "own_y": row % 2 * at_end == 1,
        "edge_t": (row % 2 + (1 - at_start) == 0) & (lane >= 64),
        "edge_z": row + 8 * (1 - at_start) == 6,
    }


def pick(mask, a, b):
    return jnp.where(jnp.broadcast_to(mask, a.shape), a, b)


def unpack(m, first, second):
    return (
        pick(m["low"], first, lane_roll(second, 64)),
        pick(m["low"], lane_roll(first, 64), second),
    )


def pack_first(m, re, im):
    return pick(m["low"], re, lane_roll(im, 64))


def pack_second(m, re, im):
    return pick(m["low"], lane_roll(re, 64), im)


def c_add(a, b):
    return (a[0] + b[0], a[1] + b[1])


def c_sub(a, b):
    return (a[0] - b[0], a[1] - b[1])


def add_i(a, b):
    return (a[0] - b[1], a[1] + b[0])


def sub_i(a, b):
    return (a[0] + b[1], a[1] - b[0])


def project(direction, sign, psi):
    u0, u1, l0, l1 = psi
    plus, minus = (c_add, c_sub) if sign < 0 else (c_sub, c_add)
    plus_i, minus_i = (add_i, sub_i) if sign < 0 else (sub_i, add_i)
    if direction == X_DIR:
        return [plus_i(u0, l1), plus_i(u1, l0)]
    if direction == Y_DIR:
        return [plus(u0, l1), minus(u1, l0)]
    if direction == Z_DIR:
        return [plus_i(u0, l0), minus_i(u1, l1)]
    return [minus(u0, l0), minus(u1, l1)]


def add_spins(direction, sign, total, half):
    h0, h1 = half
    plus, minus = (c_sub, c_add) if sign < 0 else (c_add, c_sub)
    plus_i, minus_i = (sub_i, add_i) if sign < 0 else (add_i, sub_i)
    t0, t1, t2, t3 = total
    upper = [c_add(t0, h0), c_add(t1, h1)]
    if direction == X_DIR:
        return upper + [plus_i(t2, h1), plus_i(t3, h0)]
    if direction == Y_DIR:
        return upper + [plus(t2, h1), minus(t3, h0)]
    if direction == Z_DIR:
        return upper + [plus_i(t2, h0), minus_i(t3, h1)]
    return upper + [plus(t2, h0), plus(t3, h1)]


def link_times(u, half):
    ur, ui = u
    out = []
    for hr, hi in half:
        re = im = None
        for b in range(3):
            cr, ci = ur[:, b], ui[:, b]
            r = cr * hr[b][None] - ci * hi[b][None]
            i = cr * hi[b][None] + ci * hr[b][None]
            re = r if re is None else re + r
            im = i if im is None else im + i
        out.append((re, im))
    return out


def adjoint_times(u, half):
    ur, ui = u
    out = []
    for hr, hi in half:
        re = im = None
        for b in range(3):
            cr, ci = ur[b], ui[b]
            r = cr * hr[b][None] + ci * hi[b][None]
            i = cr * hi[b][None] - ci * hr[b][None]
            re = r if re is None else re + r
            im = i if im is None else im + i
        out.append((re, im))
    return out


def outer(left, right):
    re = im = None
    for (lr, li), (rr, ri) in zip(left, right):
        r = lr[:, None] * rr[None] + li[:, None] * ri[None]
        i = li[:, None] * rr[None] - lr[:, None] * ri[None]
        re = r if re is None else re + r
        im = i if im is None else im + i
    return re, im


def shift_x(m, half, steps):
    def one(v):
        if steps > 0:
            return pick(m["last_x"], lane_roll(v, 63), lane_roll(v, 127))
        return pick(m["first_x"], lane_roll(v, 65), lane_roll(v, 1))

    return [(one(re), one(im)) for re, im in half]


def stage_face(m, direction, end, half, ref):
    if direction == T_DIR:
        for s, (re, im) in enumerate(half):
            ref[3 * s:3 * s + 3] = (pack_second if end else pack_first)(m, re, im)
    elif direction == Y_DIR:
        for s, (re, im) in enumerate(half):
            if end:
                tile = pick(m["even"], row_roll(re, -1), im)
            else:
                tile = pick(m["even"], re, row_roll(im, 1))
            ref[3 * s:3 * s + 3] = tile
    else:
        tiles = [part[c] for re, im in half for part in (re, im) for c in range(3)]
        for j in range(3):
            tile = row_roll(tiles[4 * j], 2 if end else 0)
            for k in range(1, 4):
                moved = row_roll(tiles[4 * j + k], 2 * k + (2 if end else 0))
                tile = pick(m["row"] < 2 * k, tile, moved)
            ref[j] = tile


def shift_face(m, direction, steps, half, ref, sign):
    out = []
    if direction == T_DIR:
        for s, (re, im) in enumerate(half):
            face = ref[3 * s:3 * s + 3] * sign
            if steps > 0:
                out.append((
                    lane_roll(pick(m["low"], face, re), 64),
                    pick(m["low"], lane_roll(im, 64), face),
                ))
            else:
                out.append((
                    pick(m["low"], face, lane_roll(re, 64)),
                    lane_roll(pick(m["low"], im, face), 64),
                ))
    elif direction == Y_DIR:
        for s, (re, im) in enumerate(half):
            face = ref[3 * s:3 * s + 3]
            if steps > 0:
                out.append((
                    pick(m["even"], row_roll(re, -1), row_roll(face, 1)),
                    pick(m["even"], row_roll(im, -1), face),
                ))
            else:
                out.append((
                    pick(m["even"], face, row_roll(re, 1)),
                    pick(m["even"], row_roll(face, -1), row_roll(im, 1)),
                ))
    else:
        n = 0
        for re, im in half:
            parts = []
            for part in (re, im):
                moved = []
                for c in range(3):
                    face = ref[n // 4]
                    k = n % 4
                    n += 1
                    if steps > 0:
                        moved.append(row_roll(pick(m["z_first"], row_roll(face, -2 * k), part[c]), -2))
                    else:
                        moved.append(row_roll(pick(m["z_last"], row_roll(face, 6 - 2 * k), part[c]), 2))
                parts.append(jnp.stack(moved))
            out.append(tuple(parts))
    return out


def only(mask, v):
    return pick(mask, v, jnp.zeros_like(v))


def local_y(m, half):
    return [tuple(pick(m["even"], jnp.zeros_like(v), row_roll(v, 1)) for v in parts) for parts in half]


def face_y(mask, faces):
    return [(only(mask, face), only(mask, row_roll(face, -1))) for face in faces]


def both_spins(ref):
    return [ref[0:3], ref[3:6]]


def edge_term(direction, half):
    h0, h1 = half
    return project(direction, 1, [h0, h1, h1, (-h0[0], -h0[1])])


def kernel(
    x_hbm, u_hbm, y_buf, f_buf,
    x_buf, u_buf,
    outbox, inbox, y_now, edge_out, edge_t, edge_z,
    load_sem, send_sem, recv_sem, here_sem,
):
    def face_of(box, d, slot, faces=1):
        return box.at[pl.ds(FACE_START[d] + slot * FACE_TILES[d], faces * FACE_TILES[d])]

    x_load = pltpu.make_async_copy(x_hbm, x_buf, load_sem.at[0])
    y_load = pltpu.make_async_copy(u_hbm.at[Y_DIR], u_buf.at[Y_DIR], load_sem.at[1])
    rest_load = pltpu.make_async_copy(u_hbm.at[pl.ds(0, 3)], u_buf.at[pl.ds(0, 3)], load_sem.at[2])
    for s in range(4):
        part = pl.ds(3 * s, 3)
        pltpu.make_async_copy(x_hbm.at[part], x_buf.at[part], load_sem.at[0]).start()
    for a in range(3):
        part = (Y_DIR, pl.ds(3 * a, 3))
        pltpu.make_async_copy(u_hbm.at[part], u_buf.at[part], load_sem.at[1]).start()
    me = {d: lax.axis_index(AXES[d]) for d in FACES}
    size = {d: lax.axis_size(AXES[d]) for d in FACES}
    ahead = {d: lax.rem(me[d] + 1, size[d]) for d in FACES}
    behind = {d: lax.rem(me[d] + size[d] - 1, size[d]) for d in FACES}

    barrier = pltpu.get_barrier_semaphore()
    is_first = {d: me[d] == 0 for d in FACES}
    is_last = {d: me[d] == size[d] - 1 for d in FACES}
    is_last_y = is_last[Y_DIR]

    def greet(where):
        pl.semaphore_signal(barrier, inc=1, device_id=where, device_id_type=MESH)

    for d in (T_DIR, Z_DIR):
        greet({AXES[d]: behind[d]})
    for d in FACES:
        pl.when(jnp.logical_not(is_last[d]))(functools.partial(greet, {AXES[d]: ahead[d]}))

    @pl.when(is_first[Y_DIR])
    def _():
        greet({AXES[Y_DIR]: behind[Y_DIR]})
        for d in (T_DIR, Z_DIR):
            greet({AXES[d]: ahead[d], AXES[Y_DIR]: behind[Y_DIR]})

    arrivals = 5 - sum(is_first[d].astype(jnp.int32) for d in FACES) + 3 * is_last_y.astype(jnp.int32)
    for d in (T_DIR, Z_DIR, X_DIR):
        pltpu.make_async_copy(u_hbm.at[d], u_buf.at[d], load_sem.at[2]).start()

    def link(d, slot, there, faces=1):
        return pltpu.make_async_remote_copy(
            src_ref=face_of(outbox, d, slot, faces),
            dst_ref=face_of(inbox, d, slot, faces),
            send_sem=send_sem.at[0],
            recv_sem=recv_sem.at[RECV_SEM.get((d, slot), 3 + d)],
            device_id={AXES[d]: there},
            device_id_type=MESH,
        )

    forward = {d: link(d, 0, behind[d]) for d in FACES}
    backward = {d: link(d, 1, ahead[d]) for d in FACES}
    upward = {d: link(d, 2, behind[d]) for d in FACES}
    both = {d: link(d, 0, behind[d], 2) for d in (T_DIR, Z_DIR)}
    all_sent = pltpu.make_async_copy(outbox, inbox, send_sem.at[0])

    def edge_link(d, src, dst):
        return pltpu.make_async_remote_copy(
            src_ref=src,
            dst_ref=dst,
            send_sem=send_sem.at[d - 1],
            recv_sem=recv_sem.at[5 + d],
            device_id={AXES[d]: behind[d], AXES[Y_DIR]: ahead[Y_DIR]},
            device_id_type=MESH,
        )

    edges = {
        T_DIR: edge_link(T_DIR, edge_out, edge_t),
        Z_DIR: edge_link(Z_DIR, face_of(outbox, Y_DIR, 1).at[:, 0:2], edge_z.at[:, 6:8]),
    }

    here = {d: here_sem.at[d - 1] for d in FACES}
    here_ahead = here_sem.at[3]

    def say_here():
        def say(sem, there):
            pl.semaphore_signal(sem, inc=1, device_id=there, device_id_type=MESH)

        for d in FACES:
            pl.when(is_last[d])(functools.partial(say, here[d], {AXES[d]: ahead[d]}))
        there = {AXES[Y_DIR]: behind[Y_DIR]}
        pl.when(jnp.logical_not(is_first[Y_DIR]))(functools.partial(say, here_ahead, there))

    def greeted(d):
        pl.semaphore_wait(here[d], 1)
        forward[d].start()

    m = masks(is_first[Y_DIR].astype(jnp.int32), is_last_y.astype(jnp.int32))
    last_t = jnp.where(me[T_DIR] == size[T_DIR] - 1, -1.0, 1.0).astype(jnp.float32)
    first_t = jnp.where(me[T_DIR] == 0, -1.0, 1.0).astype(jnp.float32)
    ahead_sign = {T_DIR: last_t, Z_DIR: None, Y_DIR: None}
    behind_sign = {T_DIR: first_t, Z_DIR: None, Y_DIR: None}

    x_load.wait()
    psi = [unpack(m, x_buf[3 * s:3 * s + 3, 0:8], x_buf[3 * s:3 * s + 3, 8:16]) for s in range(4)]
    minus = {}
    plus = {}
    u = {}
    back = {}

    def links(d):
        first, second = unpack(m, u_buf[d, :, 0:8], u_buf[d, :, 8:16])
        return first.reshape(3, 3, 8, 128), second.reshape(3, 3, 8, 128)

    def prepare_backward(d):
        u[d] = links(d)
        plus[d] = project(d, 1, psi)
        back[d] = adjoint_times(u[d], plus[d])
        stage_face(m, d, 1, back[d], face_of(outbox, d, 1))

    y_load.wait()
    prepare_backward(Y_DIR)

    @pl.when(is_last_y)
    def _():
        spins = both_spins(face_of(outbox, Y_DIR, 1))
        edge_out[...] = pick(m["low"], spins[0], lane_roll(spins[1], 64))
        pl.semaphore_wait(barrier, arrivals)
        edges[Z_DIR].start()
        edges[T_DIR].start()
        backward[Y_DIR].start()
        say_here()

    for d in FACES:
        minus[d] = project(d, -1, psi)
        stage_face(m, d, 0, minus[d], face_of(outbox, d, 0))
    rest_load.wait()
    for d in (T_DIR, Z_DIR):
        prepare_backward(d)

    @pl.when(jnp.logical_not(is_last_y))
    def _():
        pl.semaphore_wait(barrier, arrivals)
        say_here()

    for d in (T_DIR, Z_DIR):
        backward[d].start()
    for d in FACES:
        pl.when(jnp.logical_not(is_first[d]))(forward[d].start)
    for d in (T_DIR, Z_DIR):
        pl.when(is_first[d])(functools.partial(greeted, d))

    @pl.when(jnp.logical_not(is_last_y))
    def _():
        pl.semaphore_wait(here_ahead, 1)
        backward[Y_DIR].start()

    zero = jnp.zeros((3, 8, 128), jnp.float32)
    hop = [(zero, zero)] * 4
    d = X_DIR
    u[d] = links(d)
    plus[d] = project(d, 1, psi)
    minus[d] = project(d, -1, psi)
    moved = {}
    moved[d] = link_times(u[d], shift_x(m, minus[d], 1))
    hop = add_spins(d, -1, hop, moved[d])
    hop = add_spins(d, 1, hop, shift_x(m, adjoint_times(u[d], plus[d]), -1))

    def take_backward(d, hop):
        there = shift_face(m, d, -1, back[d], face_of(inbox, d, 1), behind_sign[d])
        return add_spins(d, 1, hop, there)

    def take_forward(d, hop):
        there = shift_face(m, d, 1, minus[d], face_of(inbox, d, 0), ahead_sign[d])
        moved[d] = link_times(u[d], there)
        return add_spins(d, -1, hop, moved[d])

    def wilson(hop):
        return [(pr - KAPPA * hr, pi - KAPPA * hi) for (pr, pi), (hr, hi) in zip(psi, hop)]

    both[Z_DIR].wait_recv()
    hop = take_backward(Z_DIR, hop)
    hop = take_forward(Z_DIR, hop)
    forward[Y_DIR].wait_recv()
    hop = take_forward(Y_DIR, hop)
    hop = add_spins(Y_DIR, 1, hop, local_y(m, back[Y_DIR]))

    @pl.when(jnp.logical_not(is_first[Y_DIR]))
    def _():
        backward[Y_DIR].wait_recv()
        y_now[...] = face_of(inbox, Y_DIR, 1)[...]

    hop = add_spins(Y_DIR, 1, hop, face_y(m["halo_now"], both_spins(y_now)))

    inner = [tuple(lane_roll(v, 64) for v in parts) for parts in minus[T_DIR]]
    inner = add_spins(T_DIR, -1, hop, link_times(u[T_DIR], inner))
    stage_face(m, T_DIR, 0, project(T_DIR, 1, wilson(inner)), face_of(outbox, T_DIR, 2))
    upward[T_DIR].start()
    both[T_DIR].wait_recv()
    hop = take_backward(T_DIR, hop)
    hop = take_forward(T_DIR, hop)
    early = wilson(hop)
    for d in (Z_DIR, Y_DIR):
        stage_face(m, d, 0, project(d, 1, early), face_of(outbox, d, 2))
    upward[Z_DIR].start()
    pl.when(jnp.logical_not(is_first[Y_DIR]))(upward[Y_DIR].start)

    @pl.when(is_first[Y_DIR])
    def _():
        greeted(Y_DIR)
        upward[Y_DIR].start()
        backward[Y_DIR].wait_recv()

    late = face_y(m["halo_late"], both_spins(face_of(inbox, Y_DIR, 1)))
    missing = add_spins(Y_DIR, 1, [(zero, zero)] * 4, late)
    result = [
        (er - KAPPA * lr, ei - KAPPA * li) for (er, ei), (lr, li) in zip(early, missing)
    ]
    later = {d: project(d, 1, result) for d in FACES}
    for s, (re, im) in enumerate(result):
        y_buf[3 * s:3 * s + 3, 0:8] = pack_first(m, re, im)
        y_buf[3 * s:3 * s + 3, 8:16] = pack_second(m, re, im)

    def finish(d, first, later_there):
        second = outer(link_times(u[d], later_there), plus[d])
        wr, wi = c_add(first, second)
        third = (wi[0, 0] + wi[1, 1] + wi[2, 2]) / 3.0
        for a in range(3):
            for b in range(a, 3):
                if a == b:
                    im = KAPPA * (wi[a, a] - third)
                    re = jnp.zeros_like(im)
                else:
                    re = (0.5 * KAPPA) * (wr[a, b] - wr[b, a])
                    im = (0.5 * KAPPA) * (wi[a, b] + wi[b, a])
                top = pack_first(m, re, im)
                bottom = pack_second(m, re, im)
                f_buf[d, 3 * a + b, 0:8] = top
                f_buf[d, 3 * a + b, 8:16] = bottom
                if a != b:
                    f_buf[d, 3 * b + a, 0:8] = pick(m["low"], -top, top)
                    f_buf[d, 3 * b + a, 8:16] = pick(m["low"], -bottom, bottom)

    d = X_DIR
    finish(d, outer(moved[d], project(d, -1, result)), shift_x(m, project(d, 1, result), 1))
    first = {d: outer(moved[d], project(d, -1, result)) for d in FACES}
    upward[Y_DIR].wait_recv()
    there = shift_face(m, Y_DIR, 1, later[Y_DIR], face_of(inbox, Y_DIR, 2), None)
    there = [
        (tr - 2 * KAPPA * only(m["own_y"], br), ti - 2 * KAPPA * only(m["own_y"], bi))
        for (tr, ti), (br, bi) in zip(there, back[Y_DIR])
    ]
    finish(Y_DIR, first[Y_DIR], there)
    edge_half = {
        T_DIR: lambda: face_y(m["edge_t"], [lane_roll(edge_t[...], 64), edge_t[...]]),
        Z_DIR: lambda: face_y(m["edge_z"], both_spins(edge_z)),
    }
    for d in (T_DIR, Z_DIR):
        upward[d].wait_recv()
        there = shift_face(m, d, 1, later[d], face_of(inbox, d, 2), ahead_sign[d])
        if d == T_DIR:
            there = [
                (tr - 2 * KAPPA * pick(m["low"], zero, br), ti - 2 * KAPPA * pick(m["low"], zero, bi))
                for (tr, ti), (br, bi) in zip(there, back[T_DIR])
            ]
        pl.when(is_first[Y_DIR])(edges[d].wait_recv)
        scale = KAPPA * last_t if d == T_DIR else KAPPA
        extra = edge_term(d, edge_half[d]())
        there = [
            (tr - scale * er, ti - scale * ei) for (tr, ti), (er, ei) in zip(there, extra)
        ]
        finish(d, first[d], there)
    all_sent.wait()

    @pl.when(is_last_y)
    def _():
        edges[T_DIR].wait_send()
        edges[Z_DIR].wait_send()


def store_kernel(y_in, f_in, y_out, f_out, sems):
    copies = [
        pltpu.make_async_copy(f_in, f_out, sems.at[0]),
        pltpu.make_async_copy(y_in, y_out, sems.at[1]),
    ]
    for copy in copies:
        copy.start()
    for copy in copies:
        copy.wait()


def body(quark_field, gauge_links):
    x = quark_field.reshape(12, 16, 128)
    u = gauge_links.reshape(4, 9, 16, 128)
    y, f = pl.pallas_call(
        kernel,
        out_shape=(pltpu.VMEM(x.shape, jnp.float32), pltpu.VMEM(u.shape, jnp.float32)),
        in_specs=[pl.BlockSpec(memory_space=pltpu.HBM)] * 2,
        out_specs=(pl.BlockSpec(memory_space=pltpu.VMEM),) * 2,
        scratch_shapes=[
            pltpu.VMEM(x.shape, jnp.float32),
            pltpu.VMEM(u.shape, jnp.float32),
            pltpu.VMEM((ALL_TILES, 8, 128), jnp.float32),
            pltpu.VMEM((ALL_TILES, 8, 128), jnp.float32),
            pltpu.VMEM((6, 8, 128), jnp.float32),
            pltpu.VMEM((3, 8, 128), jnp.float32),
            pltpu.VMEM((3, 8, 128), jnp.float32),
            pltpu.VMEM((6, 8, 128), jnp.float32),
            pltpu.SemaphoreType.DMA((3,)),
            pltpu.SemaphoreType.DMA((3,)),
            pltpu.SemaphoreType.DMA((9,)),
            pltpu.SemaphoreType.REGULAR((4,)),
        ],
        compiler_params=pltpu.CompilerParams(collective_id=0, has_side_effects=True, vmem_limit_bytes=16 * 1024 * 1024),
        cost_estimate=pl.CostEstimate(flops=6_000_000, bytes_accessed=800_000, transcendentals=0),
    )(pltpu.with_memory_space_constraint(x, pltpu.HBM), pltpu.with_memory_space_constraint(u, pltpu.HBM))
    y, f = pl.pallas_call(
        store_kernel,
        out_shape=(
            jax.ShapeDtypeStruct(x.shape, jnp.float32),
            jax.ShapeDtypeStruct(u.shape, jnp.float32),
        ),
        in_specs=[pl.BlockSpec(memory_space=pltpu.VMEM)] * 2,
        out_specs=(pl.BlockSpec(memory_space=pl.ANY),) * 2,
        scratch_shapes=[pltpu.SemaphoreType.DMA((2,))],
        compiler_params=pltpu.CompilerParams(vmem_limit_bytes=16 * 1024 * 1024),
        cost_estimate=pl.CostEstimate(flops=0, bytes_accessed=800_000, transcendentals=0),
    )(y, f)
    return y.reshape(quark_field.shape), f.reshape(gauge_links.shape)


def solution(mesh):
    specs = (
        P(None, None, "ta", "gz", "gy", None),
        P(None, None, None, "ta", "gz", "gy", None),
    )
    return jax.shard_map(body, mesh=mesh, in_specs=specs, out_specs=specs, check_vma=False)
```

```python
import functools

import jax
import jax.numpy as jnp
from jax import lax
from jax.experimental import pallas as pl
from jax.experimental.pallas import tpu as pltpu
from jax.sharding import PartitionSpec as P

KAPPA = 0.125
MESH = pl.DeviceIdType.MESH
X_DIR, Y_DIR, Z_DIR, T_DIR = 0, 1, 2, 3
AXES = {T_DIR: "ta", Z_DIR: "gz", Y_DIR: "gy"}
FACES = (T_DIR, Z_DIR, Y_DIR)
FACE_TILES = {T_DIR: 6, Z_DIR: 3, Y_DIR: 6}
FACE_START = {T_DIR: 0, Z_DIR: 18, Y_DIR: 27}
ALL_TILES = 45
RECV_SEM = {(T_DIR, 0): 0, (T_DIR, 1): 0, (Z_DIR, 0): 1, (Z_DIR, 1): 1, (Y_DIR, 0): 2, (Y_DIR, 1): 3}
RECV_UP, RECV_EDGE = 4, 5


def lane_roll(v, steps):
    return pltpu.roll(v.reshape(-1, 128), steps, 1).reshape(v.shape)


def row_roll(v, steps):
    if steps % 8 == 0:
        return v
    flat = v.reshape(-1, 8, 128)
    return jnp.stack([pltpu.roll(flat[i], steps % 8, 0) for i in range(flat.shape[0])]).reshape(v.shape)


def masks(at_start, at_end):
    lane = lax.broadcasted_iota(jnp.int32, (8, 128), 1)
    row = lax.broadcasted_iota(jnp.int32, (8, 128), 0)
    return {
        "low": lane < 64,
        "last_x": lane % 64 == 63,
        "first_x": lane % 64 == 0,
        "even": row % 2 == 0,
        "z_first": row < 2,
        "z_last": row >= 6,
        "row": row,
        "halo_now": row % 2 + at_start == 0,
        "halo_late": row % 2 + (1 - at_start) == 0,
        "own_y": row % 2 * at_end == 1,
        "edge_t": (row % 2 + (1 - at_start) == 0) & (lane >= 64),
        "edge_z": row + 8 * (1 - at_start) == 6,
    }


def pick(mask, a, b):
    return jnp.where(jnp.broadcast_to(mask, a.shape), a, b)


def unpack(m, first, second):
    return (
        pick(m["low"], first, lane_roll(second, 64)),
        pick(m["low"], lane_roll(first, 64), second),
    )


def pack_first(m, re, im):
    return pick(m["low"], re, lane_roll(im, 64))


def pack_second(m, re, im):
    return pick(m["low"], lane_roll(re, 64), im)


def c_add(a, b):
    return (a[0] + b[0], a[1] + b[1])


def c_sub(a, b):
    return (a[0] - b[0], a[1] - b[1])


def add_i(a, b):
    return (a[0] - b[1], a[1] + b[0])


def sub_i(a, b):
    return (a[0] + b[1], a[1] - b[0])


def project(direction, sign, psi):
    u0, u1, l0, l1 = psi
    plus, minus = (c_add, c_sub) if sign < 0 else (c_sub, c_add)
    plus_i, minus_i = (add_i, sub_i) if sign < 0 else (sub_i, add_i)
    if direction == X_DIR:
        return [plus_i(u0, l1), plus_i(u1, l0)]
    if direction == Y_DIR:
        return [plus(u0, l1), minus(u1, l0)]
    if direction == Z_DIR:
        return [plus_i(u0, l0), minus_i(u1, l1)]
    return [minus(u0, l0), minus(u1, l1)]


def add_spins(direction, sign, total, half):
    h0, h1 = half
    plus, minus = (c_sub, c_add) if sign < 0 else (c_add, c_sub)
    plus_i, minus_i = (sub_i, add_i) if sign < 0 else (add_i, sub_i)
    t0, t1, t2, t3 = total
    upper = [c_add(t0, h0), c_add(t1, h1)]
    if direction == X_DIR:
        return upper + [plus_i(t2, h1), plus_i(t3, h0)]
    if direction == Y_DIR:
        return upper + [plus(t2, h1), minus(t3, h0)]
    if direction == Z_DIR:
        return upper + [plus_i(t2, h0), minus_i(t3, h1)]
    return upper + [plus(t2, h0), plus(t3, h1)]


def link_times(u, half):
    ur, ui = u
    out = []
    for hr, hi in half:
        re = im = None
        for b in range(3):
            cr, ci = ur[:, b], ui[:, b]
            r = cr * hr[b][None] - ci * hi[b][None]
            i = cr * hi[b][None] + ci * hr[b][None]
            re = r if re is None else re + r
            im = i if im is None else im + i
        out.append((re, im))
    return out


def adjoint_times(u, half):
    ur, ui = u
    out = []
    for hr, hi in half:
        re = im = None
        for b in range(3):
            cr, ci = ur[b], ui[b]
            r = cr * hr[b][None] + ci * hi[b][None]
            i = cr * hi[b][None] - ci * hr[b][None]
            re = r if re is None else re + r
            im = i if im is None else im + i
        out.append((re, im))
    return out


def outer(left, right):
    re = im = None
    for (lr, li), (rr, ri) in zip(left, right):
        r = lr[:, None] * rr[None] + li[:, None] * ri[None]
        i = li[:, None] * rr[None] - lr[:, None] * ri[None]
        re = r if re is None else re + r
        im = i if im is None else im + i
    return re, im


def shift_x(m, half, steps):
    def one(v):
        if steps > 0:
            return pick(m["last_x"], lane_roll(v, 63), lane_roll(v, 127))
        return pick(m["first_x"], lane_roll(v, 65), lane_roll(v, 1))

    return [(one(re), one(im)) for re, im in half]


def stage_face(m, direction, end, half, ref):
    if direction == T_DIR:
        for s, (re, im) in enumerate(half):
            ref[3 * s:3 * s + 3] = (pack_second if end else pack_first)(m, re, im)
    elif direction == Y_DIR:
        for s, (re, im) in enumerate(half):
            if end:
                tile = pick(m["even"], row_roll(re, -1), im)
            else:
                tile = pick(m["even"], re, row_roll(im, 1))
            ref[3 * s:3 * s + 3] = tile
    else:
        tiles = [part[c] for re, im in half for part in (re, im) for c in range(3)]
        for j in range(3):
            tile = row_roll(tiles[4 * j], 2 if end else 0)
            for k in range(1, 4):
                moved = row_roll(tiles[4 * j + k], 2 * k + (2 if end else 0))
                tile = pick(m["row"] < 2 * k, tile, moved)
            ref[j] = tile


def shift_face(m, direction, steps, half, ref, sign):
    out = []
    if direction == T_DIR:
        for s, (re, im) in enumerate(half):
            face = ref[3 * s:3 * s + 3] * sign
            if steps > 0:
                out.append((
                    lane_roll(pick(m["low"], face, re), 64),
                    pick(m["low"], lane_roll(im, 64), face),
                ))
            else:
                out.append((
                    pick(m["low"], face, lane_roll(re, 64)),
                    lane_roll(pick(m["low"], im, face), 64),
                ))
    elif direction == Y_DIR:
        for s, (re, im) in enumerate(half):
            face = ref[3 * s:3 * s + 3]
            if steps > 0:
                out.append((
                    pick(m["even"], row_roll(re, -1), row_roll(face, 1)),
                    pick(m["even"], row_roll(im, -1), face),
                ))
            else:
                out.append((
                    pick(m["even"], face, row_roll(re, 1)),
                    pick(m["even"], row_roll(face, -1), row_roll(im, 1)),
                ))
    else:
        n = 0
        for re, im in half:
            parts = []
            for part in (re, im):
                moved = []
                for c in range(3):
                    face = ref[n // 4]
                    k = n % 4
                    n += 1
                    if steps > 0:
                        moved.append(row_roll(pick(m["z_first"], row_roll(face, -2 * k), part[c]), -2))
                    else:
                        moved.append(row_roll(pick(m["z_last"], row_roll(face, 6 - 2 * k), part[c]), 2))
                parts.append(jnp.stack(moved))
            out.append(tuple(parts))
    return out


def only(mask, v):
    return pick(mask, v, jnp.zeros_like(v))


def local_y(m, half):
    return [tuple(pick(m["even"], jnp.zeros_like(v), row_roll(v, 1)) for v in parts) for parts in half]


def face_y(mask, faces):
    return [(only(mask, face), only(mask, row_roll(face, -1))) for face in faces]


def both_spins(ref):
    return [ref[0:3], ref[3:6]]


def edge_term(direction, half):
    h0, h1 = half
    return project(direction, 1, [h0, h1, h1, (-h0[0], -h0[1])])


def kernel(
    x_hbm, u_hbm, y_buf, f_buf,
    x_buf, u_buf,
    outbox, inbox, y_now, edge_out, edge_t, edge_z,
    load_sem, send_sem, recv_sem, here_sem,
):
    def face_of(box, d, slot, faces=1):
        return box.at[pl.ds(FACE_START[d] + slot * FACE_TILES[d], faces * FACE_TILES[d])]

    first_load = pltpu.make_async_copy(u_hbm.at[pl.ds(0, 21)], u_buf.at[pl.ds(0, 21)], load_sem.at[0])
    rest_load = pltpu.make_async_copy(u_hbm.at[pl.ds(0, 27)], u_buf.at[pl.ds(0, 27)], load_sem.at[1])

    def load(source, target, start, count, sem):
        part = pl.ds(start, count)
        pltpu.make_async_copy(source.at[part], target.at[part], load_sem.at[sem]).start()

    for s in range(4):
        load(x_hbm, x_buf, 3 * s, 3, 0)
    for a in range(3):
        load(u_hbm, u_buf, 9 * Y_DIR + 3 * a, 3, 0)
    me = {d: lax.axis_index(AXES[d]) for d in FACES}
    size = {d: lax.axis_size(AXES[d]) for d in FACES}
    ahead = {d: lax.rem(me[d] + 1, size[d]) for d in FACES}
    behind = {d: lax.rem(me[d] + size[d] - 1, size[d]) for d in FACES}

    barrier = pltpu.get_barrier_semaphore()
    is_first = {d: me[d] == 0 for d in FACES}
    is_last = {d: me[d] == size[d] - 1 for d in FACES}
    is_last_y = is_last[Y_DIR]

    def greet(where):
        pl.semaphore_signal(barrier, inc=1, device_id=where, device_id_type=MESH)

    odd = lax.rem(me[T_DIR], 2) == 1
    plain = jnp.logical_not(is_last_y)
    pl.when(plain | odd | is_first[T_DIR])(functools.partial(greet, {AXES[T_DIR]: behind[T_DIR]}))
    pl.when(plain | is_first[Z_DIR])(functools.partial(greet, {AXES[Z_DIR]: behind[Z_DIR]}))
    pl.when((plain | odd) & jnp.logical_not(is_last[T_DIR]))(functools.partial(greet, {AXES[T_DIR]: ahead[T_DIR]}))
    for d in (Z_DIR, Y_DIR):
        pl.when(jnp.logical_not(is_last[d]))(functools.partial(greet, {AXES[d]: ahead[d]}))

    @pl.when(is_first[Y_DIR])
    def _():
        greet({AXES[Y_DIR]: behind[Y_DIR]})
        for d in (T_DIR, Z_DIR):
            greet({AXES[d]: ahead[d], AXES[Y_DIR]: behind[Y_DIR]})

    def one(flag):
        return flag.astype(jnp.int32)

    plain_arrivals = 5 - sum(one(is_first[d]) for d in FACES)
    late_t = jnp.where(odd, one(is_last[T_DIR]), 2 - one(is_first[T_DIR]))
    late_arrivals = late_t + 1 + one(is_last[Z_DIR]) - one(is_first[Z_DIR]) + 4
    late_replies = one(jnp.logical_not(is_last[Z_DIR])) + jnp.where(odd, 2 - one(is_last[T_DIR]), 0)
    arrivals = jnp.where(is_last_y, late_arrivals, plain_arrivals)
    replies = jnp.where(is_last_y, late_replies, 1)
    for d in (T_DIR, Z_DIR, X_DIR):
        load(u_hbm, u_buf, 9 * d, 9, 1)

    def link(d, slot, there, faces=1):
        return pltpu.make_async_remote_copy(
            src_ref=face_of(outbox, d, slot, faces),
            dst_ref=face_of(inbox, d, slot, faces),
            send_sem=send_sem.at[0],
            recv_sem=recv_sem.at[RECV_SEM.get((d, slot), RECV_UP)],
            device_id={AXES[d]: there},
            device_id_type=MESH,
        )

    forward = {d: link(d, 0, behind[d]) for d in FACES}
    backward = {d: link(d, 1, ahead[d]) for d in FACES}
    upward = {d: link(d, 2, behind[d]) for d in FACES}
    both = {d: link(d, 0, behind[d], 2) for d in (T_DIR, Z_DIR)}
    all_up = pltpu.make_async_copy(outbox.at[pl.ds(0, 15)], inbox.at[pl.ds(0, 15)], recv_sem.at[RECV_UP])
    all_sent = pltpu.make_async_copy(outbox, inbox, send_sem.at[0])

    def edge_link(d, src, dst):
        return pltpu.make_async_remote_copy(
            src_ref=src,
            dst_ref=dst,
            send_sem=send_sem.at[1],
            recv_sem=recv_sem.at[RECV_EDGE],
            device_id={AXES[d]: behind[d], AXES[Y_DIR]: ahead[Y_DIR]},
            device_id_type=MESH,
        )

    edges = {
        T_DIR: edge_link(T_DIR, edge_out, edge_t),
        Z_DIR: edge_link(Z_DIR, face_of(outbox, Y_DIR, 1).at[:, 0:2], edge_z.at[:, 6:8]),
    }
    both_edges = edge_link(T_DIR, y_now.at[:, 0:6], y_now.at[:, 0:6])

    here = {T_DIR: here_sem.at[0], Z_DIR: here_sem.at[0], Y_DIR: here_sem.at[1]}
    here_near = here_sem.at[2]

    def say_here():
        def say(sem, there):
            pl.semaphore_signal(sem, inc=1, device_id=there, device_id_type=MESH)

        for d in FACES:
            pl.when(is_last[d])(functools.partial(say, here[d], {AXES[d]: ahead[d]}))
        there = {AXES[Y_DIR]: behind[Y_DIR]}
        pl.when(jnp.logical_not(is_first[Y_DIR]))(functools.partial(say, here_near, there))

        @pl.when(is_last_y)
        def _():
            pl.when(jnp.logical_not(is_first[Z_DIR]))(functools.partial(say, here_near, {AXES[Z_DIR]: behind[Z_DIR]}))
            even = jnp.logical_not(odd)
            pl.when(even)(functools.partial(say, here_near, {AXES[T_DIR]: ahead[T_DIR]}))
            pl.when(even & jnp.logical_not(is_first[T_DIR]))(
                functools.partial(say, here_near, {AXES[T_DIR]: behind[T_DIR]})
            )

    m = masks(is_first[Y_DIR].astype(jnp.int32), is_last_y.astype(jnp.int32))
    last_t = jnp.where(me[T_DIR] == size[T_DIR] - 1, -1.0, 1.0).astype(jnp.float32)
    first_t = jnp.where(me[T_DIR] == 0, -1.0, 1.0).astype(jnp.float32)
    ahead_sign = {T_DIR: last_t, Z_DIR: None, Y_DIR: None}
    behind_sign = {T_DIR: first_t, Z_DIR: None, Y_DIR: None}

    first_load.wait()
    psi = [unpack(m, x_buf[3 * s:3 * s + 3, 0:8], x_buf[3 * s:3 * s + 3, 8:16]) for s in range(4)]
    minus = {}
    plus = {}
    u = {}
    back = {}

    def links(d):
        first, second = unpack(m, u_buf[9 * d:9 * d + 9, 0:8], u_buf[9 * d:9 * d + 9, 8:16])
        return first.reshape(3, 3, 8, 128), second.reshape(3, 3, 8, 128)

    def prepare_backward(d):
        u[d] = links(d)
        plus[d] = project(d, 1, psi)
        back[d] = adjoint_times(u[d], plus[d])
        stage_face(m, d, 1, back[d], face_of(outbox, d, 1))

    prepare_backward(Y_DIR)

    @pl.when(is_last_y)
    def _():
        pl.semaphore_wait(barrier, arrivals)
        edges[Z_DIR].start()
        spins = both_spins(face_of(outbox, Y_DIR, 1))
        edge_out[...] = pick(m["low"], spins[0], lane_roll(spins[1], 64))
        edges[T_DIR].start()
        backward[Y_DIR].start()
        say_here()

    for d in FACES:
        minus[d] = project(d, -1, psi)
        stage_face(m, d, 0, minus[d], face_of(outbox, d, 0))
    rest_load.wait()
    for d in (T_DIR, Z_DIR):
        prepare_backward(d)

    @pl.when(jnp.logical_not(is_last_y))
    def _():
        pl.semaphore_wait(barrier, arrivals)
        say_here()

    pl.when(is_last_y & (replies > 0))(lambda: pl.semaphore_wait(here_near, replies))
    for d in (T_DIR, Z_DIR):
        backward[d].start()
    for d in FACES:
        pl.when(jnp.logical_not(is_first[d]))(forward[d].start)

    @pl.when(is_first[T_DIR] | is_first[Z_DIR])
    def _():
        pl.semaphore_wait(here[T_DIR], is_first[T_DIR].astype(jnp.int32) + is_first[Z_DIR].astype(jnp.int32))
        for d in (T_DIR, Z_DIR):
            pl.when(is_first[d])(forward[d].start)

    @pl.when(jnp.logical_not(is_last_y))
    def _():
        pl.semaphore_wait(here_near, replies)
        backward[Y_DIR].start()

    zero = jnp.zeros((3, 8, 128), jnp.float32)
    hop = [(zero, zero)] * 4
    d = X_DIR
    u[d] = links(d)
    plus[d] = project(d, 1, psi)
    minus[d] = project(d, -1, psi)
    moved = {}
    moved[d] = link_times(u[d], shift_x(m, minus[d], 1))
    hop = add_spins(d, -1, hop, moved[d])
    hop = add_spins(d, 1, hop, shift_x(m, adjoint_times(u[d], plus[d]), -1))

    def take_backward(d, hop):
        there = shift_face(m, d, -1, back[d], face_of(inbox, d, 1), behind_sign[d])
        return add_spins(d, 1, hop, there)

    def take_forward(d, hop):
        there = shift_face(m, d, 1, minus[d], face_of(inbox, d, 0), ahead_sign[d])
        moved[d] = link_times(u[d], there)
        return add_spins(d, -1, hop, moved[d])

    def wilson(hop):
        return [(pr - KAPPA * hr, pi - KAPPA * hi) for (pr, pi), (hr, hi) in zip(psi, hop)]

    both[Z_DIR].wait_recv()
    hop = take_backward(Z_DIR, hop)
    hop = take_forward(Z_DIR, hop)
    forward[Y_DIR].wait_recv()
    hop = take_forward(Y_DIR, hop)
    hop = add_spins(Y_DIR, 1, hop, local_y(m, back[Y_DIR]))

    @pl.when(jnp.logical_not(is_first[Y_DIR]))
    def _():
        backward[Y_DIR].wait_recv()
        y_now[...] = face_of(inbox, Y_DIR, 1)[...]

    hop = add_spins(Y_DIR, 1, hop, face_y(m["halo_now"], both_spins(y_now)))

    inner = [tuple(lane_roll(v, 64) for v in parts) for parts in minus[T_DIR]]
    inner = add_spins(T_DIR, -1, hop, link_times(u[T_DIR], inner))
    stage_face(m, T_DIR, 0, project(T_DIR, 1, wilson(inner)), face_of(outbox, T_DIR, 2))
    upward[T_DIR].start()
    both[T_DIR].wait_recv()
    hop = take_backward(T_DIR, hop)
    hop = take_forward(T_DIR, hop)
    early = wilson(hop)
    for d in (Z_DIR, Y_DIR):
        stage_face(m, d, 0, project(d, 1, early), face_of(outbox, d, 2))
    upward[Z_DIR].start()
    pl.when(jnp.logical_not(is_first[Y_DIR]))(upward[Y_DIR].start)

    @pl.when(is_first[Y_DIR])
    def _():
        pl.semaphore_wait(here[Y_DIR], 1)
        forward[Y_DIR].start()
        upward[Y_DIR].start()
        backward[Y_DIR].wait_recv()

    late = face_y(m["halo_late"], both_spins(face_of(inbox, Y_DIR, 1)))
    missing = add_spins(Y_DIR, 1, [(zero, zero)] * 4, late)
    result = [
        (er - KAPPA * lr, ei - KAPPA * li) for (er, ei), (lr, li) in zip(early, missing)
    ]
    later = {d: project(d, 1, result) for d in FACES}
    for s, (re, im) in enumerate(result):
        y_buf[3 * s:3 * s + 3, 0:8] = pack_first(m, re, im)
        y_buf[3 * s:3 * s + 3, 8:16] = pack_second(m, re, im)

    def finish(d, first, later_there):
        second = outer(link_times(u[d], later_there), plus[d])
        wr, wi = c_add(first, second)
        third = (wi[0, 0] + wi[1, 1] + wi[2, 2]) / 3.0
        for a in range(3):
            for b in range(a, 3):
                if a == b:
                    im = KAPPA * (wi[a, a] - third)
                    re = jnp.zeros_like(im)
                else:
                    re = (0.5 * KAPPA) * (wr[a, b] - wr[b, a])
                    im = (0.5 * KAPPA) * (wi[a, b] + wi[b, a])
                top = pack_first(m, re, im)
                bottom = pack_second(m, re, im)
                f_buf[9 * d + 3 * a + b, 0:8] = top
                f_buf[9 * d + 3 * a + b, 8:16] = bottom
                if a != b:
                    f_buf[9 * d + 3 * b + a, 0:8] = pick(m["low"], -top, top)
                    f_buf[9 * d + 3 * b + a, 8:16] = pick(m["low"], -bottom, bottom)

    d = X_DIR
    finish(d, outer(moved[d], project(d, -1, result)), shift_x(m, project(d, 1, result), 1))
    first = {d: outer(moved[d], project(d, -1, result)) for d in FACES}
    all_up.wait()
    there = shift_face(m, Y_DIR, 1, later[Y_DIR], face_of(inbox, Y_DIR, 2), None)
    there = [
        (tr - 2 * KAPPA * only(m["own_y"], br), ti - 2 * KAPPA * only(m["own_y"], bi))
        for (tr, ti), (br, bi) in zip(there, back[Y_DIR])
    ]
    finish(Y_DIR, first[Y_DIR], there)
    edge_half = {
        T_DIR: lambda: face_y(m["edge_t"], [lane_roll(edge_t[...], 64), edge_t[...]]),
        Z_DIR: lambda: face_y(m["edge_z"], both_spins(edge_z)),
    }
    pl.when(is_first[Y_DIR])(both_edges.wait_recv)
    for d in (T_DIR, Z_DIR):
        there = shift_face(m, d, 1, later[d], face_of(inbox, d, 2), ahead_sign[d])
        if d == T_DIR:
            there = [
                (tr - 2 * KAPPA * pick(m["low"], zero, br), ti - 2 * KAPPA * pick(m["low"], zero, bi))
                for (tr, ti), (br, bi) in zip(there, back[T_DIR])
            ]
        scale = KAPPA * last_t if d == T_DIR else KAPPA
        extra = edge_term(d, edge_half[d]())
        there = [
            (tr - scale * er, ti - scale * ei) for (tr, ti), (er, ei) in zip(there, extra)
        ]
        finish(d, first[d], there)
    all_sent.wait()

    pl.when(is_last_y)(both_edges.wait_send)


def store_kernel(y_in, f_in, y_out, f_out, sems):
    copies = [
        pltpu.make_async_copy(f_in, f_out, sems.at[0]),
        pltpu.make_async_copy(y_in, y_out, sems.at[1]),
    ]
    for copy in copies:
        copy.start()
    for copy in copies:
        copy.wait()


def body(quark_field, gauge_links):
    x = quark_field.reshape(12, 16, 128)
    u = gauge_links.reshape(36, 16, 128)
    y, f = pl.pallas_call(
        kernel,
        out_shape=(pltpu.VMEM(x.shape, jnp.float32), pltpu.VMEM(u.shape, jnp.float32)),
        in_specs=[pl.BlockSpec(memory_space=pltpu.HBM)] * 2,
        out_specs=(pl.BlockSpec(memory_space=pltpu.VMEM),) * 2,
        scratch_shapes=[
            pltpu.VMEM(x.shape, jnp.float32),
            pltpu.VMEM(u.shape, jnp.float32),
            pltpu.VMEM((ALL_TILES, 8, 128), jnp.float32),
            pltpu.VMEM((ALL_TILES, 8, 128), jnp.float32),
            pltpu.VMEM((6, 8, 128), jnp.float32),
            pltpu.VMEM((3, 8, 128), jnp.float32),
            pltpu.VMEM((3, 8, 128), jnp.float32),
            pltpu.VMEM((6, 8, 128), jnp.float32),
            pltpu.SemaphoreType.DMA((2,)),
            pltpu.SemaphoreType.DMA((2,)),
            pltpu.SemaphoreType.DMA((6,)),
            pltpu.SemaphoreType.REGULAR((3,)),
        ],
        compiler_params=pltpu.CompilerParams(collective_id=0, has_side_effects=True, vmem_limit_bytes=16 * 1024 * 1024),
        cost_estimate=pl.CostEstimate(flops=6_000_000, bytes_accessed=800_000, transcendentals=0),
    )(pltpu.with_memory_space_constraint(x, pltpu.HBM), pltpu.with_memory_space_constraint(u, pltpu.HBM))
    y, f = pl.pallas_call(
        store_kernel,
        out_shape=(
            jax.ShapeDtypeStruct(x.shape, jnp.float32),
            jax.ShapeDtypeStruct(u.shape, jnp.float32),
        ),
        in_specs=[pl.BlockSpec(memory_space=pltpu.VMEM)] * 2,
        out_specs=(pl.BlockSpec(memory_space=pl.ANY),) * 2,
        scratch_shapes=[pltpu.SemaphoreType.DMA((2,))],
        compiler_params=pltpu.CompilerParams(vmem_limit_bytes=16 * 1024 * 1024),
        cost_estimate=pl.CostEstimate(flops=0, bytes_accessed=800_000, transcendentals=0),
    )(y, f)
    return y.reshape(quark_field.shape), f.reshape(gauge_links.shape)


def solution(mesh):
    specs = (
        P(None, None, "ta", "gz", "gy", None),
        P(None, None, None, "ta", "gz", "gy", None),
    )
    return jax.shard_map(body, mesh=mesh, in_specs=specs, out_specs=specs, check_vma=False)
```

```python
import functools

import jax
import jax.numpy as jnp
from jax import lax
from jax.experimental import pallas as pl
from jax.experimental.pallas import tpu as pltpu
from jax.sharding import PartitionSpec as P

KAPPA = 0.125
MESH = pl.DeviceIdType.MESH
X_DIR, Y_DIR, Z_DIR, T_DIR = 0, 1, 2, 3
AXES = {T_DIR: "ta", Z_DIR: "gz", Y_DIR: "gy"}
FACES = (T_DIR, Z_DIR, Y_DIR)
FACE_TILES = {T_DIR: 6, Z_DIR: 3, Y_DIR: 6}
FACE_START = {T_DIR: 0, Z_DIR: 18, Y_DIR: 27}
ALL_TILES = 45
RECV_SEM = {(T_DIR, 0): 0, (T_DIR, 1): 0, (Z_DIR, 0): 1, (Z_DIR, 1): 1, (Y_DIR, 0): 2, (Y_DIR, 1): 3}
RECV_UP, RECV_EDGE = 4, {T_DIR: 5, Z_DIR: 6}


def lane_roll(v, steps):
    return pltpu.roll(v.reshape(-1, 128), steps, 1).reshape(v.shape)


def row_roll(v, steps):
    if steps % 8 == 0:
        return v
    flat = v.reshape(-1, 8, 128)
    return jnp.stack([pltpu.roll(flat[i], steps % 8, 0) for i in range(flat.shape[0])]).reshape(v.shape)


def masks(at_start, at_end):
    lane = lax.broadcasted_iota(jnp.int32, (8, 128), 1)
    row = lax.broadcasted_iota(jnp.int32, (8, 128), 0)
    return {
        "low": lane < 64,
        "last_x": lane % 64 == 63,
        "first_x": lane % 64 == 0,
        "even": row % 2 == 0,
        "z_first": row < 2,
        "z_last": row >= 6,
        "row": row,
        "halo_now": row % 2 + at_start == 0,
        "halo_late": row % 2 + (1 - at_start) == 0,
        "own_y": row % 2 * at_end == 1,
        "edge_t": (row % 2 + (1 - at_start) == 0) & (lane >= 64),
        "edge_z": row + 8 * (1 - at_start) == 6,
    }


def pick(mask, a, b):
    return jnp.where(jnp.broadcast_to(mask, a.shape), a, b)


def unpack(m, first, second):
    return (
        pick(m["low"], first, lane_roll(second, 64)),
        pick(m["low"], lane_roll(first, 64), second),
    )


def pack_first(m, re, im):
    return pick(m["low"], re, lane_roll(im, 64))


def pack_second(m, re, im):
    return pick(m["low"], lane_roll(re, 64), im)


def c_add(a, b):
    return (a[0] + b[0], a[1] + b[1])


def c_sub(a, b):
    return (a[0] - b[0], a[1] - b[1])


def add_i(a, b):
    return (a[0] - b[1], a[1] + b[0])


def sub_i(a, b):
    return (a[0] + b[1], a[1] - b[0])


def project(direction, sign, psi):
    u0, u1, l0, l1 = psi
    plus, minus = (c_add, c_sub) if sign < 0 else (c_sub, c_add)
    plus_i, minus_i = (add_i, sub_i) if sign < 0 else (sub_i, add_i)
    if direction == X_DIR:
        return [plus_i(u0, l1), plus_i(u1, l0)]
    if direction == Y_DIR:
        return [plus(u0, l1), minus(u1, l0)]
    if direction == Z_DIR:
        return [plus_i(u0, l0), minus_i(u1, l1)]
    return [minus(u0, l0), minus(u1, l1)]


def add_spins(direction, sign, total, half):
    h0, h1 = half
    plus, minus = (c_sub, c_add) if sign < 0 else (c_add, c_sub)
    plus_i, minus_i = (sub_i, add_i) if sign < 0 else (add_i, sub_i)
    t0, t1, t2, t3 = total
    upper = [c_add(t0, h0), c_add(t1, h1)]
    if direction == X_DIR:
        return upper + [plus_i(t2, h1), plus_i(t3, h0)]
    if direction == Y_DIR:
        return upper + [plus(t2, h1), minus(t3, h0)]
    if direction == Z_DIR:
        return upper + [plus_i(t2, h0), minus_i(t3, h1)]
    return upper + [plus(t2, h0), plus(t3, h1)]


def link_times(u, half):
    ur, ui = u
    out = []
    for hr, hi in half:
        re = im = None
        for b in range(3):
            cr, ci = ur[:, b], ui[:, b]
            r = cr * hr[b][None] - ci * hi[b][None]
            i = cr * hi[b][None] + ci * hr[b][None]
            re = r if re is None else re + r
            im = i if im is None else im + i
        out.append((re, im))
    return out


def adjoint_times(u, half):
    ur, ui = u
    out = []
    for hr, hi in half:
        re = im = None
        for b in range(3):
            cr, ci = ur[b], ui[b]
            r = cr * hr[b][None] + ci * hi[b][None]
            i = cr * hi[b][None] - ci * hr[b][None]
            re = r if re is None else re + r
            im = i if im is None else im + i
        out.append((re, im))
    return out


def outer(left, right):
    re = im = None
    for (lr, li), (rr, ri) in zip(left, right):
        r = lr[:, None] * rr[None] + li[:, None] * ri[None]
        i = li[:, None] * rr[None] - lr[:, None] * ri[None]
        re = r if re is None else re + r
        im = i if im is None else im + i
    return re, im


def shift_x(m, half, steps):
    def one(v):
        if steps > 0:
            return pick(m["last_x"], lane_roll(v, 63), lane_roll(v, 127))
        return pick(m["first_x"], lane_roll(v, 65), lane_roll(v, 1))

    return [(one(re), one(im)) for re, im in half]


def stage_face(m, direction, end, half, ref):
    if direction == T_DIR:
        for s, (re, im) in enumerate(half):
            ref[3 * s:3 * s + 3] = (pack_second if end else pack_first)(m, re, im)
    elif direction == Y_DIR:
        for s, (re, im) in enumerate(half):
            if end:
                tile = pick(m["even"], row_roll(re, -1), im)
            else:
                tile = pick(m["even"], re, row_roll(im, 1))
            ref[3 * s:3 * s + 3] = tile
    else:
        tiles = [part[c] for re, im in half for part in (re, im) for c in range(3)]
        for j in range(3):
            tile = row_roll(tiles[4 * j], 2 if end else 0)
            for k in range(1, 4):
                moved = row_roll(tiles[4 * j + k], 2 * k + (2 if end else 0))
                tile = pick(m["row"] < 2 * k, tile, moved)
            ref[j] = tile


def shift_face(m, direction, steps, half, ref, sign):
    out = []
    if direction == T_DIR:
        for s, (re, im) in enumerate(half):
            face = ref[3 * s:3 * s + 3] * sign
            if steps > 0:
                out.append((
                    lane_roll(pick(m["low"], face, re), 64),
                    pick(m["low"], lane_roll(im, 64), face),
                ))
            else:
                out.append((
                    pick(m["low"], face, lane_roll(re, 64)),
                    lane_roll(pick(m["low"], im, face), 64),
                ))
    elif direction == Y_DIR:
        for s, (re, im) in enumerate(half):
            face = ref[3 * s:3 * s + 3]
            if steps > 0:
                out.append((
                    pick(m["even"], row_roll(re, -1), row_roll(face, 1)),
                    pick(m["even"], row_roll(im, -1), face),
                ))
            else:
                out.append((
                    pick(m["even"], face, row_roll(re, 1)),
                    pick(m["even"], row_roll(face, -1), row_roll(im, 1)),
                ))
    else:
        n = 0
        for re, im in half:
            parts = []
            for part in (re, im):
                moved = []
                for c in range(3):
                    face = ref[n // 4]
                    k = n % 4
                    n += 1
                    if steps > 0:
                        moved.append(row_roll(pick(m["z_first"], row_roll(face, -2 * k), part[c]), -2))
                    else:
                        moved.append(row_roll(pick(m["z_last"], row_roll(face, 6 - 2 * k), part[c]), 2))
                parts.append(jnp.stack(moved))
            out.append(tuple(parts))
    return out


def only(mask, v):
    return pick(mask, v, jnp.zeros_like(v))


def local_y(m, half):
    return [tuple(pick(m["even"], jnp.zeros_like(v), row_roll(v, 1)) for v in parts) for parts in half]


def face_y(mask, faces):
    return [(only(mask, face), only(mask, row_roll(face, -1))) for face in faces]


def both_spins(ref):
    return [ref[0:3], ref[3:6]]


def edge_term(direction, half):
    h0, h1 = half
    return project(direction, 1, [h0, h1, h1, (-h0[0], -h0[1])])


def kernel(
    x_hbm, u_hbm, y_buf, f_buf,
    x_buf, u_buf,
    outbox, inbox, y_now, edge_out, edge_t, edge_z,
    load_sem, send_sem, recv_sem, here_sem,
):
    def face_of(box, d, slot, faces=1):
        return box.at[pl.ds(FACE_START[d] + slot * FACE_TILES[d], faces * FACE_TILES[d])]

    first_load = pltpu.make_async_copy(u_hbm.at[pl.ds(0, 21)], u_buf.at[pl.ds(0, 21)], load_sem.at[0])
    rest_load = pltpu.make_async_copy(u_hbm.at[pl.ds(0, 27)], u_buf.at[pl.ds(0, 27)], load_sem.at[1])

    def load(source, target, start, count, sem):
        part = pl.ds(start, count)
        pltpu.make_async_copy(source.at[part], target.at[part], load_sem.at[sem]).start()

    for s in range(3):
        load(x_hbm, x_buf, 4 * s, 4, 0)
    for a in range(3):
        load(u_hbm, u_buf, 9 * Y_DIR + 3 * a, 3, 0)
    me = {d: lax.axis_index(AXES[d]) for d in FACES}
    size = {d: lax.axis_size(AXES[d]) for d in FACES}
    ahead = {d: lax.rem(me[d] + 1, size[d]) for d in FACES}
    behind = {d: lax.rem(me[d] + size[d] - 1, size[d]) for d in FACES}

    barrier = pltpu.get_barrier_semaphore()
    is_first = {d: me[d] == 0 for d in FACES}
    is_last = {d: me[d] == size[d] - 1 for d in FACES}
    is_last_y = is_last[Y_DIR]

    def greet(where):
        pl.semaphore_signal(barrier, inc=1, device_id=where, device_id_type=MESH)

    odd = lax.rem(me[T_DIR], 2) == 1
    greeter = odd ^ (me[Z_DIR] < size[Z_DIR] // 2)
    plain = jnp.logical_not(is_last_y)
    pl.when(plain | greeter | is_first[T_DIR])(functools.partial(greet, {AXES[T_DIR]: behind[T_DIR]}))
    pl.when(plain | is_first[Z_DIR])(functools.partial(greet, {AXES[Z_DIR]: behind[Z_DIR]}))
    pl.when((plain | greeter) & jnp.logical_not(is_last[T_DIR]))(functools.partial(greet, {AXES[T_DIR]: ahead[T_DIR]}))
    for d in (Z_DIR, Y_DIR):
        pl.when(jnp.logical_not(is_last[d]))(functools.partial(greet, {AXES[d]: ahead[d]}))

    @pl.when(is_first[Y_DIR])
    def _():
        greet({AXES[Y_DIR]: behind[Y_DIR]})
        for d in (T_DIR, Z_DIR):
            greet({AXES[d]: ahead[d], AXES[Y_DIR]: behind[Y_DIR]})

    def one(flag):
        return flag.astype(jnp.int32)

    plain_arrivals = 5 - sum(one(is_first[d]) for d in FACES)
    late_t = jnp.where(greeter, one(odd & is_last[T_DIR]), 2 - one(is_first[T_DIR]))
    late_arrivals = late_t + 1 + one(is_last[Z_DIR]) - one(is_first[Z_DIR]) + 4
    late_replies = one(jnp.logical_not(is_last[Z_DIR])) + jnp.where(greeter, 2 - one(is_last[T_DIR]) - one(is_first[T_DIR]), 0)
    arrivals = jnp.where(is_last_y, late_arrivals, plain_arrivals)
    replies = jnp.where(is_last_y, late_replies, 1)
    for d in (T_DIR, Z_DIR, X_DIR):
        load(u_hbm, u_buf, 9 * d, 9, 1)

    def link(d, slot, there, faces=1):
        return pltpu.make_async_remote_copy(
            src_ref=face_of(outbox, d, slot, faces),
            dst_ref=face_of(inbox, d, slot, faces),
            send_sem=send_sem.at[0],
            recv_sem=recv_sem.at[RECV_SEM.get((d, slot), RECV_UP)],
            device_id={AXES[d]: there},
            device_id_type=MESH,
        )

    forward = {d: link(d, 0, behind[d]) for d in FACES}
    backward = {d: link(d, 1, ahead[d]) for d in FACES}
    upward = {d: link(d, 2, behind[d]) for d in FACES}
    both = {d: link(d, 0, behind[d], 2) for d in (T_DIR, Z_DIR)}
    all_up = pltpu.make_async_copy(outbox.at[pl.ds(0, 15)], inbox.at[pl.ds(0, 15)], recv_sem.at[RECV_UP])
    all_sent = pltpu.make_async_copy(outbox, inbox, send_sem.at[0])

    def edge_link(d, src, dst):
        return pltpu.make_async_remote_copy(
            src_ref=src,
            dst_ref=dst,
            send_sem=send_sem.at[1],
            recv_sem=recv_sem.at[RECV_EDGE[d]],
            device_id={AXES[d]: behind[d], AXES[Y_DIR]: ahead[Y_DIR]},
            device_id_type=MESH,
        )

    edges = {
        T_DIR: edge_link(T_DIR, edge_out, edge_t),
        Z_DIR: edge_link(Z_DIR, face_of(outbox, Y_DIR, 1).at[:, 0:2], edge_z.at[:, 6:8]),
    }
    both_edges = edge_link(T_DIR, y_now.at[:, 0:6], y_now.at[:, 0:6])

    here = {T_DIR: here_sem.at[0], Z_DIR: here_sem.at[0], Y_DIR: here_sem.at[1]}
    here_near = here_sem.at[2]

    def say_here():
        def say(sem, there):
            pl.semaphore_signal(sem, inc=1, device_id=there, device_id_type=MESH)

        for d in FACES:
            pl.when(is_last[d])(functools.partial(say, here[d], {AXES[d]: ahead[d]}))
        there = {AXES[Y_DIR]: behind[Y_DIR]}
        pl.when(jnp.logical_not(is_first[Y_DIR]))(functools.partial(say, here_near, there))

        @pl.when(is_last_y)
        def _():
            pl.when(jnp.logical_not(is_first[Z_DIR]))(functools.partial(say, here_near, {AXES[Z_DIR]: behind[Z_DIR]}))
            greeted = jnp.logical_not(greeter)
            pl.when(greeted & jnp.logical_not(is_last[T_DIR]))(
                functools.partial(say, here_near, {AXES[T_DIR]: ahead[T_DIR]})
            )
            pl.when(greeted & jnp.logical_not(is_first[T_DIR]))(
                functools.partial(say, here_near, {AXES[T_DIR]: behind[T_DIR]})
            )

    m = masks(is_first[Y_DIR].astype(jnp.int32), is_last_y.astype(jnp.int32))
    last_t = jnp.where(me[T_DIR] == size[T_DIR] - 1, -1.0, 1.0).astype(jnp.float32)
    first_t = jnp.where(me[T_DIR] == 0, -1.0, 1.0).astype(jnp.float32)
    ahead_sign = {T_DIR: last_t, Z_DIR: None, Y_DIR: None}
    behind_sign = {T_DIR: first_t, Z_DIR: None, Y_DIR: None}

    first_load.wait()
    psi = [unpack(m, x_buf[3 * s:3 * s + 3, 0:8], x_buf[3 * s:3 * s + 3, 8:16]) for s in range(4)]
    minus = {}
    plus = {}
    u = {}
    back = {}

    def links(d):
        first, second = unpack(m, u_buf[9 * d:9 * d + 9, 0:8], u_buf[9 * d:9 * d + 9, 8:16])
        return first.reshape(3, 3, 8, 128), second.reshape(3, 3, 8, 128)

    def prepare_backward(d):
        u[d] = links(d)
        plus[d] = project(d, 1, psi)
        back[d] = adjoint_times(u[d], plus[d])
        stage_face(m, d, 1, back[d], face_of(outbox, d, 1))

    prepare_backward(Y_DIR)

    @pl.when(is_last_y)
    def _():
        pl.semaphore_wait(barrier, arrivals)
        edges[Z_DIR].start()
        spins = both_spins(face_of(outbox, Y_DIR, 1))
        edge_out[...] = pick(m["low"], spins[0], lane_roll(spins[1], 64))
        edges[T_DIR].start()
        backward[Y_DIR].start()
        say_here()

    for d in FACES:
        minus[d] = project(d, -1, psi)
        stage_face(m, d, 0, minus[d], face_of(outbox, d, 0))
    rest_load.wait()
    for d in (T_DIR, Z_DIR):
        prepare_backward(d)

    @pl.when(jnp.logical_not(is_last_y))
    def _():
        pl.semaphore_wait(barrier, arrivals)
        say_here()

    pl.when(is_last_y & (replies > 0))(lambda: pl.semaphore_wait(here_near, replies))
    for d in (T_DIR, Z_DIR):
        backward[d].start()
    for d in FACES:
        pl.when(jnp.logical_not(is_first[d]))(forward[d].start)

    @pl.when(is_first[T_DIR] | is_first[Z_DIR])
    def _():
        pl.semaphore_wait(here[T_DIR], is_first[T_DIR].astype(jnp.int32) + is_first[Z_DIR].astype(jnp.int32))
        for d in (T_DIR, Z_DIR):
            pl.when(is_first[d])(forward[d].start)

    @pl.when(jnp.logical_not(is_last_y))
    def _():
        pl.semaphore_wait(here_near, replies)
        backward[Y_DIR].start()

    zero = jnp.zeros((3, 8, 128), jnp.float32)
    hop = [(zero, zero)] * 4
    d = X_DIR
    u[d] = links(d)
    plus[d] = project(d, 1, psi)
    minus[d] = project(d, -1, psi)
    moved = {}
    moved[d] = link_times(u[d], shift_x(m, minus[d], 1))
    hop = add_spins(d, -1, hop, moved[d])
    hop = add_spins(d, 1, hop, shift_x(m, adjoint_times(u[d], plus[d]), -1))

    def take_backward(d, hop):
        there = shift_face(m, d, -1, back[d], face_of(inbox, d, 1), behind_sign[d])
        return add_spins(d, 1, hop, there)

    def take_forward(d, hop):
        there = shift_face(m, d, 1, minus[d], face_of(inbox, d, 0), ahead_sign[d])
        moved[d] = link_times(u[d], there)
        return add_spins(d, -1, hop, moved[d])

    def wilson(hop):
        return [(pr - KAPPA * hr, pi - KAPPA * hi) for (pr, pi), (hr, hi) in zip(psi, hop)]

    both[Z_DIR].wait_recv()
    hop = take_backward(Z_DIR, hop)
    hop = take_forward(Z_DIR, hop)
    forward[Y_DIR].wait_recv()
    hop = take_forward(Y_DIR, hop)
    hop = add_spins(Y_DIR, 1, hop, local_y(m, back[Y_DIR]))

    @pl.when(jnp.logical_not(is_first[Y_DIR]))
    def _():
        backward[Y_DIR].wait_recv()
        y_now[...] = face_of(inbox, Y_DIR, 1)[...]

    hop = add_spins(Y_DIR, 1, hop, face_y(m["halo_now"], both_spins(y_now)))

    inner = [tuple(lane_roll(v, 64) for v in parts) for parts in minus[T_DIR]]
    inner = add_spins(T_DIR, -1, hop, link_times(u[T_DIR], inner))
    stage_face(m, T_DIR, 0, project(T_DIR, 1, wilson(inner)), face_of(outbox, T_DIR, 2))
    upward[T_DIR].start()
    both[T_DIR].wait_recv()
    hop = take_backward(T_DIR, hop)
    hop = take_forward(T_DIR, hop)
    early = wilson(hop)
    for d in (Z_DIR, Y_DIR):
        stage_face(m, d, 0, project(d, 1, early), face_of(outbox, d, 2))
    upward[Z_DIR].start()
    pl.when(jnp.logical_not(is_first[Y_DIR]))(upward[Y_DIR].start)

    @pl.when(is_first[Y_DIR])
    def _():
        pl.semaphore_wait(here[Y_DIR], 1)
        forward[Y_DIR].start()
        upward[Y_DIR].start()
        backward[Y_DIR].wait_recv()

    late = face_y(m["halo_late"], both_spins(face_of(inbox, Y_DIR, 1)))
    missing = add_spins(Y_DIR, 1, [(zero, zero)] * 4, late)
    result = [
        (er - KAPPA * lr, ei - KAPPA * li) for (er, ei), (lr, li) in zip(early, missing)
    ]
    later = {d: project(d, 1, result) for d in FACES}
    for s, (re, im) in enumerate(result):
        y_buf[3 * s:3 * s + 3, 0:8] = pack_first(m, re, im)
        y_buf[3 * s:3 * s + 3, 8:16] = pack_second(m, re, im)

    def finish(d, first, later_there):
        second = outer(link_times(u[d], later_there), plus[d])
        wr, wi = c_add(first, second)
        third = (wi[0, 0] + wi[1, 1] + wi[2, 2]) / 3.0
        for a in range(3):
            for b in range(a, 3):
                if a == b:
                    im = KAPPA * (wi[a, a] - third)
                    re = jnp.zeros_like(im)
                else:
                    re = (0.5 * KAPPA) * (wr[a, b] - wr[b, a])
                    im = (0.5 * KAPPA) * (wi[a, b] + wi[b, a])
                top = pack_first(m, re, im)
                bottom = pack_second(m, re, im)
                f_buf[9 * d + 3 * a + b, 0:8] = top
                f_buf[9 * d + 3 * a + b, 8:16] = bottom
                if a != b:
                    f_buf[9 * d + 3 * b + a, 0:8] = pick(m["low"], -top, top)
                    f_buf[9 * d + 3 * b + a, 8:16] = pick(m["low"], -bottom, bottom)

    d = X_DIR
    finish(d, outer(moved[d], project(d, -1, result)), shift_x(m, project(d, 1, result), 1))
    first = {d: outer(moved[d], project(d, -1, result)) for d in FACES}
    all_up.wait()
    there = shift_face(m, Y_DIR, 1, later[Y_DIR], face_of(inbox, Y_DIR, 2), None)
    there = [
        (tr - 2 * KAPPA * only(m["own_y"], br), ti - 2 * KAPPA * only(m["own_y"], bi))
        for (tr, ti), (br, bi) in zip(there, back[Y_DIR])
    ]
    finish(Y_DIR, first[Y_DIR], there)
    edge_half = {
        T_DIR: lambda: face_y(m["edge_t"], [lane_roll(edge_t[...], 64), edge_t[...]]),
        Z_DIR: lambda: face_y(m["edge_z"], both_spins(edge_z)),
    }
    for d in (T_DIR, Z_DIR):
        there = shift_face(m, d, 1, later[d], face_of(inbox, d, 2), ahead_sign[d])
        if d == T_DIR:
            there = [
                (tr - 2 * KAPPA * pick(m["low"], zero, br), ti - 2 * KAPPA * pick(m["low"], zero, bi))
                for (tr, ti), (br, bi) in zip(there, back[T_DIR])
            ]
        pl.when(is_first[Y_DIR])(edges[d].wait_recv)
        scale = KAPPA * last_t if d == T_DIR else KAPPA
        extra = edge_term(d, edge_half[d]())
        there = [
            (tr - scale * er, ti - scale * ei) for (tr, ti), (er, ei) in zip(there, extra)
        ]
        finish(d, first[d], there)
    all_sent.wait()

    pl.when(is_last_y)(both_edges.wait_send)


def store_kernel(y_in, f_in, y_out, f_out, sems):
    copies = [
        pltpu.make_async_copy(f_in, f_out, sems.at[0]),
        pltpu.make_async_copy(y_in, y_out, sems.at[1]),
    ]
    for copy in copies:
        copy.start()
    for copy in copies:
        copy.wait()


def body(quark_field, gauge_links):
    x = quark_field.reshape(12, 16, 128)
    u = gauge_links.reshape(36, 16, 128)
    y, f = pl.pallas_call(
        kernel,
        out_shape=(pltpu.VMEM(x.shape, jnp.float32), pltpu.VMEM(u.shape, jnp.float32)),
        in_specs=[pl.BlockSpec(memory_space=pltpu.HBM)] * 2,
        out_specs=(pl.BlockSpec(memory_space=pltpu.VMEM),) * 2,
        scratch_shapes=[
            pltpu.VMEM(x.shape, jnp.float32),
            pltpu.VMEM(u.shape, jnp.float32),
            pltpu.VMEM((ALL_TILES, 8, 128), jnp.float32),
            pltpu.VMEM((ALL_TILES, 8, 128), jnp.float32),
            pltpu.VMEM((6, 8, 128), jnp.float32),
            pltpu.VMEM((3, 8, 128), jnp.float32),
            pltpu.VMEM((3, 8, 128), jnp.float32),
            pltpu.VMEM((6, 8, 128), jnp.float32),
            pltpu.SemaphoreType.DMA((2,)),
            pltpu.SemaphoreType.DMA((2,)),
            pltpu.SemaphoreType.DMA((7,)),
            pltpu.SemaphoreType.REGULAR((3,)),
        ],
        compiler_params=pltpu.CompilerParams(collective_id=0, has_side_effects=True, vmem_limit_bytes=16 * 1024 * 1024),
        cost_estimate=pl.CostEstimate(flops=6_000_000, bytes_accessed=800_000, transcendentals=0),
    )(pltpu.with_memory_space_constraint(x, pltpu.HBM), pltpu.with_memory_space_constraint(u, pltpu.HBM))
    y, f = pl.pallas_call(
        store_kernel,
        out_shape=(
            jax.ShapeDtypeStruct(x.shape, jnp.float32),
            jax.ShapeDtypeStruct(u.shape, jnp.float32),
        ),
        in_specs=[pl.BlockSpec(memory_space=pltpu.VMEM)] * 2,
        out_specs=(pl.BlockSpec(memory_space=pl.ANY),) * 2,
        scratch_shapes=[pltpu.SemaphoreType.DMA((2,))],
        compiler_params=pltpu.CompilerParams(vmem_limit_bytes=16 * 1024 * 1024),
        cost_estimate=pl.CostEstimate(flops=0, bytes_accessed=800_000, transcendentals=0),
    )(y, f)
    return y.reshape(quark_field.shape), f.reshape(gauge_links.shape)


def solution(mesh):
    specs = (
        P(None, None, "ta", "gz", "gy", None),
        P(None, None, None, "ta", "gz", "gy", None),
    )
    return jax.shard_map(body, mesh=mesh, in_specs=specs, out_specs=specs, check_vma=False)
```

```python
import functools

import jax
import jax.numpy as jnp
from jax import lax
from jax.experimental import pallas as pl
from jax.experimental.pallas import tpu as pltpu
from jax.sharding import PartitionSpec as P

KAPPA = 0.125
MESH = pl.DeviceIdType.MESH
X_DIR, Y_DIR, Z_DIR, T_DIR = 0, 1, 2, 3
AXES = {T_DIR: "ta", Z_DIR: "gz", Y_DIR: "gy"}
FACES = (T_DIR, Z_DIR, Y_DIR)
FACE_TILES = {T_DIR: 6, Z_DIR: 3, Y_DIR: 6}
FACE_START = {T_DIR: 0, Z_DIR: 18, Y_DIR: 27}
ALL_TILES = 45
RECV_SEM = {(T_DIR, 0): 0, (T_DIR, 1): 0, (Z_DIR, 0): 1, (Z_DIR, 1): 1, (Y_DIR, 0): 2, (Y_DIR, 1): 3}
RECV_UP, RECV_EDGE = 4, {T_DIR: 5, Z_DIR: 6}


def lane_roll(v, steps):
    return pltpu.roll(v.reshape(-1, 128), steps, 1).reshape(v.shape)


def row_roll(v, steps):
    if steps % 8 == 0:
        return v
    flat = v.reshape(-1, 8, 128)
    return jnp.stack([pltpu.roll(flat[i], steps % 8, 0) for i in range(flat.shape[0])]).reshape(v.shape)


def masks(at_start, at_end):
    lane = lax.broadcasted_iota(jnp.int32, (8, 128), 1)
    row = lax.broadcasted_iota(jnp.int32, (8, 128), 0)
    return {
        "low": lane < 64,
        "last_x": lane % 64 == 63,
        "first_x": lane % 64 == 0,
        "even": row % 2 == 0,
        "z_first": row < 2,
        "z_last": row >= 6,
        "row": row,
        "halo_now": row % 2 + at_start == 0,
        "halo_late": row % 2 + (1 - at_start) == 0,
        "own_y": row % 2 * at_end == 1,
        "edge_t": (row % 2 + (1 - at_start) == 0) & (lane >= 64),
        "edge_z": row + 8 * (1 - at_start) == 6,
    }


def pick(mask, a, b):
    return jnp.where(jnp.broadcast_to(mask, a.shape), a, b)


def unpack(m, first, second):
    return (
        pick(m["low"], first, lane_roll(second, 64)),
        pick(m["low"], lane_roll(first, 64), second),
    )


def pack_first(m, re, im):
    return pick(m["low"], re, lane_roll(im, 64))


def pack_second(m, re, im):
    return pick(m["low"], lane_roll(re, 64), im)


def c_add(a, b):
    return (a[0] + b[0], a[1] + b[1])


def c_sub(a, b):
    return (a[0] - b[0], a[1] - b[1])


def add_i(a, b):
    return (a[0] - b[1], a[1] + b[0])


def sub_i(a, b):
    return (a[0] + b[1], a[1] - b[0])


def project(direction, sign, psi):
    u0, u1, l0, l1 = psi
    plus, minus = (c_add, c_sub) if sign < 0 else (c_sub, c_add)
    plus_i, minus_i = (add_i, sub_i) if sign < 0 else (sub_i, add_i)
    if direction == X_DIR:
        return [plus_i(u0, l1), plus_i(u1, l0)]
    if direction == Y_DIR:
        return [plus(u0, l1), minus(u1, l0)]
    if direction == Z_DIR:
        return [plus_i(u0, l0), minus_i(u1, l1)]
    return [minus(u0, l0), minus(u1, l1)]


def add_spins(direction, sign, total, half):
    h0, h1 = half
    plus, minus = (c_sub, c_add) if sign < 0 else (c_add, c_sub)
    plus_i, minus_i = (sub_i, add_i) if sign < 0 else (add_i, sub_i)
    t0, t1, t2, t3 = total
    upper = [c_add(t0, h0), c_add(t1, h1)]
    if direction == X_DIR:
        return upper + [plus_i(t2, h1), plus_i(t3, h0)]
    if direction == Y_DIR:
        return upper + [plus(t2, h1), minus(t3, h0)]
    if direction == Z_DIR:
        return upper + [plus_i(t2, h0), minus_i(t3, h1)]
    return upper + [plus(t2, h0), plus(t3, h1)]


def link_times(u, half):
    ur, ui = u
    out = []
    for hr, hi in half:
        re = im = None
        for b in range(3):
            cr, ci = ur[:, b], ui[:, b]
            r = cr * hr[b][None] - ci * hi[b][None]
            i = cr * hi[b][None] + ci * hr[b][None]
            re = r if re is None else re + r
            im = i if im is None else im + i
        out.append((re, im))
    return out


def adjoint_times(u, half):
    ur, ui = u
    out = []
    for hr, hi in half:
        re = im = None
        for b in range(3):
            cr, ci = ur[b], ui[b]
            r = cr * hr[b][None] + ci * hi[b][None]
            i = cr * hi[b][None] - ci * hr[b][None]
            re = r if re is None else re + r
            im = i if im is None else im + i
        out.append((re, im))
    return out


def outer(left, right):
    re = im = None
    for (lr, li), (rr, ri) in zip(left, right):
        r = lr[:, None] * rr[None] + li[:, None] * ri[None]
        i = li[:, None] * rr[None] - lr[:, None] * ri[None]
        re = r if re is None else re + r
        im = i if im is None else im + i
    return re, im


def shift_x(m, half, steps):
    def one(v):
        if steps > 0:
            return pick(m["last_x"], lane_roll(v, 63), lane_roll(v, 127))
        return pick(m["first_x"], lane_roll(v, 65), lane_roll(v, 1))

    return [(one(re), one(im)) for re, im in half]


def stage_face(m, direction, end, half, ref):
    if direction == T_DIR:
        for s, (re, im) in enumerate(half):
            ref[3 * s:3 * s + 3] = (pack_second if end else pack_first)(m, re, im)
    elif direction == Y_DIR:
        for s, (re, im) in enumerate(half):
            if end:
                tile = pick(m["even"], row_roll(re, -1), im)
            else:
                tile = pick(m["even"], re, row_roll(im, 1))
            ref[3 * s:3 * s + 3] = tile
    else:
        tiles = [part[c] for re, im in half for part in (re, im) for c in range(3)]
        for j in range(3):
            tile = row_roll(tiles[4 * j], 2 if end else 0)
            for k in range(1, 4):
                moved = row_roll(tiles[4 * j + k], 2 * k + (2 if end else 0))
                tile = pick(m["row"] < 2 * k, tile, moved)
            ref[j] = tile


def shift_face(m, direction, steps, half, ref, sign):
    out = []
    if direction == T_DIR:
        for s, (re, im) in enumerate(half):
            face = ref[3 * s:3 * s + 3] * sign
            if steps > 0:
                out.append((
                    lane_roll(pick(m["low"], face, re), 64),
                    pick(m["low"], lane_roll(im, 64), face),
                ))
            else:
                out.append((
                    pick(m["low"], face, lane_roll(re, 64)),
                    lane_roll(pick(m["low"], im, face), 64),
                ))
    elif direction == Y_DIR:
        for s, (re, im) in enumerate(half):
            face = ref[3 * s:3 * s + 3]
            if steps > 0:
                out.append((
                    pick(m["even"], row_roll(re, -1), row_roll(face, 1)),
                    pick(m["even"], row_roll(im, -1), face),
                ))
            else:
                out.append((
                    pick(m["even"], face, row_roll(re, 1)),
                    pick(m["even"], row_roll(face, -1), row_roll(im, 1)),
                ))
    else:
        n = 0
        for re, im in half:
            parts = []
            for part in (re, im):
                moved = []
                for c in range(3):
                    face = ref[n // 4]
                    k = n % 4
                    n += 1
                    if steps > 0:
                        moved.append(row_roll(pick(m["z_first"], row_roll(face, -2 * k), part[c]), -2))
                    else:
                        moved.append(row_roll(pick(m["z_last"], row_roll(face, 6 - 2 * k), part[c]), 2))
                parts.append(jnp.stack(moved))
            out.append(tuple(parts))
    return out


def only(mask, v):
    return pick(mask, v, jnp.zeros_like(v))


def local_y(m, half):
    return [tuple(pick(m["even"], jnp.zeros_like(v), row_roll(v, 1)) for v in parts) for parts in half]


def face_y(mask, faces):
    return [(only(mask, face), only(mask, row_roll(face, -1))) for face in faces]


def both_spins(ref):
    return [ref[0:3], ref[3:6]]


def edge_term(direction, half):
    h0, h1 = half
    return project(direction, 1, [h0, h1, h1, (-h0[0], -h0[1])])


def write_force(low, u, plus, first, later_there, f_buf, start):
    second = outer(link_times(u, later_there), plus)
    wr, wi = c_add(first, second)
    third = (wi[0, 0] + wi[1, 1] + wi[2, 2]) / 3.0
    m = {"low": low}
    for a in range(3):
        for b in range(a, 3):
            if a == b:
                im = KAPPA * (wi[a, a] - third)
                re = jnp.zeros_like(im)
            else:
                re = (0.5 * KAPPA) * (wr[a, b] - wr[b, a])
                im = (0.5 * KAPPA) * (wi[a, b] + wi[b, a])
            top = pack_first(m, re, im)
            bottom = pack_second(m, re, im)
            f_buf[start + 3 * a + b, 0:8] = top
            f_buf[start + 3 * a + b, 8:16] = bottom
            if a != b:
                f_buf[start + 3 * b + a, 0:8] = pick(low, -top, top)
                f_buf[start + 3 * b + a, 8:16] = pick(low, -bottom, bottom)


def kernel(
    x_hbm, u_hbm, y_buf, f_buf, z_buf,
    x_buf, u_buf,
    outbox, inbox, y_now, edge_out, edge_t, edge_z,
    load_sem, send_sem, recv_sem, here_sem,
):
    def face_of(box, d, slot, faces=1):
        return box.at[pl.ds(FACE_START[d] + slot * FACE_TILES[d], faces * FACE_TILES[d])]

    first_load = pltpu.make_async_copy(u_hbm.at[pl.ds(0, 21)], u_buf.at[pl.ds(0, 21)], load_sem.at[0])
    rest_load = pltpu.make_async_copy(u_hbm.at[pl.ds(0, 27)], u_buf.at[pl.ds(0, 27)], load_sem.at[1])

    def load(source, target, start, count, sem):
        part = pl.ds(start, count)
        pltpu.make_async_copy(source.at[part], target.at[part], load_sem.at[sem]).start()

    for s in range(3):
        load(x_hbm, x_buf, 4 * s, 4, 0)
    for a in range(3):
        load(u_hbm, u_buf, 9 * Y_DIR + 3 * a, 3, 0)
    me = {d: lax.axis_index(AXES[d]) for d in FACES}
    size = {d: lax.axis_size(AXES[d]) for d in FACES}
    ahead = {d: lax.rem(me[d] + 1, size[d]) for d in FACES}
    behind = {d: lax.rem(me[d] + size[d] - 1, size[d]) for d in FACES}

    barrier = pltpu.get_barrier_semaphore()
    is_first = {d: me[d] == 0 for d in FACES}
    is_last = {d: me[d] == size[d] - 1 for d in FACES}
    is_last_y = is_last[Y_DIR]

    def greet(where):
        pl.semaphore_signal(barrier, inc=1, device_id=where, device_id_type=MESH)

    odd = lax.rem(me[T_DIR], 2) == 1
    greeter = odd ^ (me[Z_DIR] < size[Z_DIR] // 2)
    plain = jnp.logical_not(is_last_y)
    pl.when(plain | greeter | is_first[T_DIR])(functools.partial(greet, {AXES[T_DIR]: behind[T_DIR]}))
    pl.when(plain | is_first[Z_DIR])(functools.partial(greet, {AXES[Z_DIR]: behind[Z_DIR]}))
    pl.when((plain | greeter) & jnp.logical_not(is_last[T_DIR]))(functools.partial(greet, {AXES[T_DIR]: ahead[T_DIR]}))
    for d in (Z_DIR, Y_DIR):
        pl.when(jnp.logical_not(is_last[d]))(functools.partial(greet, {AXES[d]: ahead[d]}))

    @pl.when(is_first[Y_DIR])
    def _():
        greet({AXES[Y_DIR]: behind[Y_DIR]})
        for d in (T_DIR, Z_DIR):
            greet({AXES[d]: ahead[d], AXES[Y_DIR]: behind[Y_DIR]})

    def one(flag):
        return flag.astype(jnp.int32)

    plain_arrivals = 5 - sum(one(is_first[d]) for d in FACES)
    late_t = jnp.where(greeter, one(odd & is_last[T_DIR]), 2 - one(is_first[T_DIR]))
    late_arrivals = late_t + 1 + one(is_last[Z_DIR]) - one(is_first[Z_DIR]) + 4
    late_replies = one(jnp.logical_not(is_last[Z_DIR])) + jnp.where(greeter, 2 - one(is_last[T_DIR]) - one(is_first[T_DIR]), 0)
    arrivals = jnp.where(is_last_y, late_arrivals, plain_arrivals)
    replies = jnp.where(is_last_y, late_replies, 1)
    for d in (T_DIR, Z_DIR, X_DIR):
        load(u_hbm, u_buf, 9 * d, 9, 1)

    def link(d, slot, there, faces=1):
        return pltpu.make_async_remote_copy(
            src_ref=face_of(outbox, d, slot, faces),
            dst_ref=face_of(inbox, d, slot, faces),
            send_sem=send_sem.at[0],
            recv_sem=recv_sem.at[RECV_SEM.get((d, slot), RECV_UP)],
            device_id={AXES[d]: there},
            device_id_type=MESH,
        )

    forward = {d: link(d, 0, behind[d]) for d in FACES}
    backward = {d: link(d, 1, ahead[d]) for d in FACES}
    upward = {d: link(d, 2, behind[d]) for d in FACES}
    both = {d: link(d, 0, behind[d], 2) for d in (T_DIR, Z_DIR)}
    all_up = pltpu.make_async_copy(outbox.at[pl.ds(0, 15)], inbox.at[pl.ds(0, 15)], recv_sem.at[RECV_UP])
    all_sent = pltpu.make_async_copy(outbox, inbox, send_sem.at[0])

    def edge_link(d, src, dst):
        return pltpu.make_async_remote_copy(
            src_ref=src,
            dst_ref=dst,
            send_sem=send_sem.at[1],
            recv_sem=recv_sem.at[RECV_EDGE[d]],
            device_id={AXES[d]: behind[d], AXES[Y_DIR]: ahead[Y_DIR]},
            device_id_type=MESH,
        )

    edges = {
        T_DIR: edge_link(T_DIR, edge_out, edge_t),
        Z_DIR: edge_link(Z_DIR, face_of(outbox, Y_DIR, 1).at[:, 0:2], edge_z.at[:, 6:8]),
    }
    both_edges = edge_link(T_DIR, y_now.at[:, 0:6], y_now.at[:, 0:6])

    here = {T_DIR: here_sem.at[0], Z_DIR: here_sem.at[0], Y_DIR: here_sem.at[1]}
    here_near = here_sem.at[2]

    def say_here():
        def say(sem, there):
            pl.semaphore_signal(sem, inc=1, device_id=there, device_id_type=MESH)

        for d in FACES:
            pl.when(is_last[d])(functools.partial(say, here[d], {AXES[d]: ahead[d]}))
        there = {AXES[Y_DIR]: behind[Y_DIR]}
        pl.when(jnp.logical_not(is_first[Y_DIR]))(functools.partial(say, here_near, there))

        @pl.when(is_last_y)
        def _():
            pl.when(jnp.logical_not(is_first[Z_DIR]))(functools.partial(say, here_near, {AXES[Z_DIR]: behind[Z_DIR]}))
            greeted = jnp.logical_not(greeter)
            pl.when(greeted & jnp.logical_not(is_last[T_DIR]))(
                functools.partial(say, here_near, {AXES[T_DIR]: ahead[T_DIR]})
            )
            pl.when(greeted & jnp.logical_not(is_first[T_DIR]))(
                functools.partial(say, here_near, {AXES[T_DIR]: behind[T_DIR]})
            )

    m = masks(is_first[Y_DIR].astype(jnp.int32), is_last_y.astype(jnp.int32))
    last_t = jnp.where(me[T_DIR] == size[T_DIR] - 1, -1.0, 1.0).astype(jnp.float32)
    first_t = jnp.where(me[T_DIR] == 0, -1.0, 1.0).astype(jnp.float32)
    ahead_sign = {T_DIR: last_t, Z_DIR: None, Y_DIR: None}
    behind_sign = {T_DIR: first_t, Z_DIR: None, Y_DIR: None}

    first_load.wait()
    psi = [unpack(m, x_buf[3 * s:3 * s + 3, 0:8], x_buf[3 * s:3 * s + 3, 8:16]) for s in range(4)]
    minus = {}
    plus = {}
    u = {}
    back = {}

    def links(d):
        first, second = unpack(m, u_buf[9 * d:9 * d + 9, 0:8], u_buf[9 * d:9 * d + 9, 8:16])
        return first.reshape(3, 3, 8, 128), second.reshape(3, 3, 8, 128)

    def prepare_backward(d):
        u[d] = links(d)
        plus[d] = project(d, 1, psi)
        back[d] = adjoint_times(u[d], plus[d])
        stage_face(m, d, 1, back[d], face_of(outbox, d, 1))

    prepare_backward(Y_DIR)

    @pl.when(is_last_y)
    def _():
        pl.semaphore_wait(barrier, arrivals)
        edges[Z_DIR].start()
        spins = both_spins(face_of(outbox, Y_DIR, 1))
        edge_out[...] = pick(m["low"], spins[0], lane_roll(spins[1], 64))
        edges[T_DIR].start()
        backward[Y_DIR].start()
        say_here()

    for d in FACES:
        minus[d] = project(d, -1, psi)
        stage_face(m, d, 0, minus[d], face_of(outbox, d, 0))
    rest_load.wait()
    for d in (T_DIR, Z_DIR):
        prepare_backward(d)

    @pl.when(jnp.logical_not(is_last_y))
    def _():
        pl.semaphore_wait(barrier, arrivals)
        say_here()

    pl.when(is_last_y & (replies > 0))(lambda: pl.semaphore_wait(here_near, replies))
    for d in (T_DIR, Z_DIR):
        backward[d].start()
    for d in FACES:
        pl.when(jnp.logical_not(is_first[d]))(forward[d].start)

    @pl.when(is_first[T_DIR] | is_first[Z_DIR])
    def _():
        pl.semaphore_wait(here[T_DIR], is_first[T_DIR].astype(jnp.int32) + is_first[Z_DIR].astype(jnp.int32))
        for d in (T_DIR, Z_DIR):
            pl.when(is_first[d])(forward[d].start)

    @pl.when(jnp.logical_not(is_last_y))
    def _():
        pl.semaphore_wait(here_near, replies)
        backward[Y_DIR].start()

    zero = jnp.zeros((3, 8, 128), jnp.float32)
    hop = [(zero, zero)] * 4
    d = X_DIR
    u[d] = links(d)
    plus[d] = project(d, 1, psi)
    minus[d] = project(d, -1, psi)
    moved = {}
    moved[d] = link_times(u[d], shift_x(m, minus[d], 1))
    hop = add_spins(d, -1, hop, moved[d])
    hop = add_spins(d, 1, hop, shift_x(m, adjoint_times(u[d], plus[d]), -1))

    def take_backward(d, hop):
        there = shift_face(m, d, -1, back[d], face_of(inbox, d, 1), behind_sign[d])
        return add_spins(d, 1, hop, there)

    def take_forward(d, hop):
        there = shift_face(m, d, 1, minus[d], face_of(inbox, d, 0), ahead_sign[d])
        moved[d] = link_times(u[d], there)
        return add_spins(d, -1, hop, moved[d])

    def wilson(hop):
        return [(pr - KAPPA * hr, pi - KAPPA * hi) for (pr, pi), (hr, hi) in zip(psi, hop)]

    both[Z_DIR].wait_recv()
    hop = take_backward(Z_DIR, hop)
    hop = take_forward(Z_DIR, hop)
    forward[Y_DIR].wait_recv()
    hop = take_forward(Y_DIR, hop)
    hop = add_spins(Y_DIR, 1, hop, local_y(m, back[Y_DIR]))

    @pl.when(jnp.logical_not(is_first[Y_DIR]))
    def _():
        backward[Y_DIR].wait_recv()
        y_now[...] = face_of(inbox, Y_DIR, 1)[...]

    hop = add_spins(Y_DIR, 1, hop, face_y(m["halo_now"], both_spins(y_now)))

    inner = [tuple(lane_roll(v, 64) for v in parts) for parts in minus[T_DIR]]
    inner = add_spins(T_DIR, -1, hop, link_times(u[T_DIR], inner))
    stage_face(m, T_DIR, 0, project(T_DIR, 1, wilson(inner)), face_of(outbox, T_DIR, 2))
    upward[T_DIR].start()
    both[T_DIR].wait_recv()
    hop = take_backward(T_DIR, hop)
    hop = take_forward(T_DIR, hop)
    early = wilson(hop)
    for d in (Z_DIR, Y_DIR):
        stage_face(m, d, 0, project(d, 1, early), face_of(outbox, d, 2))
    upward[Z_DIR].start()
    pl.when(jnp.logical_not(is_first[Y_DIR]))(upward[Y_DIR].start)

    @pl.when(is_first[Y_DIR])
    def _():
        pl.semaphore_wait(here[Y_DIR], 1)
        forward[Y_DIR].start()
        upward[Y_DIR].start()
        backward[Y_DIR].wait_recv()

    late = face_y(m["halo_late"], both_spins(face_of(inbox, Y_DIR, 1)))
    missing = add_spins(Y_DIR, 1, [(zero, zero)] * 4, late)
    result = [
        (er - KAPPA * lr, ei - KAPPA * li) for (er, ei), (lr, li) in zip(early, missing)
    ]
    later = {d: project(d, 1, result) for d in FACES}
    for s, (re, im) in enumerate(result):
        y_buf[3 * s:3 * s + 3, 0:8] = pack_first(m, re, im)
        y_buf[3 * s:3 * s + 3, 8:16] = pack_second(m, re, im)

    def finish(d, first, later_there):
        write_force(m["low"], u[d], plus[d], first, later_there, f_buf, 9 * d)

    d = X_DIR
    finish(d, outer(moved[d], project(d, -1, result)), shift_x(m, project(d, 1, result), 1))
    first = {d: outer(moved[d], project(d, -1, result)) for d in FACES}
    all_up.wait()
    there = shift_face(m, Y_DIR, 1, later[Y_DIR], face_of(inbox, Y_DIR, 2), None)
    there = [
        (tr - 2 * KAPPA * only(m["own_y"], br), ti - 2 * KAPPA * only(m["own_y"], bi))
        for (tr, ti), (br, bi) in zip(there, back[Y_DIR])
    ]
    finish(Y_DIR, first[Y_DIR], there)
    z_buf[12:30] = jnp.concatenate([part.reshape(9, 8, 128) for part in u[Z_DIR]])
    z_buf[30:48] = jnp.concatenate([part.reshape(9, 8, 128) for part in first[Z_DIR]])
    z_buf[48:60] = jnp.concatenate([part for half in plus[Z_DIR] for part in half])
    edge_half = {
        T_DIR: lambda: face_y(m["edge_t"], [lane_roll(edge_t[...], 64), edge_t[...]]),
        Z_DIR: lambda: face_y(m["edge_z"], both_spins(edge_z)),
    }
    for d in (T_DIR, Z_DIR):
        there = shift_face(m, d, 1, later[d], face_of(inbox, d, 2), ahead_sign[d])
        if d == T_DIR:
            there = [
                (tr - 2 * KAPPA * pick(m["low"], zero, br), ti - 2 * KAPPA * pick(m["low"], zero, bi))
                for (tr, ti), (br, bi) in zip(there, back[T_DIR])
            ]
        pl.when(is_first[Y_DIR])(edges[d].wait_recv)
        scale = KAPPA * last_t if d == T_DIR else KAPPA
        extra = edge_term(d, edge_half[d]())
        there = [
            (tr - scale * er, ti - scale * ei) for (tr, ti), (er, ei) in zip(there, extra)
        ]
        if d == T_DIR:
            finish(d, first[d], there)
        else:
            for n, part in enumerate([part for half in there for part in half]):
                z_buf[3 * n:3 * n + 3] = part
    all_sent.wait()

    pl.when(is_last_y)(both_edges.wait_send)


def store_kernel(y_in, f_in, z_in, y_out, f_out, fz_buf, sems):
    def store(source, start, count):
        pltpu.make_async_copy(source, f_out.at[pl.ds(start, count)], sems.at[0]).start()

    store(f_in.at[pl.ds(0, 18)], 0, 18)
    store(f_in.at[pl.ds(27, 9)], 27, 9)
    y_store = pltpu.make_async_copy(y_in, y_out, sems.at[1])
    y_store.start()

    def halves(start):
        return [tuple(z_in[start + 6 * s + 3 * p:start + 6 * s + 3 * p + 3] for p in range(2)) for s in range(2)]

    def matrix(start):
        return tuple(z_in[start + 9 * p:start + 9 * p + 9].reshape(3, 3, 8, 128) for p in range(2))

    low = lax.broadcasted_iota(jnp.int32, (8, 128), 1) < 64
    write_force(low, matrix(12), halves(48), matrix(30), halves(0), fz_buf, 0)
    store(fz_buf, 18, 9)
    pltpu.make_async_copy(f_in, f_out, sems.at[0]).wait()
    y_store.wait()


def body(quark_field, gauge_links):
    x = quark_field.reshape(12, 16, 128)
    u = gauge_links.reshape(36, 16, 128)
    y, f, z = pl.pallas_call(
        kernel,
        out_shape=tuple(pltpu.VMEM(shape, jnp.float32) for shape in (x.shape, u.shape, (60, 8, 128))),
        in_specs=[pl.BlockSpec(memory_space=pltpu.HBM)] * 2,
        out_specs=(pl.BlockSpec(memory_space=pltpu.VMEM),) * 3,
        scratch_shapes=[
            pltpu.VMEM(x.shape, jnp.float32),
            pltpu.VMEM(u.shape, jnp.float32),
            pltpu.VMEM((ALL_TILES, 8, 128), jnp.float32),
            pltpu.VMEM((ALL_TILES, 8, 128), jnp.float32),
            pltpu.VMEM((6, 8, 128), jnp.float32),
            pltpu.VMEM((3, 8, 128), jnp.float32),
            pltpu.VMEM((3, 8, 128), jnp.float32),
            pltpu.VMEM((6, 8, 128), jnp.float32),
            pltpu.SemaphoreType.DMA((2,)),
            pltpu.SemaphoreType.DMA((2,)),
            pltpu.SemaphoreType.DMA((7,)),
            pltpu.SemaphoreType.REGULAR((3,)),
        ],
        compiler_params=pltpu.CompilerParams(collective_id=0, has_side_effects=True, vmem_limit_bytes=16 * 1024 * 1024),
        cost_estimate=pl.CostEstimate(flops=6_000_000, bytes_accessed=800_000, transcendentals=0),
    )(pltpu.with_memory_space_constraint(x, pltpu.HBM), pltpu.with_memory_space_constraint(u, pltpu.HBM))
    y, f = pl.pallas_call(
        store_kernel,
        out_shape=(
            jax.ShapeDtypeStruct(x.shape, jnp.float32),
            jax.ShapeDtypeStruct(u.shape, jnp.float32),
        ),
        in_specs=[pl.BlockSpec(memory_space=pltpu.VMEM)] * 3,
        out_specs=(pl.BlockSpec(memory_space=pl.ANY),) * 2,
        scratch_shapes=[pltpu.VMEM((9, 16, 128), jnp.float32), pltpu.SemaphoreType.DMA((2,))],
        compiler_params=pltpu.CompilerParams(vmem_limit_bytes=16 * 1024 * 1024),
        cost_estimate=pl.CostEstimate(flops=400_000, bytes_accessed=800_000, transcendentals=0),
    )(y, f, z)
    return y.reshape(quark_field.shape), f.reshape(gauge_links.shape)


def solution(mesh):
    specs = (
        P(None, None, "ta", "gz", "gy", None),
        P(None, None, None, "ta", "gz", "gy", None),
    )
    return jax.shard_map(body, mesh=mesh, in_specs=specs, out_specs=specs, check_vma=False)
```

```python
import functools

import jax
import jax.numpy as jnp
from jax import lax
from jax.experimental import pallas as pl
from jax.experimental.pallas import tpu as pltpu
from jax.sharding import PartitionSpec as P

KAPPA = 0.125
MESH = pl.DeviceIdType.MESH
X_DIR, Y_DIR, Z_DIR, T_DIR = 0, 1, 2, 3
AXES = {T_DIR: "ta", Z_DIR: "gz", Y_DIR: "gy"}
FACES = (T_DIR, Z_DIR, Y_DIR)
FACE_TILES = {T_DIR: 6, Z_DIR: 3, Y_DIR: 6}
FACE_START = {T_DIR: 0, Z_DIR: 18, Y_DIR: 27}
ALL_TILES = 45
RECV_SEM = {(T_DIR, 0): 0, (T_DIR, 1): 0, (Z_DIR, 0): 1, (Z_DIR, 1): 1, (Y_DIR, 0): 1, (Y_DIR, 1): 2}
RECV_UP, RECV_EDGE = 3, {T_DIR: 4, Z_DIR: 5}


def lane_roll(v, steps):
    return pltpu.roll(v.reshape(-1, 128), steps, 1).reshape(v.shape)


def row_roll(v, steps):
    if steps % 8 == 0:
        return v
    flat = v.reshape(-1, 8, 128)
    return jnp.stack([pltpu.roll(flat[i], steps % 8, 0) for i in range(flat.shape[0])]).reshape(v.shape)


def masks(at_start, at_end):
    lane = lax.broadcasted_iota(jnp.int32, (8, 128), 1)
    row = lax.broadcasted_iota(jnp.int32, (8, 128), 0)
    return {
        "low": lane < 64,
        "last_x": lane % 64 == 63,
        "first_x": lane % 64 == 0,
        "even": row % 2 == 0,
        "z_first": row < 2,
        "z_last": row >= 6,
        "row": row,
        "halo_now": row % 2 + at_start == 0,
        "halo_late": row % 2 + (1 - at_start) == 0,
        "own_y": row % 2 * at_end == 1,
        "edge_t": (row % 2 + (1 - at_start) == 0) & (lane >= 64),
        "edge_z": row + 8 * (1 - at_start) == 6,
    }


def pick(mask, a, b):
    return jnp.where(jnp.broadcast_to(mask, a.shape), a, b)


def unpack(m, first, second):
    return (
        pick(m["low"], first, lane_roll(second, 64)),
        pick(m["low"], lane_roll(first, 64), second),
    )


def pack_first(m, re, im):
    return pick(m["low"], re, lane_roll(im, 64))


def pack_second(m, re, im):
    return pick(m["low"], lane_roll(re, 64), im)


def c_add(a, b):
    return (a[0] + b[0], a[1] + b[1])


def c_sub(a, b):
    return (a[0] - b[0], a[1] - b[1])


def add_i(a, b):
    return (a[0] - b[1], a[1] + b[0])


def sub_i(a, b):
    return (a[0] + b[1], a[1] - b[0])


def project(direction, sign, psi):
    u0, u1, l0, l1 = psi
    plus, minus = (c_add, c_sub) if sign < 0 else (c_sub, c_add)
    plus_i, minus_i = (add_i, sub_i) if sign < 0 else (sub_i, add_i)
    if direction == X_DIR:
        return [plus_i(u0, l1), plus_i(u1, l0)]
    if direction == Y_DIR:
        return [plus(u0, l1), minus(u1, l0)]
    if direction == Z_DIR:
        return [plus_i(u0, l0), minus_i(u1, l1)]
    return [minus(u0, l0), minus(u1, l1)]


def add_spins(direction, sign, total, half):
    h0, h1 = half
    plus, minus = (c_sub, c_add) if sign < 0 else (c_add, c_sub)
    plus_i, minus_i = (sub_i, add_i) if sign < 0 else (add_i, sub_i)
    t0, t1, t2, t3 = total
    upper = [c_add(t0, h0), c_add(t1, h1)]
    if direction == X_DIR:
        return upper + [plus_i(t2, h1), plus_i(t3, h0)]
    if direction == Y_DIR:
        return upper + [plus(t2, h1), minus(t3, h0)]
    if direction == Z_DIR:
        return upper + [plus_i(t2, h0), minus_i(t3, h1)]
    return upper + [plus(t2, h0), plus(t3, h1)]


def link_times(u, half):
    ur, ui = u
    out = []
    for hr, hi in half:
        re = im = None
        for b in range(3):
            cr, ci = ur[:, b], ui[:, b]
            r = cr * hr[b][None] - ci * hi[b][None]
            i = cr * hi[b][None] + ci * hr[b][None]
            re = r if re is None else re + r
            im = i if im is None else im + i
        out.append((re, im))
    return out


def adjoint_times(u, half):
    ur, ui = u
    out = []
    for hr, hi in half:
        re = im = None
        for b in range(3):
            cr, ci = ur[b], ui[b]
            r = cr * hr[b][None] + ci * hi[b][None]
            i = cr * hi[b][None] - ci * hr[b][None]
            re = r if re is None else re + r
            im = i if im is None else im + i
        out.append((re, im))
    return out


def outer(left, right):
    re = im = None
    for (lr, li), (rr, ri) in zip(left, right):
        r = lr[:, None] * rr[None] + li[:, None] * ri[None]
        i = li[:, None] * rr[None] - lr[:, None] * ri[None]
        re = r if re is None else re + r
        im = i if im is None else im + i
    return re, im


def shift_x(m, half, steps):
    def one(v):
        if steps > 0:
            return pick(m["last_x"], lane_roll(v, 63), lane_roll(v, 127))
        return pick(m["first_x"], lane_roll(v, 65), lane_roll(v, 1))

    return [(one(re), one(im)) for re, im in half]


def stage_face(m, direction, end, half, ref):
    if direction == T_DIR:
        for s, (re, im) in enumerate(half):
            ref[3 * s:3 * s + 3] = (pack_second if end else pack_first)(m, re, im)
    elif direction == Y_DIR:
        for s, (re, im) in enumerate(half):
            if end:
                tile = pick(m["even"], row_roll(re, -1), im)
            else:
                tile = pick(m["even"], re, row_roll(im, 1))
            ref[3 * s:3 * s + 3] = tile
    else:
        tiles = [part[c] for re, im in half for part in (re, im) for c in range(3)]
        for j in range(3):
            tile = row_roll(tiles[4 * j], 2 if end else 0)
            for k in range(1, 4):
                moved = row_roll(tiles[4 * j + k], 2 * k + (2 if end else 0))
                tile = pick(m["row"] < 2 * k, tile, moved)
            ref[j] = tile


def shift_face(m, direction, steps, half, ref, sign):
    out = []
    if direction == T_DIR:
        for s, (re, im) in enumerate(half):
            face = ref[3 * s:3 * s + 3] * sign
            if steps > 0:
                out.append((
                    lane_roll(pick(m["low"], face, re), 64),
                    pick(m["low"], lane_roll(im, 64), face),
                ))
            else:
                out.append((
                    pick(m["low"], face, lane_roll(re, 64)),
                    lane_roll(pick(m["low"], im, face), 64),
                ))
    elif direction == Y_DIR:
        for s, (re, im) in enumerate(half):
            face = ref[3 * s:3 * s + 3]
            if steps > 0:
                out.append((
                    pick(m["even"], row_roll(re, -1), row_roll(face, 1)),
                    pick(m["even"], row_roll(im, -1), face),
                ))
            else:
                out.append((
                    pick(m["even"], face, row_roll(re, 1)),
                    pick(m["even"], row_roll(face, -1), row_roll(im, 1)),
                ))
    else:
        n = 0
        for re, im in half:
            parts = []
            for part in (re, im):
                moved = []
                for c in range(3):
                    face = ref[n // 4]
                    k = n % 4
                    n += 1
                    if steps > 0:
                        moved.append(row_roll(pick(m["z_first"], row_roll(face, -2 * k), part[c]), -2))
                    else:
                        moved.append(row_roll(pick(m["z_last"], row_roll(face, 6 - 2 * k), part[c]), 2))
                parts.append(jnp.stack(moved))
            out.append(tuple(parts))
    return out


def only(mask, v):
    return pick(mask, v, jnp.zeros_like(v))


def local_y(m, half):
    return [tuple(pick(m["even"], jnp.zeros_like(v), row_roll(v, 1)) for v in parts) for parts in half]


def face_y(mask, faces):
    return [(only(mask, face), only(mask, row_roll(face, -1))) for face in faces]


def both_spins(ref):
    return [ref[0:3], ref[3:6]]


def edge_term(direction, half):
    h0, h1 = half
    return project(direction, 1, [h0, h1, h1, (-h0[0], -h0[1])])


def write_force(low, u, plus, first, later_there, f_buf, start):
    second = outer(link_times(u, later_there), plus)
    wr, wi = c_add(first, second)
    third = (wi[0, 0] + wi[1, 1] + wi[2, 2]) / 3.0
    m = {"low": low}
    for a in range(3):
        for b in range(a, 3):
            if a == b:
                im = KAPPA * (wi[a, a] - third)
                re = jnp.zeros_like(im)
            else:
                re = (0.5 * KAPPA) * (wr[a, b] - wr[b, a])
                im = (0.5 * KAPPA) * (wi[a, b] + wi[b, a])
            top = pack_first(m, re, im)
            bottom = pack_second(m, re, im)
            f_buf[start + 3 * a + b, 0:8] = top
            f_buf[start + 3 * a + b, 8:16] = bottom
            if a != b:
                f_buf[start + 3 * b + a, 0:8] = pick(low, -top, top)
                f_buf[start + 3 * b + a, 8:16] = pick(low, -bottom, bottom)


def kernel(
    x_hbm, u_hbm, out_buf, z_buf,
    x_buf, u_buf,
    outbox, inbox, y_now, edge_out, edge_t, edge_z,
    load_sem, send_sem, recv_sem, here_sem,
):
    y_buf, f_buf = out_buf.at[pl.ds(0, 12)], out_buf.at[pl.ds(12, 36)]

    def face_of(box, d, slot, faces=1):
        return box.at[pl.ds(FACE_START[d] + slot * FACE_TILES[d], faces * FACE_TILES[d])]

    first_load = pltpu.make_async_copy(u_hbm.at[pl.ds(0, 21)], u_buf.at[pl.ds(0, 21)], load_sem.at[0])
    rest_load = pltpu.make_async_copy(u_hbm.at[pl.ds(0, 27)], u_buf.at[pl.ds(0, 27)], load_sem.at[1])

    def load(source, target, start, count, sem):
        part = pl.ds(start, count)
        pltpu.make_async_copy(source.at[part], target.at[part], load_sem.at[sem]).start()

    for s in range(3):
        load(x_hbm, x_buf, 4 * s, 4, 0)
    for a in range(3):
        load(u_hbm, u_buf, 9 * Y_DIR + 3 * a, 3, 0)
    me = {d: lax.axis_index(AXES[d]) for d in FACES}
    size = {d: lax.axis_size(AXES[d]) for d in FACES}
    ahead = {d: lax.rem(me[d] + 1, size[d]) for d in FACES}
    behind = {d: lax.rem(me[d] + size[d] - 1, size[d]) for d in FACES}

    barrier = pltpu.get_barrier_semaphore()
    is_first = {d: me[d] == 0 for d in FACES}
    is_last = {d: me[d] == size[d] - 1 for d in FACES}
    is_last_y = is_last[Y_DIR]

    def greet(where):
        pl.semaphore_signal(barrier, inc=1, device_id=where, device_id_type=MESH)

    odd = lax.rem(me[T_DIR], 2) == 1
    greeter = odd ^ (me[Z_DIR] < size[Z_DIR] // 2)
    plain = jnp.logical_not(is_last_y)
    pl.when(plain | greeter | is_first[T_DIR])(functools.partial(greet, {AXES[T_DIR]: behind[T_DIR]}))
    pl.when(plain | is_first[Z_DIR])(functools.partial(greet, {AXES[Z_DIR]: behind[Z_DIR]}))
    pl.when((plain | greeter) & jnp.logical_not(is_last[T_DIR]))(functools.partial(greet, {AXES[T_DIR]: ahead[T_DIR]}))
    for d in (Z_DIR, Y_DIR):
        pl.when(jnp.logical_not(is_last[d]))(functools.partial(greet, {AXES[d]: ahead[d]}))

    @pl.when(is_first[Y_DIR])
    def _():
        greet({AXES[Y_DIR]: behind[Y_DIR]})
        for d in (T_DIR, Z_DIR):
            greet({AXES[d]: ahead[d], AXES[Y_DIR]: behind[Y_DIR]})

    def one(flag):
        return flag.astype(jnp.int32)

    plain_arrivals = 5 - sum(one(is_first[d]) for d in FACES)
    late_t = jnp.where(greeter, one(odd & is_last[T_DIR]), 2 - one(is_first[T_DIR]))
    late_arrivals = late_t + 1 + one(is_last[Z_DIR]) - one(is_first[Z_DIR]) + 4
    late_replies = one(jnp.logical_not(is_last[Z_DIR])) + jnp.where(greeter, 2 - one(is_last[T_DIR]) - one(is_first[T_DIR]), 0)
    arrivals = jnp.where(is_last_y, late_arrivals, plain_arrivals)
    replies = jnp.where(is_last_y, late_replies, 1)
    for d in (T_DIR, Z_DIR, X_DIR):
        load(u_hbm, u_buf, 9 * d, 9, 1)

    def link(d, slot, there, faces=1):
        return pltpu.make_async_remote_copy(
            src_ref=face_of(outbox, d, slot, faces),
            dst_ref=face_of(inbox, d, slot, faces),
            send_sem=send_sem.at[0],
            recv_sem=recv_sem.at[RECV_SEM.get((d, slot), RECV_UP)],
            device_id={AXES[d]: there},
            device_id_type=MESH,
        )

    forward = {d: link(d, 0, behind[d]) for d in FACES}
    backward = {d: link(d, 1, ahead[d]) for d in FACES}
    upward = {d: link(d, 2, behind[d]) for d in FACES}
    both_t = link(T_DIR, 0, behind[T_DIR], 2)
    z_and_y = pltpu.make_async_copy(outbox.at[pl.ds(0, 12)], inbox.at[pl.ds(0, 12)], recv_sem.at[RECV_SEM[Z_DIR, 0]])
    all_up = pltpu.make_async_copy(outbox.at[pl.ds(0, 15)], inbox.at[pl.ds(0, 15)], recv_sem.at[RECV_UP])
    all_sent = pltpu.make_async_copy(outbox, inbox, send_sem.at[0])

    def edge_link(d, src, dst):
        return pltpu.make_async_remote_copy(
            src_ref=src,
            dst_ref=dst,
            send_sem=send_sem.at[1],
            recv_sem=recv_sem.at[RECV_EDGE[d]],
            device_id={AXES[d]: behind[d], AXES[Y_DIR]: ahead[Y_DIR]},
            device_id_type=MESH,
        )

    edges = {
        T_DIR: edge_link(T_DIR, edge_out, edge_t),
        Z_DIR: edge_link(Z_DIR, face_of(outbox, Y_DIR, 1).at[:, 0:2], edge_z.at[:, 6:8]),
    }
    both_edges = edge_link(T_DIR, y_now.at[:, 0:6], y_now.at[:, 0:6])

    here = {T_DIR: here_sem.at[0], Z_DIR: here_sem.at[0], Y_DIR: here_sem.at[1]}
    here_near = here_sem.at[2]

    def say_here():
        def say(sem, there):
            pl.semaphore_signal(sem, inc=1, device_id=there, device_id_type=MESH)

        for d in FACES:
            pl.when(is_last[d])(functools.partial(say, here[d], {AXES[d]: ahead[d]}))
        there = {AXES[Y_DIR]: behind[Y_DIR]}
        pl.when(jnp.logical_not(is_first[Y_DIR]))(functools.partial(say, here_near, there))

        @pl.when(is_last_y)
        def _():
            pl.when(jnp.logical_not(is_first[Z_DIR]))(functools.partial(say, here_near, {AXES[Z_DIR]: behind[Z_DIR]}))
            greeted = jnp.logical_not(greeter)
            pl.when(greeted & jnp.logical_not(is_last[T_DIR]))(
                functools.partial(say, here_near, {AXES[T_DIR]: ahead[T_DIR]})
            )
            pl.when(greeted & jnp.logical_not(is_first[T_DIR]))(
                functools.partial(say, here_near, {AXES[T_DIR]: behind[T_DIR]})
            )

    m = masks(is_first[Y_DIR].astype(jnp.int32), is_last_y.astype(jnp.int32))
    last_t = jnp.where(me[T_DIR] == size[T_DIR] - 1, -1.0, 1.0).astype(jnp.float32)
    first_t = jnp.where(me[T_DIR] == 0, -1.0, 1.0).astype(jnp.float32)
    ahead_sign = {T_DIR: last_t, Z_DIR: None, Y_DIR: None}
    behind_sign = {T_DIR: first_t, Z_DIR: None, Y_DIR: None}

    first_load.wait()
    psi = [unpack(m, x_buf[3 * s:3 * s + 3, 0:8], x_buf[3 * s:3 * s + 3, 8:16]) for s in range(4)]
    minus = {}
    plus = {}
    u = {}
    back = {}

    def links(d):
        first, second = unpack(m, u_buf[9 * d:9 * d + 9, 0:8], u_buf[9 * d:9 * d + 9, 8:16])
        return first.reshape(3, 3, 8, 128), second.reshape(3, 3, 8, 128)

    def prepare_backward(d):
        u[d] = links(d)
        plus[d] = project(d, 1, psi)
        back[d] = adjoint_times(u[d], plus[d])
        stage_face(m, d, 1, back[d], face_of(outbox, d, 1))

    prepare_backward(Y_DIR)

    @pl.when(is_last_y)
    def _():
        pl.semaphore_wait(barrier, arrivals)
        edges[Z_DIR].start()
        spins = both_spins(face_of(outbox, Y_DIR, 1))
        edge_out[...] = pick(m["low"], spins[0], lane_roll(spins[1], 64))
        edges[T_DIR].start()
        backward[Y_DIR].start()
        say_here()

    for d in FACES:
        minus[d] = project(d, -1, psi)
        stage_face(m, d, 0, minus[d], face_of(outbox, d, 0))
    rest_load.wait()
    for d in (T_DIR, Z_DIR):
        prepare_backward(d)

    @pl.when(jnp.logical_not(is_last_y))
    def _():
        pl.semaphore_wait(barrier, arrivals)
        say_here()

    pl.when(is_last_y & (replies > 0))(lambda: pl.semaphore_wait(here_near, replies))
    for d in (T_DIR, Z_DIR):
        backward[d].start()
    for d in FACES:
        pl.when(jnp.logical_not(is_first[d]))(forward[d].start)

    @pl.when(is_first[T_DIR] | is_first[Z_DIR])
    def _():
        pl.semaphore_wait(here[T_DIR], is_first[T_DIR].astype(jnp.int32) + is_first[Z_DIR].astype(jnp.int32))
        for d in (T_DIR, Z_DIR):
            pl.when(is_first[d])(forward[d].start)

    @pl.when(jnp.logical_not(is_last_y))
    def _():
        pl.semaphore_wait(here_near, replies)
        backward[Y_DIR].start()

    zero = jnp.zeros((3, 8, 128), jnp.float32)
    hop = [(zero, zero)] * 4
    d = X_DIR
    u[d] = links(d)
    plus[d] = project(d, 1, psi)
    minus[d] = project(d, -1, psi)
    moved = {}
    moved[d] = link_times(u[d], shift_x(m, minus[d], 1))
    hop = add_spins(d, -1, hop, moved[d])
    hop = add_spins(d, 1, hop, shift_x(m, adjoint_times(u[d], plus[d]), -1))

    def take_backward(d, hop):
        there = shift_face(m, d, -1, back[d], face_of(inbox, d, 1), behind_sign[d])
        return add_spins(d, 1, hop, there)

    def take_forward(d, hop):
        there = shift_face(m, d, 1, minus[d], face_of(inbox, d, 0), ahead_sign[d])
        moved[d] = link_times(u[d], there)
        return add_spins(d, -1, hop, moved[d])

    def wilson(hop):
        return [(pr - KAPPA * hr, pi - KAPPA * hi) for (pr, pi), (hr, hi) in zip(psi, hop)]

    z_and_y.wait()
    hop = take_backward(Z_DIR, hop)
    hop = take_forward(Z_DIR, hop)
    hop = take_forward(Y_DIR, hop)
    hop = add_spins(Y_DIR, 1, hop, local_y(m, back[Y_DIR]))

    @pl.when(jnp.logical_not(is_first[Y_DIR]))
    def _():
        backward[Y_DIR].wait_recv()
        y_now[...] = face_of(inbox, Y_DIR, 1)[...]

    hop = add_spins(Y_DIR, 1, hop, face_y(m["halo_now"], both_spins(y_now)))

    inner = [tuple(lane_roll(v, 64) for v in parts) for parts in minus[T_DIR]]
    inner = add_spins(T_DIR, -1, hop, link_times(u[T_DIR], inner))
    stage_face(m, T_DIR, 0, project(T_DIR, 1, wilson(inner)), face_of(outbox, T_DIR, 2))
    upward[T_DIR].start()
    both_t.wait_recv()
    hop = take_backward(T_DIR, hop)
    hop = take_forward(T_DIR, hop)
    early = wilson(hop)
    for d in (Z_DIR, Y_DIR):
        stage_face(m, d, 0, project(d, 1, early), face_of(outbox, d, 2))
    upward[Z_DIR].start()
    pl.when(jnp.logical_not(is_first[Y_DIR]))(upward[Y_DIR].start)

    @pl.when(is_first[Y_DIR])
    def _():
        pl.semaphore_wait(here[Y_DIR], 1)
        forward[Y_DIR].start()
        upward[Y_DIR].start()
        backward[Y_DIR].wait_recv()

    late = face_y(m["halo_late"], both_spins(face_of(inbox, Y_DIR, 1)))
    missing = add_spins(Y_DIR, 1, [(zero, zero)] * 4, late)
    result = [
        (er - KAPPA * lr, ei - KAPPA * li) for (er, ei), (lr, li) in zip(early, missing)
    ]
    later = {d: project(d, 1, result) for d in FACES}
    for s, (re, im) in enumerate(result):
        y_buf[3 * s:3 * s + 3, 0:8] = pack_first(m, re, im)
        y_buf[3 * s:3 * s + 3, 8:16] = pack_second(m, re, im)

    def finish(d, first, later_there):
        write_force(m["low"], u[d], plus[d], first, later_there, f_buf, 9 * d)

    d = X_DIR
    finish(d, outer(moved[d], project(d, -1, result)), shift_x(m, project(d, 1, result), 1))
    first = {d: outer(moved[d], project(d, -1, result)) for d in FACES}
    all_up.wait()
    there = shift_face(m, Y_DIR, 1, later[Y_DIR], face_of(inbox, Y_DIR, 2), None)
    there = [
        (tr - 2 * KAPPA * only(m["own_y"], br), ti - 2 * KAPPA * only(m["own_y"], bi))
        for (tr, ti), (br, bi) in zip(there, back[Y_DIR])
    ]
    finish(Y_DIR, first[Y_DIR], there)
    z_buf[12:30] = jnp.concatenate([part.reshape(9, 8, 128) for part in u[Z_DIR]])
    z_buf[30:48] = jnp.concatenate([part.reshape(9, 8, 128) for part in first[Z_DIR]])
    z_buf[48:60] = jnp.concatenate([part for half in plus[Z_DIR] for part in half])
    edge_half = {
        T_DIR: lambda: face_y(m["edge_t"], [lane_roll(edge_t[...], 64), edge_t[...]]),
        Z_DIR: lambda: face_y(m["edge_z"], both_spins(edge_z)),
    }
    for d in (T_DIR, Z_DIR):
        there = shift_face(m, d, 1, later[d], face_of(inbox, d, 2), ahead_sign[d])
        if d == T_DIR:
            there = [
                (tr - 2 * KAPPA * pick(m["low"], zero, br), ti - 2 * KAPPA * pick(m["low"], zero, bi))
                for (tr, ti), (br, bi) in zip(there, back[T_DIR])
            ]
        pl.when(is_first[Y_DIR])(edges[d].wait_recv)
        scale = KAPPA * last_t if d == T_DIR else KAPPA
        extra = edge_term(d, edge_half[d]())
        there = [
            (tr - scale * er, ti - scale * ei) for (tr, ti), (er, ei) in zip(there, extra)
        ]
        if d == T_DIR:
            finish(d, first[d], there)
        else:
            for n, part in enumerate([part for half in there for part in half]):
                z_buf[3 * n:3 * n + 3] = part
    all_sent.wait()

    pl.when(is_last_y)(both_edges.wait_send)


def store_kernel(out_in, z_in, y_out, f_out, fz_buf, sem):
    def store(source, target):
        pltpu.make_async_copy(source, target, sem).start()

    store(out_in.at[pl.ds(12, 18)], f_out.at[pl.ds(0, 18)])
    store(out_in.at[pl.ds(39, 9)], f_out.at[pl.ds(27, 9)])
    store(out_in.at[pl.ds(0, 12)], y_out)

    def halves(start):
        return [tuple(z_in[start + 6 * s + 3 * p:start + 6 * s + 3 * p + 3] for p in range(2)) for s in range(2)]

    def matrix(start):
        return tuple(z_in[start + 9 * p:start + 9 * p + 9].reshape(3, 3, 8, 128) for p in range(2))

    low = lax.broadcasted_iota(jnp.int32, (8, 128), 1) < 64
    write_force(low, matrix(12), halves(48), matrix(30), halves(0), fz_buf, 0)
    store(fz_buf, f_out.at[pl.ds(18, 9)])
    pltpu.make_async_copy(out_in, out_in, sem).wait()


def body(quark_field, gauge_links):
    x = quark_field.reshape(12, 16, 128)
    u = gauge_links.reshape(36, 16, 128)
    out, z = pl.pallas_call(
        kernel,
        out_shape=tuple(pltpu.VMEM(shape, jnp.float32) for shape in ((48, 16, 128), (60, 8, 128))),
        in_specs=[pl.BlockSpec(memory_space=pltpu.HBM)] * 2,
        out_specs=(pl.BlockSpec(memory_space=pltpu.VMEM),) * 2,
        scratch_shapes=[
            pltpu.VMEM(x.shape, jnp.float32),
            pltpu.VMEM(u.shape, jnp.float32),
            pltpu.VMEM((ALL_TILES, 8, 128), jnp.float32),
            pltpu.VMEM((ALL_TILES, 8, 128), jnp.float32),
            pltpu.VMEM((6, 8, 128), jnp.float32),
            pltpu.VMEM((3, 8, 128), jnp.float32),
            pltpu.VMEM((3, 8, 128), jnp.float32),
            pltpu.VMEM((6, 8, 128), jnp.float32),
            pltpu.SemaphoreType.DMA((2,)),
            pltpu.SemaphoreType.DMA((2,)),
            pltpu.SemaphoreType.DMA((6,)),
            pltpu.SemaphoreType.REGULAR((3,)),
        ],
        compiler_params=pltpu.CompilerParams(collective_id=0, has_side_effects=True, vmem_limit_bytes=16 * 1024 * 1024),
        cost_estimate=pl.CostEstimate(flops=6_000_000, bytes_accessed=800_000, transcendentals=0),
    )(pltpu.with_memory_space_constraint(x, pltpu.HBM), pltpu.with_memory_space_constraint(u, pltpu.HBM))
    y, f = pl.pallas_call(
        store_kernel,
        out_shape=(
            jax.ShapeDtypeStruct(x.shape, jnp.float32),
            jax.ShapeDtypeStruct(u.shape, jnp.float32),
        ),
        in_specs=[pl.BlockSpec(memory_space=pltpu.VMEM)] * 2,
        out_specs=(pl.BlockSpec(memory_space=pl.ANY),) * 2,
        scratch_shapes=[pltpu.VMEM((9, 16, 128), jnp.float32), pltpu.SemaphoreType.DMA],
        compiler_params=pltpu.CompilerParams(vmem_limit_bytes=16 * 1024 * 1024),
        cost_estimate=pl.CostEstimate(flops=400_000, bytes_accessed=800_000, transcendentals=0),
    )(out, z)
    return y.reshape(quark_field.shape), f.reshape(gauge_links.shape)


def solution(mesh):
    specs = (
        P(None, None, "ta", "gz", "gy", None),
        P(None, None, None, "ta", "gz", "gy", None),
    )
    return jax.shard_map(body, mesh=mesh, in_specs=specs, out_specs=specs, check_vma=False)
```

```python
import functools

import jax
import jax.numpy as jnp
from jax import lax
from jax.experimental import pallas as pl
from jax.experimental.pallas import tpu as pltpu
from jax.sharding import PartitionSpec as P

KAPPA = 0.125
MESH = pl.DeviceIdType.MESH
X_DIR, Y_DIR, Z_DIR, T_DIR = 0, 1, 2, 3
AXES = {T_DIR: "ta", Z_DIR: "gz", Y_DIR: "gy"}
FACES = (T_DIR, Z_DIR, Y_DIR)
FACE_TILES = {T_DIR: 6, Z_DIR: 3, Y_DIR: 6}
FACE_START = {T_DIR: 0, Z_DIR: 18, Y_DIR: 27}
ALL_TILES = 45
RECV_SEM = {(T_DIR, 0): 0, (T_DIR, 1): 0, (Z_DIR, 0): 1, (Z_DIR, 1): 1, (Y_DIR, 0): 1, (Y_DIR, 1): 2}
RECV_UP, RECV_EDGE = 3, {T_DIR: 4, Z_DIR: 5}


def lane_roll(v, steps):
    return pltpu.roll(v.reshape(-1, 128), steps, 1).reshape(v.shape)


def row_roll(v, steps):
    if steps % 8 == 0:
        return v
    flat = v.reshape(-1, 8, 128)
    return jnp.stack([pltpu.roll(flat[i], steps % 8, 0) for i in range(flat.shape[0])]).reshape(v.shape)


def masks(at_start, at_end):
    lane = lax.broadcasted_iota(jnp.int32, (8, 128), 1)
    row = lax.broadcasted_iota(jnp.int32, (8, 128), 0)
    return {
        "low": lane < 64,
        "last_x": lane % 64 == 63,
        "first_x": lane % 64 == 0,
        "even": row % 2 == 0,
        "z_first": row < 2,
        "z_last": row >= 6,
        "row": row,
        "halo_now": row % 2 + at_start == 0,
        "halo_late": row % 2 + (1 - at_start) == 0,
        "own_y": row % 2 * at_end == 1,
        "edge_t": (row % 2 + (1 - at_start) == 0) & (lane >= 64),
        "edge_z": row + 8 * (1 - at_start) == 6,
    }


def pick(mask, a, b):
    return jnp.where(jnp.broadcast_to(mask, a.shape), a, b)


def unpack(m, first, second):
    return (
        pick(m["low"], first, lane_roll(second, 64)),
        pick(m["low"], lane_roll(first, 64), second),
    )


def pack_first(m, re, im):
    return pick(m["low"], re, lane_roll(im, 64))


def pack_second(m, re, im):
    return pick(m["low"], lane_roll(re, 64), im)


def c_add(a, b):
    return (a[0] + b[0], a[1] + b[1])


def c_sub(a, b):
    return (a[0] - b[0], a[1] - b[1])


def add_i(a, b):
    return (a[0] - b[1], a[1] + b[0])


def sub_i(a, b):
    return (a[0] + b[1], a[1] - b[0])


def project(direction, sign, psi):
    u0, u1, l0, l1 = psi
    plus, minus = (c_add, c_sub) if sign < 0 else (c_sub, c_add)
    plus_i, minus_i = (add_i, sub_i) if sign < 0 else (sub_i, add_i)
    if direction == X_DIR:
        return [plus_i(u0, l1), plus_i(u1, l0)]
    if direction == Y_DIR:
        return [plus(u0, l1), minus(u1, l0)]
    if direction == Z_DIR:
        return [plus_i(u0, l0), minus_i(u1, l1)]
    return [minus(u0, l0), minus(u1, l1)]


def add_spins(direction, sign, total, half):
    h0, h1 = half
    plus, minus = (c_sub, c_add) if sign < 0 else (c_add, c_sub)
    plus_i, minus_i = (sub_i, add_i) if sign < 0 else (add_i, sub_i)
    t0, t1, t2, t3 = total
    upper = [c_add(t0, h0), c_add(t1, h1)]
    if direction == X_DIR:
        return upper + [plus_i(t2, h1), plus_i(t3, h0)]
    if direction == Y_DIR:
        return upper + [plus(t2, h1), minus(t3, h0)]
    if direction == Z_DIR:
        return upper + [plus_i(t2, h0), minus_i(t3, h1)]
    return upper + [plus(t2, h0), plus(t3, h1)]


def link_times(u, half):
    ur, ui = u
    out = []
    for hr, hi in half:
        re = im = None
        for b in range(3):
            cr, ci = ur[:, b], ui[:, b]
            r = cr * hr[b][None] - ci * hi[b][None]
            i = cr * hi[b][None] + ci * hr[b][None]
            re = r if re is None else re + r
            im = i if im is None else im + i
        out.append((re, im))
    return out


def adjoint_times(u, half):
    ur, ui = u
    out = []
    for hr, hi in half:
        re = im = None
        for b in range(3):
            cr, ci = ur[b], ui[b]
            r = cr * hr[b][None] + ci * hi[b][None]
            i = cr * hi[b][None] - ci * hr[b][None]
            re = r if re is None else re + r
            im = i if im is None else im + i
        out.append((re, im))
    return out


def outer(left, right):
    re = im = None
    for (lr, li), (rr, ri) in zip(left, right):
        r = lr[:, None] * rr[None] + li[:, None] * ri[None]
        i = li[:, None] * rr[None] - lr[:, None] * ri[None]
        re = r if re is None else re + r
        im = i if im is None else im + i
    return re, im


def shift_x(m, half, steps):
    def one(v):
        if steps > 0:
            return pick(m["last_x"], lane_roll(v, 63), lane_roll(v, 127))
        return pick(m["first_x"], lane_roll(v, 65), lane_roll(v, 1))

    return [(one(re), one(im)) for re, im in half]


def stage_face(m, direction, end, half, ref):
    if direction == T_DIR:
        for s, (re, im) in enumerate(half):
            ref[3 * s:3 * s + 3] = (pack_second if end else pack_first)(m, re, im)
    elif direction == Y_DIR:
        for s, (re, im) in enumerate(half):
            if end:
                tile = pick(m["even"], row_roll(re, -1), im)
            else:
                tile = pick(m["even"], re, row_roll(im, 1))
            ref[3 * s:3 * s + 3] = tile
    else:
        tiles = [part[c] for re, im in half for part in (re, im) for c in range(3)]
        for j in range(3):
            tile = row_roll(tiles[4 * j], 2 if end else 0)
            for k in range(1, 4):
                moved = row_roll(tiles[4 * j + k], 2 * k + (2 if end else 0))
                tile = pick(m["row"] < 2 * k, tile, moved)
            ref[j] = tile


def shift_face(m, direction, steps, half, ref, sign):
    out = []
    if direction == T_DIR:
        for s, (re, im) in enumerate(half):
            face = ref[3 * s:3 * s + 3] * sign
            if steps > 0:
                out.append((
                    lane_roll(pick(m["low"], face, re), 64),
                    pick(m["low"], lane_roll(im, 64), face),
                ))
            else:
                out.append((
                    pick(m["low"], face, lane_roll(re, 64)),
                    lane_roll(pick(m["low"], im, face), 64),
                ))
    elif direction == Y_DIR:
        for s, (re, im) in enumerate(half):
            face = ref[3 * s:3 * s + 3]
            if steps > 0:
                out.append((
                    pick(m["even"], row_roll(re, -1), row_roll(face, 1)),
                    pick(m["even"], row_roll(im, -1), face),
                ))
            else:
                out.append((
                    pick(m["even"], face, row_roll(re, 1)),
                    pick(m["even"], row_roll(face, -1), row_roll(im, 1)),
                ))
    else:
        n = 0
        for re, im in half:
            parts = []
            for part in (re, im):
                moved = []
                for c in range(3):
                    face = ref[n // 4]
                    k = n % 4
                    n += 1
                    if steps > 0:
                        moved.append(row_roll(pick(m["z_first"], row_roll(face, -2 * k), part[c]), -2))
                    else:
                        moved.append(row_roll(pick(m["z_last"], row_roll(face, 6 - 2 * k), part[c]), 2))
                parts.append(jnp.stack(moved))
            out.append(tuple(parts))
    return out


def only(mask, v):
    return pick(mask, v, jnp.zeros_like(v))


def local_y(m, half):
    return [tuple(pick(m["even"], jnp.zeros_like(v), row_roll(v, 1)) for v in parts) for parts in half]


def face_y(mask, faces):
    return [(only(mask, face), only(mask, row_roll(face, -1))) for face in faces]


def both_spins(ref):
    return [ref[0:3], ref[3:6]]


def edge_term(direction, half):
    h0, h1 = half
    return project(direction, 1, [h0, h1, h1, (-h0[0], -h0[1])])


def write_force(low, u, plus, first, later_there, f_buf, start):
    second = outer(link_times(u, later_there), plus)
    wr, wi = c_add(first, second)
    third = (wi[0, 0] + wi[1, 1] + wi[2, 2]) / 3.0
    m = {"low": low}
    for a in range(3):
        for b in range(a, 3):
            if a == b:
                im = KAPPA * (wi[a, a] - third)
                re = jnp.zeros_like(im)
            else:
                re = (0.5 * KAPPA) * (wr[a, b] - wr[b, a])
                im = (0.5 * KAPPA) * (wi[a, b] + wi[b, a])
            top = pack_first(m, re, im)
            bottom = pack_second(m, re, im)
            f_buf[start + 3 * a + b, 0:8] = top
            f_buf[start + 3 * a + b, 8:16] = bottom
            if a != b:
                f_buf[start + 3 * b + a, 0:8] = pick(low, -top, top)
                f_buf[start + 3 * b + a, 8:16] = pick(low, -bottom, bottom)


def kernel(
    x_hbm, u_hbm, out_buf, z_buf,
    x_buf, u_buf,
    outbox, inbox, y_now, edge_out, edge_t, edge_z,
    load_sem, send_sem, recv_sem, here_sem,
):
    y_buf, f_buf = out_buf.at[pl.ds(0, 12)], out_buf.at[pl.ds(12, 36)]

    def face_of(box, d, slot, faces=1):
        return box.at[pl.ds(FACE_START[d] + slot * FACE_TILES[d], faces * FACE_TILES[d])]

    first_load = pltpu.make_async_copy(u_hbm.at[pl.ds(0, 21)], u_buf.at[pl.ds(0, 21)], load_sem.at[0])
    rest_load = pltpu.make_async_copy(u_hbm.at[pl.ds(0, 27)], u_buf.at[pl.ds(0, 27)], load_sem.at[1])

    def load(source, target, start, count, sem):
        part = pl.ds(start, count)
        pltpu.make_async_copy(source.at[part], target.at[part], load_sem.at[sem]).start()

    for s in range(3):
        load(x_hbm, x_buf, 4 * s, 4, 0)
    for a in range(3):
        load(u_hbm, u_buf, 9 * Y_DIR + 3 * a, 3, 0)
    me = {d: lax.axis_index(AXES[d]) for d in FACES}
    size = {d: lax.axis_size(AXES[d]) for d in FACES}
    ahead = {d: lax.rem(me[d] + 1, size[d]) for d in FACES}
    behind = {d: lax.rem(me[d] + size[d] - 1, size[d]) for d in FACES}

    barrier = pltpu.get_barrier_semaphore()
    is_first = {d: me[d] == 0 for d in FACES}
    is_last = {d: me[d] == size[d] - 1 for d in FACES}
    is_last_y = is_last[Y_DIR]

    def greet(where):
        pl.semaphore_signal(barrier, inc=1, device_id=where, device_id_type=MESH)

    odd = lax.rem(me[T_DIR], 2) == 1
    greeter = odd ^ (me[Z_DIR] < size[Z_DIR] // 2)
    plain = jnp.logical_not(is_last_y)
    pl.when(plain | greeter | is_first[T_DIR])(functools.partial(greet, {AXES[T_DIR]: behind[T_DIR]}))
    pl.when(plain | is_first[Z_DIR])(functools.partial(greet, {AXES[Z_DIR]: behind[Z_DIR]}))
    pl.when((plain | greeter) & jnp.logical_not(is_last[T_DIR]))(functools.partial(greet, {AXES[T_DIR]: ahead[T_DIR]}))
    for d in (Z_DIR, Y_DIR):
        pl.when(jnp.logical_not(is_last[d]))(functools.partial(greet, {AXES[d]: ahead[d]}))

    @pl.when(is_first[Y_DIR])
    def _():
        greet({AXES[Y_DIR]: behind[Y_DIR]})
        for d in (T_DIR, Z_DIR):
            greet({AXES[d]: ahead[d], AXES[Y_DIR]: behind[Y_DIR]})

    def one(flag):
        return flag.astype(jnp.int32)

    plain_arrivals = 5 - sum(one(is_first[d]) for d in FACES)
    late_t = jnp.where(greeter, one(odd & is_last[T_DIR]), 2 - one(is_first[T_DIR]))
    late_arrivals = late_t + 1 + one(is_last[Z_DIR]) - one(is_first[Z_DIR]) + 4
    late_replies = one(jnp.logical_not(is_last[Z_DIR])) + jnp.where(greeter, 2 - one(is_last[T_DIR]) - one(is_first[T_DIR]), 0)
    arrivals = jnp.where(is_last_y, late_arrivals, plain_arrivals)
    replies = jnp.where(is_last_y, late_replies, 1)
    for d in (T_DIR, Z_DIR, X_DIR):
        load(u_hbm, u_buf, 9 * d, 9, 1)

    def link(d, slot, there, faces=1):
        return pltpu.make_async_remote_copy(
            src_ref=face_of(outbox, d, slot, faces),
            dst_ref=face_of(inbox, d, slot, faces),
            send_sem=send_sem.at[0],
            recv_sem=recv_sem.at[RECV_SEM.get((d, slot), RECV_UP)],
            device_id={AXES[d]: there},
            device_id_type=MESH,
        )

    forward = {d: link(d, 0, behind[d]) for d in FACES}
    backward = {d: link(d, 1, ahead[d]) for d in FACES}
    upward = {d: link(d, 2, behind[d]) for d in FACES}
    both_t = link(T_DIR, 0, behind[T_DIR], 2)
    z_and_y = pltpu.make_async_copy(outbox.at[pl.ds(0, 12)], inbox.at[pl.ds(0, 12)], recv_sem.at[RECV_SEM[Z_DIR, 0]])
    all_up = pltpu.make_async_copy(outbox.at[pl.ds(0, 15)], inbox.at[pl.ds(0, 15)], recv_sem.at[RECV_UP])
    all_sent = pltpu.make_async_copy(outbox, inbox, send_sem.at[0])

    def edge_link(d, src, dst):
        return pltpu.make_async_remote_copy(
            src_ref=src,
            dst_ref=dst,
            send_sem=send_sem.at[1],
            recv_sem=recv_sem.at[RECV_EDGE[d]],
            device_id={AXES[d]: behind[d], AXES[Y_DIR]: ahead[Y_DIR]},
            device_id_type=MESH,
        )

    edges = {
        T_DIR: edge_link(T_DIR, edge_out, edge_t),
        Z_DIR: edge_link(Z_DIR, face_of(outbox, Y_DIR, 1).at[:, 0:2], edge_z.at[:, 6:8]),
    }
    both_edges = edge_link(T_DIR, y_now.at[:, 0:6], y_now.at[:, 0:6])

    here = {T_DIR: here_sem.at[0], Z_DIR: here_sem.at[0], Y_DIR: here_sem.at[1]}
    here_near = here_sem.at[2]

    def say_here():
        def say(sem, there):
            pl.semaphore_signal(sem, inc=1, device_id=there, device_id_type=MESH)

        for d in FACES:
            pl.when(is_last[d])(functools.partial(say, here[d], {AXES[d]: ahead[d]}))
        there = {AXES[Y_DIR]: behind[Y_DIR]}
        pl.when(jnp.logical_not(is_first[Y_DIR]))(functools.partial(say, here_near, there))

        @pl.when(is_last_y)
        def _():
            pl.when(jnp.logical_not(is_first[Z_DIR]))(functools.partial(say, here_near, {AXES[Z_DIR]: behind[Z_DIR]}))
            greeted = jnp.logical_not(greeter)
            pl.when(greeted & jnp.logical_not(is_last[T_DIR]))(
                functools.partial(say, here_near, {AXES[T_DIR]: ahead[T_DIR]})
            )
            pl.when(greeted & jnp.logical_not(is_first[T_DIR]))(
                functools.partial(say, here_near, {AXES[T_DIR]: behind[T_DIR]})
            )

    m = masks(is_first[Y_DIR].astype(jnp.int32), is_last_y.astype(jnp.int32))
    last_t = jnp.where(me[T_DIR] == size[T_DIR] - 1, -1.0, 1.0).astype(jnp.float32)
    first_t = jnp.where(me[T_DIR] == 0, -1.0, 1.0).astype(jnp.float32)
    ahead_sign = {T_DIR: last_t, Z_DIR: None, Y_DIR: None}
    behind_sign = {T_DIR: first_t, Z_DIR: None, Y_DIR: None}

    first_load.wait()
    psi = [unpack(m, x_buf[3 * s:3 * s + 3, 0:8], x_buf[3 * s:3 * s + 3, 8:16]) for s in range(4)]
    minus = {}
    plus = {}
    u = {}
    back = {}

    def links(d):
        first, second = unpack(m, u_buf[9 * d:9 * d + 9, 0:8], u_buf[9 * d:9 * d + 9, 8:16])
        return first.reshape(3, 3, 8, 128), second.reshape(3, 3, 8, 128)

    def prepare_backward(d):
        u[d] = links(d)
        plus[d] = project(d, 1, psi)
        back[d] = adjoint_times(u[d], plus[d])
        stage_face(m, d, 1, back[d], face_of(outbox, d, 1))

    prepare_backward(Y_DIR)

    @pl.when(is_last_y)
    def _():
        pl.semaphore_wait(barrier, arrivals)
        edges[Z_DIR].start()
        spins = both_spins(face_of(outbox, Y_DIR, 1))
        edge_out[...] = pick(m["low"], spins[0], lane_roll(spins[1], 64))
        edges[T_DIR].start()
        backward[Y_DIR].start()
        say_here()

    for d in FACES:
        minus[d] = project(d, -1, psi)
        stage_face(m, d, 0, minus[d], face_of(outbox, d, 0))
    rest_load.wait()
    for d in (T_DIR, Z_DIR):
        prepare_backward(d)

    @pl.when(jnp.logical_not(is_last_y))
    def _():
        pl.semaphore_wait(barrier, arrivals)
        say_here()

    pl.when(is_last_y & (replies > 0))(lambda: pl.semaphore_wait(here_near, replies))
    for d in (T_DIR, Z_DIR):
        backward[d].start()
    for d in FACES:
        pl.when(jnp.logical_not(is_first[d]))(forward[d].start)

    @pl.when(is_first[T_DIR] | is_first[Z_DIR])
    def _():
        pl.semaphore_wait(here[T_DIR], is_first[T_DIR].astype(jnp.int32) + is_first[Z_DIR].astype(jnp.int32))
        for d in (T_DIR, Z_DIR):
            pl.when(is_first[d])(forward[d].start)

    @pl.when(jnp.logical_not(is_last_y))
    def _():
        pl.semaphore_wait(here_near, replies)
        backward[Y_DIR].start()

    zero = jnp.zeros((3, 8, 128), jnp.float32)
    hop = [(zero, zero)] * 4
    d = X_DIR
    u[d] = links(d)
    plus[d] = project(d, 1, psi)
    minus[d] = project(d, -1, psi)
    moved = {}
    moved[d] = link_times(u[d], shift_x(m, minus[d], 1))
    hop = add_spins(d, -1, hop, moved[d])
    hop = add_spins(d, 1, hop, shift_x(m, adjoint_times(u[d], plus[d]), -1))

    def take_backward(d, hop):
        there = shift_face(m, d, -1, back[d], face_of(inbox, d, 1), behind_sign[d])
        return add_spins(d, 1, hop, there)

    def take_forward(d, hop):
        there = shift_face(m, d, 1, minus[d], face_of(inbox, d, 0), ahead_sign[d])
        moved[d] = link_times(u[d], there)
        return add_spins(d, -1, hop, moved[d])

    def wilson(hop):
        return [(pr - KAPPA * hr, pi - KAPPA * hi) for (pr, pi), (hr, hi) in zip(psi, hop)]

    z_and_y.wait()
    hop = take_backward(Z_DIR, hop)
    hop = take_forward(Z_DIR, hop)
    hop = take_forward(Y_DIR, hop)
    hop = add_spins(Y_DIR, 1, hop, local_y(m, back[Y_DIR]))

    @pl.when(jnp.logical_not(is_first[Y_DIR]))
    def _():
        backward[Y_DIR].wait_recv()
        y_now[...] = face_of(inbox, Y_DIR, 1)[...]

    hop = add_spins(Y_DIR, 1, hop, face_y(m["halo_now"], both_spins(y_now)))

    inner = [tuple(lane_roll(v, 64) for v in parts) for parts in minus[T_DIR]]
    inner = add_spins(T_DIR, -1, hop, link_times(u[T_DIR], inner))
    stage_face(m, T_DIR, 0, project(T_DIR, 1, wilson(inner)), face_of(outbox, T_DIR, 2))
    upward[T_DIR].start()
    both_t.wait_recv()
    hop = take_backward(T_DIR, hop)
    hop = take_forward(T_DIR, hop)
    early = wilson(hop)
    for d in (Z_DIR, Y_DIR):
        stage_face(m, d, 0, project(d, 1, early), face_of(outbox, d, 2))
    upward[Z_DIR].start()
    pl.when(jnp.logical_not(is_first[Y_DIR]))(upward[Y_DIR].start)

    @pl.when(is_first[Y_DIR])
    def _():
        pl.semaphore_wait(here[Y_DIR], 1)
        forward[Y_DIR].start()
        upward[Y_DIR].start()
        backward[Y_DIR].wait_recv()

    late = face_y(m["halo_late"], both_spins(face_of(inbox, Y_DIR, 1)))
    missing = add_spins(Y_DIR, 1, [(zero, zero)] * 4, late)
    result = [
        (er - KAPPA * lr, ei - KAPPA * li) for (er, ei), (lr, li) in zip(early, missing)
    ]
    later = {d: project(d, 1, result) for d in FACES}
    for s, (re, im) in enumerate(result):
        y_buf[3 * s:3 * s + 3, 0:8] = pack_first(m, re, im)
        y_buf[3 * s:3 * s + 3, 8:16] = pack_second(m, re, im)

    def finish(d, first, later_there):
        write_force(m["low"], u[d], plus[d], first, later_there, f_buf, 9 * d)

    d = X_DIR
    finish(d, outer(moved[d], project(d, -1, result)), shift_x(m, project(d, 1, result), 1))
    first = {d: outer(moved[d], project(d, -1, result)) for d in FACES}
    all_up.wait()
    there = shift_face(m, Y_DIR, 1, later[Y_DIR], face_of(inbox, Y_DIR, 2), None)
    there = [
        (tr - 2 * KAPPA * only(m["own_y"], br), ti - 2 * KAPPA * only(m["own_y"], bi))
        for (tr, ti), (br, bi) in zip(there, back[Y_DIR])
    ]
    finish(Y_DIR, first[Y_DIR], there)
    z_buf[12:30] = jnp.concatenate([part.reshape(9, 8, 128) for part in u[Z_DIR]])
    z_buf[30:48] = jnp.concatenate([part.reshape(9, 8, 128) for part in first[Z_DIR]])
    z_buf[48:60] = jnp.concatenate([part for half in plus[Z_DIR] for part in half])
    edge_half = {
        T_DIR: lambda: face_y(m["edge_t"], [lane_roll(edge_t[...], 64), edge_t[...]]),
        Z_DIR: lambda: face_y(m["edge_z"], both_spins(edge_z)),
    }
    for d in (T_DIR, Z_DIR):
        there = shift_face(m, d, 1, later[d], face_of(inbox, d, 2), ahead_sign[d])
        if d == T_DIR:
            there = [
                (tr - 2 * KAPPA * pick(m["low"], zero, br), ti - 2 * KAPPA * pick(m["low"], zero, bi))
                for (tr, ti), (br, bi) in zip(there, back[T_DIR])
            ]
        if d == Z_DIR:
            for n, part in enumerate([part for half in there for part in half]):
                z_buf[3 * n:3 * n + 3] = part
        pl.when(is_first[Y_DIR])(edges[d].wait_recv)
        if d == Z_DIR:
            for n, part in enumerate([part for half in edge_half[d]() for part in half]):
                z_buf[60 + 3 * n:63 + 3 * n] = part
            break
        scale = KAPPA * last_t
        extra = edge_term(d, edge_half[d]())
        there = [
            (tr - scale * er, ti - scale * ei) for (tr, ti), (er, ei) in zip(there, extra)
        ]
        finish(d, first[d], there)
    all_sent.wait()

    pl.when(is_last_y)(both_edges.wait_send)


def store_kernel(out_in, z_in, y_out, f_out, fz_buf, sem):
    def store(source, target):
        pltpu.make_async_copy(source, target, sem).start()

    store(out_in.at[pl.ds(12, 18)], f_out.at[pl.ds(0, 18)])
    store(out_in.at[pl.ds(39, 9)], f_out.at[pl.ds(27, 9)])
    store(out_in.at[pl.ds(0, 12)], y_out)

    def halves(start):
        return [tuple(z_in[start + 6 * s + 3 * p:start + 6 * s + 3 * p + 3] for p in range(2)) for s in range(2)]

    def matrix(start):
        return tuple(z_in[start + 9 * p:start + 9 * p + 9].reshape(3, 3, 8, 128) for p in range(2))

    low = lax.broadcasted_iota(jnp.int32, (8, 128), 1) < 64
    there = [
        (tr - KAPPA * er, ti - KAPPA * ei) for (tr, ti), (er, ei) in zip(halves(0), edge_term(Z_DIR, halves(60)))
    ]
    write_force(low, matrix(12), halves(48), matrix(30), there, fz_buf, 0)
    store(fz_buf, f_out.at[pl.ds(18, 9)])
    pltpu.make_async_copy(out_in, out_in, sem).wait()


def body(quark_field, gauge_links):
    x = quark_field.reshape(12, 16, 128)
    u = gauge_links.reshape(36, 16, 128)
    out, z = pl.pallas_call(
        kernel,
        out_shape=tuple(pltpu.VMEM(shape, jnp.float32) for shape in ((48, 16, 128), (72, 8, 128))),
        in_specs=[pl.BlockSpec(memory_space=pltpu.HBM)] * 2,
        out_specs=(pl.BlockSpec(memory_space=pltpu.VMEM),) * 2,
        scratch_shapes=[
            pltpu.VMEM(x.shape, jnp.float32),
            pltpu.VMEM(u.shape, jnp.float32),
            pltpu.VMEM((ALL_TILES, 8, 128), jnp.float32),
            pltpu.VMEM((ALL_TILES, 8, 128), jnp.float32),
            pltpu.VMEM((6, 8, 128), jnp.float32),
            pltpu.VMEM((3, 8, 128), jnp.float32),
            pltpu.VMEM((3, 8, 128), jnp.float32),
            pltpu.VMEM((6, 8, 128), jnp.float32),
            pltpu.SemaphoreType.DMA((2,)),
            pltpu.SemaphoreType.DMA((2,)),
            pltpu.SemaphoreType.DMA((6,)),
            pltpu.SemaphoreType.REGULAR((3,)),
        ],
        compiler_params=pltpu.CompilerParams(collective_id=0, has_side_effects=True, vmem_limit_bytes=16 * 1024 * 1024),
        cost_estimate=pl.CostEstimate(flops=6_000_000, bytes_accessed=800_000, transcendentals=0),
    )(pltpu.with_memory_space_constraint(x, pltpu.HBM), pltpu.with_memory_space_constraint(u, pltpu.HBM))
    y, f = pl.pallas_call(
        store_kernel,
        out_shape=(
            jax.ShapeDtypeStruct(x.shape, jnp.float32),
            jax.ShapeDtypeStruct(u.shape, jnp.float32),
        ),
        in_specs=[pl.BlockSpec(memory_space=pltpu.VMEM)] * 2,
        out_specs=(pl.BlockSpec(memory_space=pl.ANY),) * 2,
        scratch_shapes=[pltpu.VMEM((9, 16, 128), jnp.float32), pltpu.SemaphoreType.DMA],
        compiler_params=pltpu.CompilerParams(vmem_limit_bytes=16 * 1024 * 1024),
        cost_estimate=pl.CostEstimate(flops=400_000, bytes_accessed=800_000, transcendentals=0),
    )(out, z)
    return y.reshape(quark_field.shape), f.reshape(gauge_links.shape)


def solution(mesh):
    specs = (
        P(None, None, "ta", "gz", "gy", None),
        P(None, None, None, "ta", "gz", "gy", None),
    )
    return jax.shard_map(body, mesh=mesh, in_specs=specs, out_specs=specs, check_vma=False)
```

```python
import functools

import jax
import jax.numpy as jnp
from jax import lax
from jax.experimental import pallas as pl
from jax.experimental.pallas import tpu as pltpu
from jax.sharding import PartitionSpec as P

KAPPA = 0.125
MESH = pl.DeviceIdType.MESH
X_DIR, Y_DIR, Z_DIR, T_DIR = 0, 1, 2, 3
AXES = {T_DIR: "ta", Z_DIR: "gz", Y_DIR: "gy"}
FACES = (T_DIR, Z_DIR, Y_DIR)
FACE_TILES = {T_DIR: 6, Z_DIR: 3, Y_DIR: 6}
FACE_START = {T_DIR: 0, Z_DIR: 18, Y_DIR: 27}
ALL_TILES = 45
RECV_SEM = {(T_DIR, 0): 0, (T_DIR, 1): 0, (Z_DIR, 0): 1, (Z_DIR, 1): 1, (Y_DIR, 0): 1, (Y_DIR, 1): 2}
RECV_UP, RECV_EDGE = 3, {T_DIR: 4, Z_DIR: 5}


def lane_roll(v, steps):
    return pltpu.roll(v.reshape(-1, 128), steps, 1).reshape(v.shape)


def row_roll(v, steps):
    if steps % 8 == 0:
        return v
    flat = v.reshape(-1, 8, 128)
    return jnp.stack([pltpu.roll(flat[i], steps % 8, 0) for i in range(flat.shape[0])]).reshape(v.shape)


def masks(at_start, at_end):
    lane = lax.broadcasted_iota(jnp.int32, (8, 128), 1)
    row = lax.broadcasted_iota(jnp.int32, (8, 128), 0)
    return {
        "low": lane < 64,
        "last_x": lane % 64 == 63,
        "first_x": lane % 64 == 0,
        "even": row % 2 == 0,
        "z_first": row < 2,
        "z_last": row >= 6,
        "row": row,
        "halo_now": row % 2 + at_start == 0,
        "halo_late": row % 2 + (1 - at_start) == 0,
        "own_y": row % 2 * at_end == 1,
        "edge_t": (row % 2 + (1 - at_start) == 0) & (lane >= 64),
        "edge_z": row + 8 * (1 - at_start) == 6,
    }


def pick(mask, a, b):
    return jnp.where(jnp.broadcast_to(mask, a.shape), a, b)


def unpack(m, first, second):
    return (
        pick(m["low"], first, lane_roll(second, 64)),
        pick(m["low"], lane_roll(first, 64), second),
    )


def pack_first(m, re, im):
    return pick(m["low"], re, lane_roll(im, 64))


def pack_second(m, re, im):
    return pick(m["low"], lane_roll(re, 64), im)


def c_add(a, b):
    return (a[0] + b[0], a[1] + b[1])


def c_sub(a, b):
    return (a[0] - b[0], a[1] - b[1])


def add_i(a, b):
    return (a[0] - b[1], a[1] + b[0])


def sub_i(a, b):
    return (a[0] + b[1], a[1] - b[0])


def project(direction, sign, psi):
    u0, u1, l0, l1 = psi
    plus, minus = (c_add, c_sub) if sign < 0 else (c_sub, c_add)
    plus_i, minus_i = (add_i, sub_i) if sign < 0 else (sub_i, add_i)
    if direction == X_DIR:
        return [plus_i(u0, l1), plus_i(u1, l0)]
    if direction == Y_DIR:
        return [plus(u0, l1), minus(u1, l0)]
    if direction == Z_DIR:
        return [plus_i(u0, l0), minus_i(u1, l1)]
    return [minus(u0, l0), minus(u1, l1)]


def add_spins(direction, sign, total, half):
    h0, h1 = half
    plus, minus = (c_sub, c_add) if sign < 0 else (c_add, c_sub)
    plus_i, minus_i = (sub_i, add_i) if sign < 0 else (add_i, sub_i)
    t0, t1, t2, t3 = total
    upper = [c_add(t0, h0), c_add(t1, h1)]
    if direction == X_DIR:
        return upper + [plus_i(t2, h1), plus_i(t3, h0)]
    if direction == Y_DIR:
        return upper + [plus(t2, h1), minus(t3, h0)]
    if direction == Z_DIR:
        return upper + [plus_i(t2, h0), minus_i(t3, h1)]
    return upper + [plus(t2, h0), plus(t3, h1)]


def link_times(u, half):
    ur, ui = u
    out = []
    for hr, hi in half:
        re = im = None
        for b in range(3):
            cr, ci = ur[:, b], ui[:, b]
            r = cr * hr[b][None] - ci * hi[b][None]
            i = cr * hi[b][None] + ci * hr[b][None]
            re = r if re is None else re + r
            im = i if im is None else im + i
        out.append((re, im))
    return out


def adjoint_times(u, half):
    ur, ui = u
    out = []
    for hr, hi in half:
        re = im = None
        for b in range(3):
            cr, ci = ur[b], ui[b]
            r = cr * hr[b][None] + ci * hi[b][None]
            i = cr * hi[b][None] - ci * hr[b][None]
            re = r if re is None else re + r
            im = i if im is None else im + i
        out.append((re, im))
    return out


def outer(left, right):
    re = im = None
    for (lr, li), (rr, ri) in zip(left, right):
        r = lr[:, None] * rr[None] + li[:, None] * ri[None]
        i = li[:, None] * rr[None] - lr[:, None] * ri[None]
        re = r if re is None else re + r
        im = i if im is None else im + i
    return re, im


def shift_x(m, half, steps):
    def one(v):
        if steps > 0:
            return pick(m["last_x"], lane_roll(v, 63), lane_roll(v, 127))
        return pick(m["first_x"], lane_roll(v, 65), lane_roll(v, 1))

    return [(one(re), one(im)) for re, im in half]


def stage_face(m, direction, end, half, ref):
    if direction == T_DIR:
        for s, (re, im) in enumerate(half):
            ref[3 * s:3 * s + 3] = (pack_second if end else pack_first)(m, re, im)
    elif direction == Y_DIR:
        for s, (re, im) in enumerate(half):
            if end:
                tile = pick(m["even"], row_roll(re, -1), im)
            else:
                tile = pick(m["even"], re, row_roll(im, 1))
            ref[3 * s:3 * s + 3] = tile
    else:
        tiles = [part[c] for re, im in half for part in (re, im) for c in range(3)]
        for j in range(3):
            tile = row_roll(tiles[4 * j], 2 if end else 0)
            for k in range(1, 4):
                moved = row_roll(tiles[4 * j + k], 2 * k + (2 if end else 0))
                tile = pick(m["row"] < 2 * k, tile, moved)
            ref[j] = tile


def shift_face(m, direction, steps, half, ref, sign):
    out = []
    if direction == T_DIR:
        for s, (re, im) in enumerate(half):
            face = ref[3 * s:3 * s + 3] * sign
            if steps > 0:
                out.append((
                    lane_roll(pick(m["low"], face, re), 64),
                    pick(m["low"], lane_roll(im, 64), face),
                ))
            else:
                out.append((
                    pick(m["low"], face, lane_roll(re, 64)),
                    lane_roll(pick(m["low"], im, face), 64),
                ))
    elif direction == Y_DIR:
        for s, (re, im) in enumerate(half):
            face = ref[3 * s:3 * s + 3]
            if steps > 0:
                out.append((
                    pick(m["even"], row_roll(re, -1), row_roll(face, 1)),
                    pick(m["even"], row_roll(im, -1), face),
                ))
            else:
                out.append((
                    pick(m["even"], face, row_roll(re, 1)),
                    pick(m["even"], row_roll(face, -1), row_roll(im, 1)),
                ))
    else:
        n = 0
        for re, im in half:
            parts = []
            for part in (re, im):
                moved = []
                for c in range(3):
                    face = ref[n // 4]
                    k = n % 4
                    n += 1
                    if steps > 0:
                        moved.append(row_roll(pick(m["z_first"], row_roll(face, -2 * k), part[c]), -2))
                    else:
                        moved.append(row_roll(pick(m["z_last"], row_roll(face, 6 - 2 * k), part[c]), 2))
                parts.append(jnp.stack(moved))
            out.append(tuple(parts))
    return out


def only(mask, v):
    return pick(mask, v, jnp.zeros_like(v))


def local_y(m, half):
    return [tuple(pick(m["even"], jnp.zeros_like(v), row_roll(v, 1)) for v in parts) for parts in half]


def face_y(mask, faces):
    return [(only(mask, face), only(mask, row_roll(face, -1))) for face in faces]


def both_spins(ref):
    return [ref[0:3], ref[3:6]]


def edge_term(direction, half):
    h0, h1 = half
    return project(direction, 1, [h0, h1, h1, (-h0[0], -h0[1])])


def write_force(low, u, plus, first, later_there, f_buf, start):
    second = outer(link_times(u, later_there), plus)
    wr, wi = c_add(first, second)
    third = (wi[0, 0] + wi[1, 1] + wi[2, 2]) / 3.0
    m = {"low": low}
    for a in range(3):
        for b in range(a, 3):
            if a == b:
                im = KAPPA * (wi[a, a] - third)
                re = jnp.zeros_like(im)
            else:
                re = (0.5 * KAPPA) * (wr[a, b] - wr[b, a])
                im = (0.5 * KAPPA) * (wi[a, b] + wi[b, a])
            top = pack_first(m, re, im)
            bottom = pack_second(m, re, im)
            f_buf[start + 3 * a + b, 0:8] = top
            f_buf[start + 3 * a + b, 8:16] = bottom
            if a != b:
                f_buf[start + 3 * b + a, 0:8] = pick(low, -top, top)
                f_buf[start + 3 * b + a, 8:16] = pick(low, -bottom, bottom)


def kernel(
    x_hbm, u_hbm, out_buf, z_buf,
    x_buf, u_buf,
    outbox, inbox, y_now, edge_out, edge_t, edge_z,
    load_sem, send_sem, recv_sem, here_sem,
):
    y_buf, f_buf = out_buf.at[pl.ds(0, 12)], out_buf.at[pl.ds(12, 36)]

    def face_of(box, d, slot, faces=1):
        return box.at[pl.ds(FACE_START[d] + slot * FACE_TILES[d], faces * FACE_TILES[d])]

    first_load = pltpu.make_async_copy(u_hbm.at[pl.ds(0, 21)], u_buf.at[pl.ds(0, 21)], load_sem.at[0])
    rest_load = pltpu.make_async_copy(u_hbm.at[pl.ds(0, 27)], u_buf.at[pl.ds(0, 27)], load_sem.at[1])

    def load(source, target, start, count, sem):
        part = pl.ds(start, count)
        pltpu.make_async_copy(source.at[part], target.at[part], load_sem.at[sem]).start()

    for s in range(3):
        load(x_hbm, x_buf, 4 * s, 4, 0)
    for a in range(3):
        load(u_hbm, u_buf, 9 * Y_DIR + 3 * a, 3, 0)
    me = {d: lax.axis_index(AXES[d]) for d in FACES}
    size = {d: lax.axis_size(AXES[d]) for d in FACES}
    ahead = {d: lax.rem(me[d] + 1, size[d]) for d in FACES}
    behind = {d: lax.rem(me[d] + size[d] - 1, size[d]) for d in FACES}

    barrier = pltpu.get_barrier_semaphore()
    is_first = {d: me[d] == 0 for d in FACES}
    is_last = {d: me[d] == size[d] - 1 for d in FACES}
    is_last_y = is_last[Y_DIR]

    def greet(where):
        pl.semaphore_signal(barrier, inc=1, device_id=where, device_id_type=MESH)

    odd = lax.rem(me[T_DIR], 2) == 1
    greeter = odd ^ (me[Z_DIR] < size[Z_DIR] // 2)
    plain = jnp.logical_not(is_last_y)
    pl.when(plain | greeter | is_first[T_DIR])(functools.partial(greet, {AXES[T_DIR]: behind[T_DIR]}))
    pl.when(plain | is_first[Z_DIR])(functools.partial(greet, {AXES[Z_DIR]: behind[Z_DIR]}))
    pl.when((plain | greeter) & jnp.logical_not(is_last[T_DIR]))(functools.partial(greet, {AXES[T_DIR]: ahead[T_DIR]}))
    for d in (Z_DIR, Y_DIR):
        pl.when(jnp.logical_not(is_last[d]))(functools.partial(greet, {AXES[d]: ahead[d]}))

    @pl.when(is_first[Y_DIR])
    def _():
        greet({AXES[Y_DIR]: behind[Y_DIR]})
        for d in (T_DIR, Z_DIR):
            greet({AXES[d]: ahead[d], AXES[Y_DIR]: behind[Y_DIR]})

    def one(flag):
        return flag.astype(jnp.int32)

    plain_arrivals = 5 - sum(one(is_first[d]) for d in FACES)
    late_t = jnp.where(greeter, one(odd & is_last[T_DIR]), 2 - one(is_first[T_DIR]))
    late_arrivals = late_t + 1 + one(is_last[Z_DIR]) - one(is_first[Z_DIR]) + 4
    late_replies = one(jnp.logical_not(is_last[Z_DIR])) + jnp.where(greeter, 2 - one(is_last[T_DIR]) - one(is_first[T_DIR]), 0)
    arrivals = jnp.where(is_last_y, late_arrivals, plain_arrivals)
    replies = jnp.where(is_last_y, late_replies, 1)
    for d in (T_DIR, Z_DIR, X_DIR):
        load(u_hbm, u_buf, 9 * d, 9, 1)

    def link(d, slot, there, faces=1):
        return pltpu.make_async_remote_copy(
            src_ref=face_of(outbox, d, slot, faces),
            dst_ref=face_of(inbox, d, slot, faces),
            send_sem=send_sem.at[0],
            recv_sem=recv_sem.at[RECV_SEM.get((d, slot), RECV_UP)],
            device_id={AXES[d]: there},
            device_id_type=MESH,
        )

    forward = {d: link(d, 0, behind[d]) for d in FACES}
    backward = {d: link(d, 1, ahead[d]) for d in FACES}
    upward = {d: link(d, 2, behind[d]) for d in FACES}
    both_t = link(T_DIR, 0, behind[T_DIR], 2)
    z_and_y = pltpu.make_async_copy(outbox.at[pl.ds(0, 12)], inbox.at[pl.ds(0, 12)], recv_sem.at[RECV_SEM[Z_DIR, 0]])
    all_up = pltpu.make_async_copy(outbox.at[pl.ds(0, 15)], inbox.at[pl.ds(0, 15)], recv_sem.at[RECV_UP])
    all_sent = pltpu.make_async_copy(outbox, inbox, send_sem.at[0])
    edge_rows = u_buf.at[pl.ds(0, 33), 0:12]
    all_and_edges_sent = pltpu.make_async_copy(edge_rows, edge_rows, send_sem.at[0])

    def edge_link(d, src, dst):
        return pltpu.make_async_remote_copy(
            src_ref=src,
            dst_ref=dst,
            send_sem=send_sem.at[0],
            recv_sem=recv_sem.at[RECV_EDGE[d]],
            device_id={AXES[d]: behind[d], AXES[Y_DIR]: ahead[Y_DIR]},
            device_id_type=MESH,
        )

    edges = {
        T_DIR: edge_link(T_DIR, edge_out, edge_t),
        Z_DIR: edge_link(Z_DIR, face_of(outbox, Y_DIR, 1).at[:, 0:2], edge_z.at[:, 6:8]),
    }

    here = {T_DIR: here_sem.at[0], Z_DIR: here_sem.at[0], Y_DIR: here_sem.at[1]}
    here_near = here_sem.at[2]

    def say_here():
        def say(sem, there):
            pl.semaphore_signal(sem, inc=1, device_id=there, device_id_type=MESH)

        for d in FACES:
            pl.when(is_last[d])(functools.partial(say, here[d], {AXES[d]: ahead[d]}))
        there = {AXES[Y_DIR]: behind[Y_DIR]}
        pl.when(jnp.logical_not(is_first[Y_DIR]))(functools.partial(say, here_near, there))

        @pl.when(is_last_y)
        def _():
            pl.when(jnp.logical_not(is_first[Z_DIR]))(functools.partial(say, here_near, {AXES[Z_DIR]: behind[Z_DIR]}))
            greeted = jnp.logical_not(greeter)
            pl.when(greeted & jnp.logical_not(is_last[T_DIR]))(
                functools.partial(say, here_near, {AXES[T_DIR]: ahead[T_DIR]})
            )
            pl.when(greeted & jnp.logical_not(is_first[T_DIR]))(
                functools.partial(say, here_near, {AXES[T_DIR]: behind[T_DIR]})
            )

    m = masks(is_first[Y_DIR].astype(jnp.int32), is_last_y.astype(jnp.int32))
    last_t = jnp.where(me[T_DIR] == size[T_DIR] - 1, -1.0, 1.0).astype(jnp.float32)
    first_t = jnp.where(me[T_DIR] == 0, -1.0, 1.0).astype(jnp.float32)
    ahead_sign = {T_DIR: last_t, Z_DIR: None, Y_DIR: None}
    behind_sign = {T_DIR: first_t, Z_DIR: None, Y_DIR: None}

    first_load.wait()
    psi = [unpack(m, x_buf[3 * s:3 * s + 3, 0:8], x_buf[3 * s:3 * s + 3, 8:16]) for s in range(4)]
    minus = {}
    plus = {}
    u = {}
    back = {}

    def links(d):
        first, second = unpack(m, u_buf[9 * d:9 * d + 9, 0:8], u_buf[9 * d:9 * d + 9, 8:16])
        return first.reshape(3, 3, 8, 128), second.reshape(3, 3, 8, 128)

    def prepare_backward(d):
        u[d] = links(d)
        plus[d] = project(d, 1, psi)
        back[d] = adjoint_times(u[d], plus[d])
        stage_face(m, d, 1, back[d], face_of(outbox, d, 1))

    prepare_backward(Y_DIR)

    @pl.when(is_last_y)
    def _():
        pl.semaphore_wait(barrier, arrivals)
        edges[Z_DIR].start()
        spins = both_spins(face_of(outbox, Y_DIR, 1))
        edge_out[...] = pick(m["low"], spins[0], lane_roll(spins[1], 64))
        edges[T_DIR].start()
        backward[Y_DIR].start()
        say_here()

    for d in FACES:
        minus[d] = project(d, -1, psi)
        stage_face(m, d, 0, minus[d], face_of(outbox, d, 0))
    rest_load.wait()
    for d in (T_DIR, Z_DIR):
        prepare_backward(d)

    @pl.when(jnp.logical_not(is_last_y))
    def _():
        pl.semaphore_wait(barrier, arrivals)
        say_here()

    pl.when(is_last_y & (replies > 0))(lambda: pl.semaphore_wait(here_near, replies))
    for d in (T_DIR, Z_DIR):
        backward[d].start()
    for d in FACES:
        pl.when(jnp.logical_not(is_first[d]))(forward[d].start)

    @pl.when(is_first[T_DIR] | is_first[Z_DIR])
    def _():
        pl.semaphore_wait(here[T_DIR], is_first[T_DIR].astype(jnp.int32) + is_first[Z_DIR].astype(jnp.int32))
        for d in (T_DIR, Z_DIR):
            pl.when(is_first[d])(forward[d].start)

    @pl.when(jnp.logical_not(is_last_y))
    def _():
        pl.semaphore_wait(here_near, replies)
        backward[Y_DIR].start()

    zero = jnp.zeros((3, 8, 128), jnp.float32)
    hop = [(zero, zero)] * 4
    d = X_DIR
    u[d] = links(d)
    plus[d] = project(d, 1, psi)
    minus[d] = project(d, -1, psi)
    moved = {}
    moved[d] = link_times(u[d], shift_x(m, minus[d], 1))
    hop = add_spins(d, -1, hop, moved[d])
    hop = add_spins(d, 1, hop, shift_x(m, adjoint_times(u[d], plus[d]), -1))

    def take_backward(d, hop):
        there = shift_face(m, d, -1, back[d], face_of(inbox, d, 1), behind_sign[d])
        return add_spins(d, 1, hop, there)

    def take_forward(d, hop):
        there = shift_face(m, d, 1, minus[d], face_of(inbox, d, 0), ahead_sign[d])
        moved[d] = link_times(u[d], there)
        return add_spins(d, -1, hop, moved[d])

    def wilson(hop):
        return [(pr - KAPPA * hr, pi - KAPPA * hi) for (pr, pi), (hr, hi) in zip(psi, hop)]

    z_and_y.wait()
    hop = take_backward(Z_DIR, hop)
    hop = take_forward(Z_DIR, hop)
    hop = take_forward(Y_DIR, hop)
    hop = add_spins(Y_DIR, 1, hop, local_y(m, back[Y_DIR]))

    @pl.when(jnp.logical_not(is_first[Y_DIR]))
    def _():
        backward[Y_DIR].wait_recv()
        y_now[...] = face_of(inbox, Y_DIR, 1)[...]

    hop = add_spins(Y_DIR, 1, hop, face_y(m["halo_now"], both_spins(y_now)))

    inner = [tuple(lane_roll(v, 64) for v in parts) for parts in minus[T_DIR]]
    inner = add_spins(T_DIR, -1, hop, link_times(u[T_DIR], inner))
    stage_face(m, T_DIR, 0, project(T_DIR, 1, wilson(inner)), face_of(outbox, T_DIR, 2))
    upward[T_DIR].start()
    both_t.wait_recv()
    hop = take_backward(T_DIR, hop)
    hop = take_forward(T_DIR, hop)
    early = wilson(hop)
    for d in (Z_DIR, Y_DIR):
        stage_face(m, d, 0, project(d, 1, early), face_of(outbox, d, 2))
    upward[Z_DIR].start()
    pl.when(jnp.logical_not(is_first[Y_DIR]))(upward[Y_DIR].start)

    @pl.when(is_first[Y_DIR])
    def _():
        pl.semaphore_wait(here[Y_DIR], 1)
        forward[Y_DIR].start()
        upward[Y_DIR].start()
        backward[Y_DIR].wait_recv()

    late = face_y(m["halo_late"], both_spins(face_of(inbox, Y_DIR, 1)))
    missing = add_spins(Y_DIR, 1, [(zero, zero)] * 4, late)
    result = [
        (er - KAPPA * lr, ei - KAPPA * li) for (er, ei), (lr, li) in zip(early, missing)
    ]
    later = {d: project(d, 1, result) for d in FACES}
    for s, (re, im) in enumerate(result):
        y_buf[3 * s:3 * s + 3, 0:8] = pack_first(m, re, im)
        y_buf[3 * s:3 * s + 3, 8:16] = pack_second(m, re, im)

    def finish(d, first, later_there):
        write_force(m["low"], u[d], plus[d], first, later_there, f_buf, 9 * d)

    d = X_DIR
    finish(d, outer(moved[d], project(d, -1, result)), shift_x(m, project(d, 1, result), 1))
    first = {d: outer(moved[d], project(d, -1, result)) for d in FACES}
    all_up.wait()
    there = shift_face(m, Y_DIR, 1, later[Y_DIR], face_of(inbox, Y_DIR, 2), None)
    there = [
        (tr - 2 * KAPPA * only(m["own_y"], br), ti - 2 * KAPPA * only(m["own_y"], bi))
        for (tr, ti), (br, bi) in zip(there, back[Y_DIR])
    ]
    finish(Y_DIR, first[Y_DIR], there)
    z_buf[12:30] = jnp.concatenate([part.reshape(9, 8, 128) for part in u[Z_DIR]])
    z_buf[30:48] = jnp.concatenate([part.reshape(9, 8, 128) for part in first[Z_DIR]])
    z_buf[48:60] = jnp.concatenate([part for half in plus[Z_DIR] for part in half])
    edge_half = {
        T_DIR: lambda: face_y(m["edge_t"], [lane_roll(edge_t[...], 64), edge_t[...]]),
        Z_DIR: lambda: face_y(m["edge_z"], both_spins(edge_z)),
    }
    for d in (T_DIR, Z_DIR):
        there = shift_face(m, d, 1, later[d], face_of(inbox, d, 2), ahead_sign[d])
        if d == T_DIR:
            there = [
                (tr - 2 * KAPPA * pick(m["low"], zero, br), ti - 2 * KAPPA * pick(m["low"], zero, bi))
                for (tr, ti), (br, bi) in zip(there, back[T_DIR])
            ]
        if d == Z_DIR:
            for n, part in enumerate([part for half in there for part in half]):
                z_buf[3 * n:3 * n + 3] = part
        pl.when(is_first[Y_DIR])(edges[d].wait_recv)
        if d == Z_DIR:
            for n, part in enumerate([part for half in edge_half[d]() for part in half]):
                z_buf[60 + 3 * n:63 + 3 * n] = part
            break
        scale = KAPPA * last_t
        extra = edge_term(d, edge_half[d]())
        there = [
            (tr - scale * er, ti - scale * ei) for (tr, ti), (er, ei) in zip(there, extra)
        ]
        finish(d, first[d], there)
    pl.when(plain)(all_sent.wait)
    pl.when(is_last_y)(all_and_edges_sent.wait)


def store_kernel(out_in, z_in, y_out, f_out, fz_buf, sem):
    def store(source, target):
        pltpu.make_async_copy(source, target, sem).start()

    store(out_in.at[pl.ds(12, 18)], f_out.at[pl.ds(0, 18)])
    store(out_in.at[pl.ds(39, 9)], f_out.at[pl.ds(27, 9)])
    store(out_in.at[pl.ds(0, 12)], y_out)

    def halves(start):
        return [tuple(z_in[start + 6 * s + 3 * p:start + 6 * s + 3 * p + 3] for p in range(2)) for s in range(2)]

    def matrix(start):
        return tuple(z_in[start + 9 * p:start + 9 * p + 9].reshape(3, 3, 8, 128) for p in range(2))

    low = lax.broadcasted_iota(jnp.int32, (8, 128), 1) < 64
    there = [
        (tr - KAPPA * er, ti - KAPPA * ei) for (tr, ti), (er, ei) in zip(halves(0), edge_term(Z_DIR, halves(60)))
    ]
    write_force(low, matrix(12), halves(48), matrix(30), there, fz_buf, 0)
    store(fz_buf, f_out.at[pl.ds(18, 9)])
    pltpu.make_async_copy(out_in, out_in, sem).wait()


def body(quark_field, gauge_links):
    x = quark_field.reshape(12, 16, 128)
    u = gauge_links.reshape(36, 16, 128)
    out, z = pl.pallas_call(
        kernel,
        out_shape=tuple(pltpu.VMEM(shape, jnp.float32) for shape in ((48, 16, 128), (72, 8, 128))),
        in_specs=[pl.BlockSpec(memory_space=pltpu.HBM)] * 2,
        out_specs=(pl.BlockSpec(memory_space=pltpu.VMEM),) * 2,
        scratch_shapes=[
            pltpu.VMEM(x.shape, jnp.float32),
            pltpu.VMEM(u.shape, jnp.float32),
            pltpu.VMEM((ALL_TILES, 8, 128), jnp.float32),
            pltpu.VMEM((ALL_TILES, 8, 128), jnp.float32),
            pltpu.VMEM((6, 8, 128), jnp.float32),
            pltpu.VMEM((3, 8, 128), jnp.float32),
            pltpu.VMEM((3, 8, 128), jnp.float32),
            pltpu.VMEM((6, 8, 128), jnp.float32),
            pltpu.SemaphoreType.DMA((2,)),
            pltpu.SemaphoreType.DMA((1,)),
            pltpu.SemaphoreType.DMA((6,)),
            pltpu.SemaphoreType.REGULAR((3,)),
        ],
        compiler_params=pltpu.CompilerParams(collective_id=0, has_side_effects=True, vmem_limit_bytes=16 * 1024 * 1024),
        cost_estimate=pl.CostEstimate(flops=6_000_000, bytes_accessed=800_000, transcendentals=0),
    )(pltpu.with_memory_space_constraint(x, pltpu.HBM), pltpu.with_memory_space_constraint(u, pltpu.HBM))
    y, f = pl.pallas_call(
        store_kernel,
        out_shape=(
            jax.ShapeDtypeStruct(x.shape, jnp.float32),
            jax.ShapeDtypeStruct(u.shape, jnp.float32),
        ),
        in_specs=[pl.BlockSpec(memory_space=pltpu.VMEM)] * 2,
        out_specs=(pl.BlockSpec(memory_space=pl.ANY),) * 2,
        scratch_shapes=[pltpu.VMEM((9, 16, 128), jnp.float32), pltpu.SemaphoreType.DMA],
        compiler_params=pltpu.CompilerParams(vmem_limit_bytes=16 * 1024 * 1024),
        cost_estimate=pl.CostEstimate(flops=400_000, bytes_accessed=800_000, transcendentals=0),
    )(out, z)
    return y.reshape(quark_field.shape), f.reshape(gauge_links.shape)


def solution(mesh):
    specs = (
        P(None, None, "ta", "gz", "gy", None),
        P(None, None, None, "ta", "gz", "gy", None),
    )
    return jax.shard_map(body, mesh=mesh, in_specs=specs, out_specs=specs, check_vma=False)
```
